128 devices in a mesh: dp: 64 (over z_lo, x, y, core), tensor: 2 (over z_hi).
Axes of the slice: x: 4, y: 4, z: 4 (z_hi: 2, z_lo: 2; z = z_hi * 2 + z_lo), core: 2. Of those that a mesh axis runs over, the one named last changes fastest.
Arguments:
- tokens: bfloat16 [16384, 384], P('dp'), may hold values from -6 to 6
- cotangent: bfloat16 [16384, 384], P('dp'), may hold values from -6 to 6
- pos_table: float32 [50, 384], replicated, may hold values from -3 to 3
- norm_params: float32 [4, 384], replicated
- qkv_weight: float32 [384, 1152], P(None, ('tensor', 'dp'))
- out_weight: float32 [384, 384], P(('tensor', 'dp'))
- up_weight: float32 [384, 1536], P(None, ('tensor', 'dp'))
- down_weight: float32 [1536, 384], P(('tensor', 'dp'))
- qkv_moment: float32 [384, 1152], P(None, ('tensor', 'dp')), may hold values from -0.0030070327 to 0.0030070327
- out_moment: float32 [384, 384], P(('tensor', 'dp')), may hold values from -0.0030070327 to 0.0030070327
- up_moment: float32 [384, 1536], P(None, ('tensor', 'dp')), may hold values from -0.0030070327 to 0.0030070327
- down_moment: float32 [1536, 384], P(('tensor', 'dp')), may hold values from -0.0030070327 to 0.0030070327
- norm_moment: float32 [4, 384], replicated, may hold values from -0.030070327 to 0.030070327
- pos_moment: float32 [50, 384], replicated, may hold values from -0.030070327 to 0.030070327
- res_ids: int32 [320], P('dp'), may hold values from 0 to 2, as said below
- offsets: int32 [320], P('dp'), may hold values from 0 to 256, as said below
- pos_index: int32 [16384], P('dp'), may hold values from 0 to 49, as said below
Outputs:
- result: bfloat16 [16384, 384], P('dp')
- in_grad: float32 [16384, 384], P('dp')
- grad_norm: float32 [], replicated
- qkv_moment_next: float32 [384, 1152], P(None, ('tensor', 'dp'))
- qkv_weight_next: float32 [384, 1152], P(None, ('tensor', 'dp'))
- out_moment_next: float32 [384, 384], P(('tensor', 'dp'))
- out_weight_next: float32 [384, 384], P(('tensor', 'dp'))
- up_moment_next: float32 [384, 1536], P(None, ('tensor', 'dp'))
- up_weight_next: float32 [384, 1536], P(None, ('tensor', 'dp'))
- down_moment_next: float32 [1536, 384], P(('tensor', 'dp'))
- down_weight_next: float32 [1536, 384], P(('tensor', 'dp'))
- norm_moment_next: float32 [4, 384], replicated
- norm_params_next: float32 [4, 384], replicated
- pos_moment_next: float32 [50, 384], replicated
- pos_table_next: float32 [50, 384], replicated
The draws below stay inside these ranges and needn't reach their ends.
Inputs may be any that keep to these rules, and one draw needn't show every extreme that they name: `res_ids`: 0 marks a 224-pixel image of 50 tokens, 1 a 384-pixel image of 145 tokens, 2 an empty slot; the 5 slots of a dp index hold its images first and empty slots last, and at most one 384-pixel image. `offsets`: images of a dp index lie end to end from its slot 0 in slot order; an empty slot holds 256; token slots after the last image are padding. `pos_index`: 0 for an image's first token and for padding; for patch (r, c) of a g x g grid (g = 7 or 12), in row order after the first token, 1 + 7 (r * 7 // g) + (c * 7 // g).
All inputs are finite; a program needn't handle non-finite values.
Results may differ from the reference program's by a relative error of at most 0.015.
The reference program's roundings to bfloat16 on the way count: a program that leaves them out, or rounds other values in their place, can miss the bound.
Values may be sent and summed in bfloat16 or wider, within the bound.
No kernel may reach another device: no remote copies, remote signals or barrier semaphores. Data moves between devices by JAX's collectives and lax.ppermute only.
A program may use at most 128 MiB of HBM per device.

```python
import jax
import jax.numpy as jnp
from jax import lax

D = 384
HEADS = 6
HD = 64
FF = 1536
POS = 50
SMALL_LEN = 50
BIG_LEN = 145
NS_STEPS = 5
TOK_DEV = 256
IMG_DEV = 5
TOKENS = 16384
N_DP = 64
N_TENSOR = 2


def rising(key, rows_count, cols_count, along, fan_in, top_factor):
    base = jnp.clip(jax.random.normal(key, (rows_count, cols_count), jnp.float32), -4.0, 4.0)
    length = rows_count if along == 0 else cols_count
    block = length // N_TENSOR
    place = (jnp.arange(length) % block).astype(jnp.float32)
    factor = top_factor ** (place / (block - 1))
    factor = factor[:, None] if along == 0 else factor[None, :]
    return base * factor * fan_in ** (-0.5)


def packing(key):
    big = jax.random.randint(jax.random.fold_in(key, 101), (N_DP,), 0, 2).astype(jnp.int32)
    big = big.at[0].set(1).at[N_DP - 1].set(0)
    count = jnp.where(big == 1, (TOK_DEV - BIG_LEN) // SMALL_LEN + 1, TOK_DEV // SMALL_LEN).astype(jnp.int32)
    chosen = jax.random.randint(jax.random.fold_in(key, 102), (N_DP,), 0, 65536).astype(jnp.int32) % count
    slot = jnp.arange(IMG_DEV, dtype=jnp.int32)[None, :]
    used = slot < count[:, None]
    is_big = (big[:, None] == 1) & (slot == chosen[:, None])
    res = jnp.where(used, jnp.where(is_big, 1, 0), 2).astype(jnp.int32)
    lengths = jnp.where(res == 0, SMALL_LEN, jnp.where(res == 1, BIG_LEN, 0)).astype(jnp.int32)
    starts = (jnp.cumsum(lengths, axis=1) - lengths).astype(jnp.int32)
    offsets = jnp.where(used, starts, TOK_DEV).astype(jnp.int32)
    places = jnp.arange(TOK_DEV, dtype=jnp.int32)[None, :, None]
    inside = (places >= starts[:, None, :]) & (places < (starts + lengths)[:, None, :])
    relative = places - starts[:, None, :]
    patch = jnp.maximum(relative - 1, 0)
    side = jnp.where(res == 1, 12, 7).astype(jnp.int32)[:, None, :]
    mapped = 1 + patch // side * 7 // side * 7 + patch % side * 7 // side
    mapped = jnp.where(relative == 0, 0, mapped)
    position = jnp.sum(jnp.where(inside, mapped, 0), axis=2).astype(jnp.int32)
    return (res.reshape(-1), offsets.reshape(-1), position.reshape(-1))


def draw_res_ids(key, part):
    return packing(key)[0]


def draw_offsets(key, part):
    return packing(key)[1]


def draw_pos_index(key, part):
    return packing(key)[2]


def draw_qkv_weight(key, part):
    key = jax.random.fold_in(key, 11)
    return rising(key, D, 3 * D, 1, D, 3.0 ** 0.5)


def draw_out_weight(key, part):
    key = jax.random.fold_in(key, 12)
    top_factor = 3.0 ** 0.5
    return rising(key, D, D, 0, D / 16.0, top_factor)


def draw_up_weight(key, part):
    key = jax.random.fold_in(key, 13)
    top_factor = 3.0 ** 0.5
    return rising(key, D, FF, 1, D, top_factor)


def draw_down_weight(key, part):
    key = jax.random.fold_in(key, 14)
    top_factor = 3.0 ** 0.5
    return rising(key, FF, D, 0, FF, top_factor)


def draw_norm_params(key, part):
    key = jax.random.fold_in(key, 15)
    gain_key, shift_key = jax.random.split(key)
    gains = 1.0 + 0.1 * jnp.clip(jax.random.normal(gain_key, (2, D), jnp.float32), -2.5, 2.5)
    shifts = 0.3 * jnp.clip(jax.random.normal(shift_key, (2, D), jnp.float32), -3.0, 3.0)
    return jnp.stack([gains[0], shifts[0], gains[1], shifts[1]])


def levels(stream_key, extent, pieces, low, largest):
    def one(axis_at, blocks):
        steps = jax.random.uniform(jax.random.fold_in(jax.random.fold_in(stream_key, 6), axis_at), (blocks,), jnp.float32, low / len(pieces), largest / len(pieces))
        return jnp.repeat(jnp.exp(steps), extent[axis_at] // blocks).reshape((-1,) + (1,) * (len(extent) - axis_at - 1))

    loudness = one(*pieces[0])
    for cut in pieces[1:]:
        loudness = loudness * one(*cut)
    return loudness


def scatter_about(own_key, extent, deviation, limit, cuts=(), kind=jnp.bfloat16):
    entries = deviation * jax.random.normal(own_key, extent, jnp.float32)
    if cuts:
        entries = entries * levels(own_key, extent, cuts, -0.22, 0.18)
    return jnp.clip(entries, -limit, limit).astype(kind)


def setup_inputs(seed: int = 0) -> dict:
    arg_keys = jax.random.split(jax.random.key(seed), 18)
    tokens = scatter_about(arg_keys[0], (TOKENS, D), 1.0, 6.0, ((0, 64),))
    cotangent = scatter_about(arg_keys[1], (TOKENS, D), 1.0, 6.0, ((0, 64),))
    pos_table = scatter_about(arg_keys[2], (POS, D), 0.5, 3.0, (), jnp.float32)
    norm_params = draw_norm_params(jax.random.fold_in(arg_keys[17], 71), 0)
    qkv_weight = draw_qkv_weight(jax.random.fold_in(arg_keys[17], 71), 0)
    out_weight = draw_out_weight(jax.random.fold_in(arg_keys[17], 71), 0)
    up_weight = draw_up_weight(jax.random.fold_in(arg_keys[17], 71), 0)
    down_weight = draw_down_weight(jax.random.fold_in(arg_keys[17], 71), 0)
    qkv_moment = scatter_about(arg_keys[8], (D, 3 * D), ((4 * D * D + 2 * D * FF) ** -0.5), 0.0030070327, ((1, 128),), jnp.float32)
    out_moment = scatter_about(arg_keys[9], (D, D), ((4 * D * D + 2 * D * FF) ** -0.5), 0.0030070327, ((0, 128),), jnp.float32)
    up_moment = scatter_about(arg_keys[10], (D, FF), ((4 * D * D + 2 * D * FF) ** -0.5), 0.0030070327, ((1, 128),), jnp.float32)
    down_moment = scatter_about(arg_keys[11], (FF, D), ((4 * D * D + 2 * D * FF) ** -0.5), 0.0030070327, ((0, 128),), jnp.float32)
    norm_moment = scatter_about(arg_keys[12], (4, D), (10.0 * (4 * D * D + 2 * D * FF) ** -0.5), 0.030070327, (), jnp.float32)
    pos_moment = scatter_about(arg_keys[13], (POS, D), (10.0 * (4 * D * D + 2 * D * FF) ** -0.5), 0.030070327, (), jnp.float32)
    res_ids = draw_res_ids(jax.random.fold_in(arg_keys[17], 71), 0)
    offsets = draw_offsets(jax.random.fold_in(arg_keys[17], 71), 0)
    pos_index = draw_pos_index(jax.random.fold_in(arg_keys[17], 71), 0)
    return {"tokens": tokens, "cotangent": cotangent, "pos_table": pos_table, "norm_params": norm_params, "qkv_weight": qkv_weight, "out_weight": out_weight, "up_weight": up_weight, "down_weight": down_weight, "qkv_moment": qkv_moment, "out_moment": out_moment, "up_moment": up_moment, "down_moment": down_moment, "norm_moment": norm_moment, "pos_moment": pos_moment, "res_ids": res_ids, "offsets": offsets, "pos_index": pos_index}


@jax.custom_vjp
def low(v):
    return lax.optimization_barrier(v.astype(jnp.bfloat16)).astype(jnp.float32)

@jax.custom_vjp
def low_back(v):
    return v

def low_keep(v):
    return (low(v), None)

def low_pass(kept, grad):
    return (grad,)

def back_keep(v):
    return (v, None)

def back_low(kept, grad):
    return (low(grad),)
low.defvjp(low_keep, low_pass)
low_back.defvjp(back_keep, back_low)
HIGHEST = lax.Precision.HIGHEST
COEF_A = 3.4445
COEF_B = -4.775
COEF_C = 2.0315
NORM_EPS = 1e-06
CLIP_LIMIT = 1.0
MOMENTUM = 0.5
SMALL_RATE = 10.0
NORM_RATE = 40.0

def product(left, right):
    return jnp.dot(left, right, precision=HIGHEST, preferred_element_type=jnp.float32)

def layer_norm(stream, gain, shift):
    center = stream - lax.optimization_barrier(jnp.mean(stream, axis=-1, keepdims=True))
    spread = lax.optimization_barrier(jnp.mean(center * center, axis=-1, keepdims=True))
    return center * lax.rsqrt(spread + NORM_EPS) * gain + shift

def segment_ids(res_row, offset_row, count_rows):
    lengths = jnp.where(res_row == 0, SMALL_LEN, jnp.where(res_row == 1, BIG_LEN, 0)).astype(jnp.int32)
    places = jnp.arange(count_rows, dtype=jnp.int32)[:, None]
    inside = (places >= offset_row[None, :]) & (places < (offset_row + lengths)[None, :])
    labels = jnp.arange(1, res_row.shape[0] + 1, dtype=jnp.int32)
    owner = lax.optimization_barrier(jnp.sum(jnp.where(inside, labels[None, :], 0), axis=1)).astype(jnp.int32)
    return jnp.where(owner > 0, owner - 1, res_row.shape[0] + places[:, 0]).astype(jnp.int32)

def pack_attention(packed):
    qkv_block, segment = packed
    queries = qkv_block[:, :, 0]
    key_rows = qkv_block[:, :, 1]
    values = qkv_block[:, :, 2]
    scores = jnp.einsum('qhd,khd->hqk', queries, key_rows, precision=HIGHEST) * HD ** (-0.5)
    allowed = segment[:, None] == segment[None, :]
    scores = low_back(jnp.where(allowed[None], scores, -1e+30))
    top_score = lax.optimization_barrier(jnp.max(scores, axis=-1, keepdims=True))
    expo = jnp.exp(scores - top_score)
    probs = low(expo / lax.optimization_barrier(jnp.sum(expo, axis=-1, keepdims=True)))
    return jnp.einsum('hqk,khd->qhd', probs, values, precision=HIGHEST)

def forward(stream, table, norms, qkv_w, out_w, up_w, down_w, pos_index, segments):
    stream_in = stream + table[pos_index]
    normed_one = low(layer_norm(stream_in, norms[0], norms[1]))
    qkv = low(low_back(product(normed_one, low(qkv_w))))
    qkv = qkv.reshape(N_DP, TOK_DEV, HEADS, 3, HD)
    context = lax.map(jax.checkpoint(pack_attention), (qkv, segments.reshape(N_DP, TOK_DEV)))
    context = low(low_back(context.reshape(TOKENS, HEADS * HD)))
    stream_mid = stream_in + low_back(product(context, low(out_w)))
    normed_two = low(layer_norm(stream_mid, norms[2], norms[3]))
    hidden_pre = low_back(product(normed_two, low(up_w)))
    hidden = low(jax.nn.gelu(hidden_pre, approximate=False))
    return stream_mid + low_back(product(hidden, low(down_w)))

def orthogonal(moment):
    state = moment / (jnp.sqrt(jnp.sum(moment * moment)) + 1e-07)
    for step in range(NS_STEPS):
        gram = product(state, state.T)
        poly = COEF_B * gram + COEF_C * product(gram, gram)
        state = COEF_A * state + product(poly, state)
    return state

def step_rate(rows_count, cols_count):
    return (max(rows_count, cols_count) / rows_count) ** 0.5

def reference(tokens, cotangent, pos_table, norm_params, qkv_weight, out_weight, up_weight, down_weight, qkv_moment, out_moment, up_moment, down_moment, norm_moment, pos_moment, res_ids, offsets, pos_index):
    segments = jax.vmap(segment_ids, in_axes=(0, 0, None))(res_ids.reshape(N_DP, IMG_DEV), offsets.reshape(N_DP, IMG_DEV), TOK_DEV).reshape(TOKENS)

    def layer(stream, table, norms, qkv_w, out_w, up_w, down_w):
        return forward(stream, table, norms, qkv_w, out_w, up_w, down_w, pos_index, segments)
    result, pull = jax.vjp(layer, tokens.astype(jnp.float32), pos_table, norm_params, qkv_weight, out_weight, up_weight, down_weight)
    in_grad, pos_grad, norm_grad, qkv_grad, out_grad, up_grad, down_grad = pull(cotangent.astype(jnp.float32))
    grads = (qkv_grad, out_grad, up_grad, down_grad, norm_grad, pos_grad)
    squares = jnp.float32(0.0)
    for piece in grads:
        squares = squares + jnp.sum(piece * piece)
    grad_norm = jnp.sqrt(squares)
    factor = jnp.minimum(1.0, CLIP_LIMIT / (grad_norm + 1e-06))
    moments = (qkv_moment, out_moment, up_moment, down_moment, norm_moment, pos_moment)
    fresh = [MOMENTUM * moment + factor * piece for moment, piece in zip(moments, grads)]
    qkv_next = qkv_weight - step_rate(D, 3 * D) * orthogonal(fresh[0])
    out_next = out_weight - step_rate(D, D) * orthogonal(fresh[1].T).T
    up_next = up_weight - step_rate(D, FF) * orthogonal(fresh[2])
    down_next = down_weight - step_rate(FF, D) * orthogonal(fresh[3].T).T
    norm_next = norm_params - NORM_RATE * fresh[4]
    pos_next = pos_table - SMALL_RATE * fresh[5]
    return (result.astype(jnp.bfloat16), in_grad, grad_norm, fresh[0], qkv_next, fresh[1], out_next, fresh[2], up_next, fresh[3], down_next, fresh[4], norm_next, fresh[5], pos_next)
```

```python
import math

import jax
import jax.numpy as jnp
import numpy as np
from jax import lax
from jax.experimental import pallas as pl
from jax.experimental.pallas import tpu as pltpu
from jax.sharding import Mesh
from jax.sharding import PartitionSpec as P

D = 384
HEADS = 6
HD = 64
FF = 1536
SMALL_LEN = 50
BIG_LEN = 145
NS_STEPS = 5
COEF_A = 3.4445
COEF_B = -4.775
COEF_C = 2.0315
NORM_EPS = 1e-06
CLIP_LIMIT = 1.0
MOMENTUM = 0.5
SMALL_RATE = 10.0
NORM_RATE = 40.0

DP = ("zl", "x", "y", "c")
ROWS = ("zh",) + DP
COLUMN = ("zh", "zl")
PLANE = ("x", "y")
HALF = ("zl", "x", "y")
CHIPS = ("zh", "zl", "x", "y")

BF = jnp.bfloat16
F32 = jnp.float32
BLOCK = 12
GROUP = 48
SENT = 40
VMEM = 60 << 20


def unit_places():
    places = np.zeros((2, 768, 1536), np.float32)
    for core in range(2):
        for xy in range(16):
            for z in range(4):
                block = (z * 16 + xy) * 2 + core
                for r in range(BLOCK):
                    row = xy * GROUP + z * BLOCK + r
                    if r < 9:
                        head, rest = divmod(block * 9 + r, 192)
                        part, e = divmod(rest, 64)
                        places[core, row, part * 384 + head * 64 + e] = 1
                    else:
                        places[core, row, 1152 + block * 3 + r - 9] = 1
    return places


def small_places():
    places = np.zeros((768, 64), np.float32)
    for n in range(64):
        places[(n // 4) * GROUP + (n % 4) * BLOCK, n] = 1
    return places


def dot(a, b):
    return lax.dot_general(a, b, (((1,), (0,)), ((), ())), preferred_element_type=F32)


def dot_nt(a, b):
    return lax.dot_general(a, b, (((1,), (1,)), ((), ())), preferred_element_type=F32)


def dot_tn(a, b):
    return lax.dot_general(a, b, (((0,), (0,)), ((), ())), preferred_element_type=F32)


def halves(a):
    high = a.astype(BF)
    return high, (a - high.astype(F32)).astype(BF)


def norm_parts(v):
    cen = v - jnp.mean(v, axis=-1, keepdims=True)
    var = jnp.mean(cen * cen, axis=-1, keepdims=True)
    r = lax.rsqrt(var + NORM_EPS)
    return cen * r, r


def norm_back(dy, n, r, gain):
    e = dy * gain
    return r * (
        e - jnp.mean(e, axis=-1, keepdims=True) - n * jnp.mean(e * n, axis=-1, keepdims=True)
    )


def group_rows(source, first, xy):
    return jnp.concatenate(
        [source[z * 16 + xy].astype(F32)[first : first + BLOCK] for z in range(4)], axis=0
    )


def layer_kernel(
    where_ref,
    res_ref,
    off_ref,
    tok_ref,
    cot_ref,
    table_ref,
    norms_ref,
    pos_ref,
    own_ref,
    oth_ref,
    places_ref,
    small_ref,
    result_ref,
    in_grad_ref,
    keep_ref,
    send_ref,
    wup,
    wdn,
    wat,
    probs_ref,
    qkv_ref,
    ctx_ref,
    dqkv_ref,
):
    core = where_ref[0]
    half = where_ref[1]
    count = tok_ref.shape[0]

    for s, src in enumerate((own_ref, oth_ref)):

        def regroup(xy, _, s=s, src=src):
            at = pl.multiple_of(s * 768 + xy * GROUP, 16)
            for first, dst in ((0, wup), (12, wdn), (24, wat)):
                dst[pl.ds(at, GROUP), :] = group_rows(src, first, xy).astype(BF)
            return 0

        lax.fori_loop(0, 16, regroup, 0)

    def place(s):
        return core if s == 0 else 1 - core

    hits = (
        lax.broadcasted_iota(jnp.int32, (64, count), 0) == jnp.broadcast_to(pos_ref[...], (64, count))
    ).astype(BF)
    table = table_ref[...]
    t0, t_rest = halves(table)
    t1, t2 = halves(table - t0.astype(F32))
    stream_in = tok_ref[...].astype(F32) + ((dot_tn(hits, t2) + dot_tn(hits, t1)) + dot_tn(hits, t0))
    g1, s1, g2, s2 = (norms_ref[k : k + 1, :] for k in range(4))
    n1, r1 = norm_parts(stream_in)
    y1 = (n1 * g1 + s1).astype(BF)
    qkv = 0.0
    for s in range(2):
        pad = dot_nt(y1, wat[s * 768 : (s + 1) * 768, :]).astype(BF)
        qkv = qkv + dot(pad, places_ref[place(s), :, :1152])
    qkv_ref[...] = qkv.astype(BF)

    def segments(shape, dim):
        at = lax.broadcasted_iota(jnp.int32, shape, dim)
        seg = at + 8
        for k in range(5):
            res = res_ref[k]
            off = off_ref[k]
            length = jnp.where(res == 0, SMALL_LEN, jnp.where(res == 1, BIG_LEN, 0))
            seg = jnp.where((at >= off) & (at < off + length), k, seg)
        return seg

    allowed = segments((count, count), 0) == segments((count, count), 1)
    lane = lax.broadcasted_iota(jnp.int32, (1, 128), 1)
    masks = ((lane < HD).astype(F32).astype(BF), (lane >= HD).astype(F32).astype(BF))
    scale = HD**-0.5
    for p in range(HEADS // 2):
        lo = p * 128
        q = qkv_ref[:, lo : lo + 128]
        k = qkv_ref[:, 384 + lo : 512 + lo]
        v = qkv_ref[:, 768 + lo : 896 + lo]
        ctx = 0.0
        for hh in range(2):
            scores = dot_nt(q * masks[hh], k) * scale
            scores = jnp.where(allowed, scores, -1e30)
            expo = jnp.exp(scores - jnp.max(scores, axis=-1, keepdims=True))
            probs = expo / jnp.sum(expo, axis=-1, keepdims=True)
            probs_ref[2 * p + hh] = probs
            ctx = ctx + dot(probs.astype(BF), v * masks[hh])
        ctx_ref[:, lo : lo + 128] = ctx.astype(BF)
    ctx_pads = [
        dot_nt(ctx_ref[...], places_ref[place(s), :, 1152:]).astype(BF) for s in range(2)
    ]
    stream_mid = stream_in + (dot(ctx_pads[0], wat[:768, :]) + dot(ctx_pads[1], wat[768:, :]))
    n2, r2 = norm_parts(stream_mid)
    y2 = (n2 * g2 + s2).astype(BF)

    cot = cot_ref[...]
    right = jnp.where(half == 0, y2, cot)
    out = stream_mid
    d_y2 = 0.0
    for k in range(4):
        wu = wup[k * 384 : (k + 1) * 384, :]
        wd = wdn[k * 384 : (k + 1) * 384, :]
        pre = dot_nt(y2, wu)
        cdf = 0.5 * (1.0 + lax.erf(pre * (2.0**-0.5)))
        hidden = (pre * cdf).astype(BF)
        slope = cdf + pre * (jnp.exp(-0.5 * pre * pre) * ((2.0 * math.pi) ** -0.5))
        d_pre = (slope * dot_nt(cot, wd)).astype(BF)
        out = out + dot(hidden, wd)
        d_y2 = d_y2 + dot(d_pre, wu)
        grad = dot_tn(jnp.where(half == 0, d_pre, hidden), right).reshape(8, GROUP, 384)
        at = (k % 2) * 8
        if k < 2:
            keep_ref[at : at + 8] = grad
        else:
            send_ref[at : at + 8] = grad.astype(BF)
    result_ref[...] = out.astype(BF)
    gain2 = jnp.sum(d_y2 * n2, axis=0, keepdims=True)
    shift2 = jnp.sum(d_y2, axis=0, keepdims=True)
    d_mid = cot.astype(F32) + norm_back(d_y2, n2, r2, g2)

    d_attn = d_mid.astype(BF)
    d_ctx = 0.0
    for s in range(2):
        pad = dot_nt(d_attn, wat[s * 768 : (s + 1) * 768, :]).astype(BF)
        d_ctx = d_ctx + dot(pad, places_ref[place(s), :, 1152:])
    d_ctx = d_ctx.astype(BF)
    for p in range(HEADS // 2):
        lo = p * 128
        q = qkv_ref[:, lo : lo + 128]
        k = qkv_ref[:, 384 + lo : 512 + lo]
        v = qkv_ref[:, 768 + lo : 896 + lo]
        dc = d_ctx[:, lo : lo + 128]
        dq, dk, dv = 0.0, 0.0, 0.0
        for hh in range(2):
            probs = probs_ref[2 * p + hh]
            dcm = dc * masks[hh]
            d_probs = dot_nt(dcm, v)
            inner = jnp.sum(probs * d_probs, axis=-1, keepdims=True)
            d_scores = (probs * (d_probs - inner)).astype(BF)
            dq = dq + dot(d_scores, k * masks[hh])
            dk = dk + dot_tn(d_scores, q * masks[hh])
            dv = dv + dot_tn(probs.astype(BF), dcm)
        dqkv_ref[:, lo : lo + 128] = (dq * scale).astype(BF)
        dqkv_ref[:, 384 + lo : 512 + lo] = (dk * scale).astype(BF)
        dqkv_ref[:, 768 + lo : 896 + lo] = dv.astype(BF)
    d_pads = [
        dot_nt(dqkv_ref[...], places_ref[place(s), :, :1152]).astype(BF) for s in range(2)
    ]
    d_y1 = dot(d_pads[0], wat[:768, :]) + dot(d_pads[1], wat[768:, :])
    in_grad = d_mid + norm_back(d_y1, n1, r1, g1)
    in_grad_ref[...] = in_grad

    i0, i1 = halves(in_grad)
    pos_grad = dot(hits, i0) + dot(hits, i1)
    gain1 = jnp.sum(d_y1 * n1, axis=0, keepdims=True)
    shift1 = jnp.sum(d_y1, axis=0, keepdims=True)
    row = lax.broadcasted_iota(jnp.int32, (64, 384), 0)
    for at, value in ((50, gain1), (51, shift1), (52, gain2), (53, shift2)):
        pos_grad = jnp.where(row == at, jnp.broadcast_to(value, (64, 384)), pos_grad)
    small = dot(small_ref[...], jnp.where(half == 0, pos_grad, 0.0).astype(BF))
    right = jnp.where(half == 0, d_attn, y1)
    for s in range(2):
        left = jnp.where(half == 0, ctx_pads[s], d_pads[s])
        grad = (dot_tn(left, right) + small).reshape(16, GROUP, 384)
        if s == 0:
            keep_ref[16:] = grad
        else:
            send_ref[16:] = grad.astype(BF)


def run_layer(where, res_ids, offsets, tokens, cotangent, table, norms, pos, own, other):
    count = tokens.shape[0]
    places = jnp.asarray(unit_places(), BF)
    small = jnp.asarray(small_places(), BF)
    smem = pl.BlockSpec(memory_space=pltpu.SMEM)
    vmem = pl.BlockSpec(memory_space=pltpu.VMEM)
    return pl.pallas_call(
        layer_kernel,
        out_shape=(
            jax.ShapeDtypeStruct((count, D), BF),
            jax.ShapeDtypeStruct((count, D), F32),
            jax.ShapeDtypeStruct((32, GROUP, D), F32),
            jax.ShapeDtypeStruct((32, GROUP, D), BF),
        ),
        in_specs=[smem] * 3 + [vmem] * 9,
        out_specs=(vmem,) * 4,
        scratch_shapes=[
            pltpu.VMEM((1536, D), BF),
            pltpu.VMEM((1536, D), BF),
            pltpu.VMEM((1536, D), BF),
            pltpu.VMEM((HEADS, count, count), F32),
            pltpu.VMEM((count, 1152), BF),
            pltpu.VMEM((count, D), BF),
            pltpu.VMEM((count, 1152), BF),
        ],
        compiler_params=pltpu.CompilerParams(vmem_limit_bytes=VMEM),
        cost_estimate=pl.CostEstimate(
            flops=6_000_000_000, bytes_accessed=16_000_000, transcendentals=2_000_000
        ),
        name="layer",
    )(where, res_ids, offsets, tokens, cotangent, table, norms, pos, own, other, places, small)


def product(a, b):
    (ah, al), (bh, bl) = a, b
    return dot(ah, bh) + (dot(ah, bl) + dot(al, bh))


def orth_kernel(
    where_ref, factor_ref, g_own_ref, g_oth_ref, o_own_ref, o_oth_ref, piece_ref, out_ref, grad_ref, m_ref
):
    xy = where_ref[2]
    is_out = where_ref[3]
    factor = factor_ref[0]
    row = lax.broadcasted_iota(jnp.int32, (GROUP, D), 0) % BLOCK
    valid = ((is_out == 0) | (row >= 9)).astype(F32)

    def fill(at, total):
        for s, (g, o) in enumerate(((g_own_ref, o_own_ref), (g_oth_ref, o_oth_ref))):
            m = MOMENTUM * group_rows(o, 0, at) + factor * (g[at].astype(F32) * valid)
            total = total + m * m
            m_ref[pl.ds(pl.multiple_of(s * 768 + at * GROUP, 16), GROUP), :] = m.astype(BF)
        return total

    total = lax.fori_loop(0, 16, fill, jnp.zeros((GROUP, D), F32))
    inv = 1.0 / (jnp.sqrt(jnp.sum(total)) + 1e-07)
    whole = m_ref[...]
    gram = dot_tn(whole, whole) * (inv * inv)
    eye = (
        lax.broadcasted_iota(jnp.int32, (D, D), 0) == lax.broadcasted_iota(jnp.int32, (D, D), 1)
    ).astype(F32)
    run = None
    for step in range(NS_STEPS):
        parts = halves(gram)
        poly = COEF_A * eye + COEF_B * gram + COEF_C * product(parts, parts)
        poly_parts = halves(poly)
        run = poly if run is None else product(poly_parts, halves(run))
        if step < NS_STEPS - 1:
            gram = product(halves(product(poly_parts, parts)), poly_parts)
    mine = MOMENTUM * group_rows(o_own_ref, 0, xy) + factor * (piece_ref[...] * valid)
    out_ref[...] = product(halves(mine * inv), halves(run))
    grad_ref[...] = piece_ref[...] * valid


def run_orth(where, factor, g_own, g_oth, o_own, o_oth, piece):
    smem = pl.BlockSpec(memory_space=pltpu.SMEM)
    vmem = pl.BlockSpec(memory_space=pltpu.VMEM)
    return pl.pallas_call(
        orth_kernel,
        out_shape=(jax.ShapeDtypeStruct((GROUP, D), F32), jax.ShapeDtypeStruct((GROUP, D), F32)),
        in_specs=[smem] * 2 + [vmem] * 5,
        out_specs=(vmem, vmem),
        scratch_shapes=[pltpu.VMEM((1536, D), BF)],
        compiler_params=pltpu.CompilerParams(vmem_limit_bytes=VMEM),
        cost_estimate=pl.CostEstimate(
            flops=8_000_000_000, bytes_accessed=4_000_000, transcendentals=0
        ),
        name="orth",
    )(where, factor, g_own, g_oth, o_own, o_oth, piece)


def swapped(value):
    return lax.ppermute(value, "c", [(0, 1), (1, 0)])


def exchanged(value, axes):
    return lax.all_to_all(value, axes, 0, 0, tiled=True)


def everywhere(value, axes):
    peers = lax.axis_size(axes)
    return exchanged(jnp.broadcast_to(value[None], (peers, *value.shape)), axes)


def step_rate(rows_count, cols_count):
    return math.sqrt(max(rows_count, cols_count) / rows_count)


def padded(rows, before, total):
    return jnp.pad(rows, ((before, total - before - rows.shape[0]), (0, 0)))


def shards(
    tokens,
    cotangent,
    pos_table,
    norm_params,
    qkv_weight,
    out_weight,
    up_weight,
    down_weight,
    qkv_moment,
    out_moment,
    up_moment,
    down_moment,
    norm_moment,
    pos_moment,
    res_ids,
    offsets,
    pos_index,
):
    z = lax.axis_index(COLUMN)
    xy = lax.axis_index(PLANE)
    zh = lax.axis_index("zh")
    is_out = (z == 1).astype(jnp.int32)
    where = jnp.stack([lax.axis_index("c"), zh, xy, is_out]).astype(jnp.int32)

    rows = jnp.concatenate([up_weight.T, down_weight, qkv_weight.T, out_weight], axis=0).astype(BF)
    own = everywhere(padded(rows, 0, SENT), CHIPS)
    other = swapped(own)

    old = jnp.stack(
        [
            padded(up_moment.T, 0, 16),
            padded(out_moment, 9, 16),
            padded(down_moment, 0, 16),
            padded(qkv_moment.T, 0, 16),
        ]
    ).astype(BF)
    old = exchanged(
        jnp.broadcast_to(old[:, None], (4, 16, 16, D)).reshape(64, 16, D), CHIPS
    )
    old_other = swapped(old)

    result, in_grad, keep, send = run_layer(
        where,
        res_ids,
        offsets,
        tokens,
        cotangent,
        padded(pos_table, 0, 64),
        norm_params,
        pos_index.reshape(1, -1),
        own,
        other,
    )
    pair = (keep + swapped(send).astype(F32)).astype(BF)
    piece = jnp.sum(exchanged(pair, HALF).astype(F32), axis=0)
    grads = everywhere(piece.astype(BF), PLANE)
    grads_other = swapped(grads)

    small = grads.reshape(16, 4, BLOCK, D)[:, :, 0].reshape(64, D).astype(F32)
    valid = (is_out == 0) | (jnp.arange(GROUP)[None, :, None] % BLOCK >= 9)
    wide = jnp.where(valid, grads.astype(F32), 0.0)
    wide_other = jnp.where(valid, grads_other.astype(F32), 0.0)
    squares = jnp.sum(wide * wide) + jnp.sum(wide_other * wide_other)
    squares = squares + jnp.where(is_out == 1, jnp.sum(small * small), 0.0)
    message = jnp.concatenate([small, jnp.broadcast_to(squares, (8, D))], axis=0)
    told = everywhere(message, COLUMN)
    grad_norm = jnp.sqrt(jnp.sum(told[:, 64, 0]))
    factor = jnp.minimum(1.0, CLIP_LIMIT / (grad_norm + 1e-06))
    pos_sum, norm_sum = told[1, :50], told[1, 50:54]

    orth, grad = run_orth(
        where, factor.reshape(1), grads, grads_other, old, old_other, piece
    )
    back = exchanged(
        jnp.concatenate([orth.reshape(4, BLOCK, D), grad.reshape(4, BLOCK, D)], axis=1), COLUMN
    )

    def fresh(moment, z_from, first, last, turn):
        block = back[z_from, BLOCK + first : BLOCK + last]
        return MOMENTUM * moment + factor * (block.T if turn else block)

    def stepped(weight, z_from, first, last, turn, rate):
        block = back[z_from, first:last]
        return weight - rate * (block.T if turn else block)

    norm_fresh = MOMENTUM * norm_moment + factor * norm_sum
    pos_fresh = MOMENTUM * pos_moment + factor * pos_sum
    return (
        result,
        in_grad,
        grad_norm,
        fresh(qkv_moment, 3, 0, 9, True),
        stepped(qkv_weight, 3, 0, 9, True, step_rate(D, 3 * D)),
        fresh(out_moment, 1, 9, 12, False),
        stepped(out_weight, 1, 9, 12, False, step_rate(D, D)),
        fresh(up_moment, 0, 0, 12, True),
        stepped(up_weight, 0, 0, 12, True, step_rate(D, FF)),
        fresh(down_moment, 2, 0, 12, False),
        stepped(down_weight, 2, 0, 12, False, step_rate(FF, D)),
        norm_fresh,
        norm_params - NORM_RATE * norm_fresh,
        pos_fresh,
        pos_table - SMALL_RATE * pos_fresh,
    )


def solution(mesh):
    finer = Mesh(
        mesh.devices.reshape(2, 4, 4, 2, mesh.shape["tensor"]), ("zl", "x", "y", "c", "zh")
    )
    columns = P(None, ROWS)
    rows = P(ROWS, None)
    return jax.shard_map(
        shards,
        mesh=finer,
        in_specs=(
            P(DP, None),
            P(DP, None),
            P(),
            P(),
            columns,
            rows,
            columns,
            rows,
            columns,
            rows,
            columns,
            rows,
            P(),
            P(),
            P(DP),
            P(DP),
            P(DP),
        ),
        out_specs=(
            P(DP, None),
            P(DP, None),
            P(),
            columns,
            columns,
            rows,
            rows,
            columns,
            columns,
            rows,
            rows,
            P(),
            P(),
            P(),
            P(),
        ),
        check_vma=False,
    )
```

```python
import math

import jax
import jax.numpy as jnp
import numpy as np
from jax import lax
from jax.experimental import pallas as pl
from jax.experimental.pallas import tpu as pltpu
from jax.sharding import Mesh
from jax.sharding import PartitionSpec as P

D = 384
HEADS = 6
HD = 64
FF = 1536
SMALL_LEN = 50
BIG_LEN = 145
NS_STEPS = 5
COEF_A = 3.4445
COEF_B = -4.775
COEF_C = 2.0315
NORM_EPS = 1e-06
CLIP_LIMIT = 1.0
MOMENTUM = 0.5
SMALL_RATE = 10.0
NORM_RATE = 40.0

DP = ("zl", "x", "y", "c")
ROWS = ("zh",) + DP
COLUMN = ("zh", "zl")
PLANE = ("x", "y")
HALF = ("zl", "x", "y")
CHIPS = ("zh", "zl", "x", "y")

BF = jnp.bfloat16
F32 = jnp.float32
BLOCK = 12
GROUP = 48
SENT = 40
VMEM = 60 << 20


def unit_places():
    places = np.zeros((2, 768, 1536), np.float32)
    for core in range(2):
        for xy in range(16):
            for z in range(4):
                block = (z * 16 + xy) * 2 + core
                for r in range(BLOCK):
                    row = xy * GROUP + z * BLOCK + r
                    if r < 9:
                        head, rest = divmod(block * 9 + r, 192)
                        part, e = divmod(rest, 64)
                        places[core, row, part * 384 + head * 64 + e] = 1
                    else:
                        places[core, row, 1152 + block * 3 + r - 9] = 1
    return places


def small_places():
    places = np.zeros((768, 64), np.float32)
    for n in range(64):
        places[(n // 4) * GROUP + (n % 4) * BLOCK, n] = 1
    return places


def dot(a, b):
    return lax.dot_general(a, b, (((1,), (0,)), ((), ())), preferred_element_type=F32)


def dot_nt(a, b):
    return lax.dot_general(a, b, (((1,), (1,)), ((), ())), preferred_element_type=F32)


def dot_tn(a, b):
    return lax.dot_general(a, b, (((0,), (0,)), ((), ())), preferred_element_type=F32)


def halves(a):
    high = a.astype(BF)
    return high, (a - high.astype(F32)).astype(BF)


def norm_parts(v):
    cen = v - jnp.mean(v, axis=-1, keepdims=True)
    var = jnp.mean(cen * cen, axis=-1, keepdims=True)
    r = lax.rsqrt(var + NORM_EPS)
    return cen * r, r


def norm_back(dy, n, r, gain):
    e = dy * gain
    return r * (
        e - jnp.mean(e, axis=-1, keepdims=True) - n * jnp.mean(e * n, axis=-1, keepdims=True)
    )


def group_rows(source, first, xy):
    return jnp.concatenate(
        [source[z * 16 + xy].astype(F32)[first : first + BLOCK] for z in range(4)], axis=0
    )


def layer_kernel(
    where_ref,
    res_ref,
    off_ref,
    tok_ref,
    cot_ref,
    table_ref,
    norms_ref,
    pos_ref,
    own_ref,
    oth_ref,
    places_ref,
    small_ref,
    result_ref,
    in_grad_ref,
    keep_ref,
    send_ref,
    wup,
    wdn,
    wat,
    probs_ref,
    qkv_ref,
    ctx_ref,
    dqkv_ref,
):
    core = where_ref[0]
    half = where_ref[1]
    count = tok_ref.shape[0]

    for s, src in enumerate((own_ref, oth_ref)):

        def regroup(xy, _, s=s, src=src):
            at = pl.multiple_of(s * 768 + xy * GROUP, 16)
            for first, dst in ((0, wup), (12, wdn), (24, wat)):
                dst[pl.ds(at, GROUP), :] = group_rows(src, first, xy).astype(BF)
            return 0

        lax.fori_loop(0, 16, regroup, 0)

    def place(s):
        return core if s == 0 else 1 - core

    hits = (
        lax.broadcasted_iota(jnp.int32, (64, count), 0) == jnp.broadcast_to(pos_ref[...], (64, count))
    ).astype(BF)
    table = table_ref[...]
    t0, t_rest = halves(table)
    t1, t2 = halves(table - t0.astype(F32))
    stream_in = tok_ref[...].astype(F32) + ((dot_tn(hits, t2) + dot_tn(hits, t1)) + dot_tn(hits, t0))
    g1, s1, g2, s2 = (norms_ref[k : k + 1, :] for k in range(4))
    n1, r1 = norm_parts(stream_in)
    y1 = (n1 * g1 + s1).astype(BF)
    qkv = 0.0
    for s in range(2):
        pad = dot_nt(y1, wat[s * 768 : (s + 1) * 768, :]).astype(BF)
        qkv = qkv + dot(pad, places_ref[place(s), :, :1152])
    qkv_ref[...] = qkv.astype(BF)

    def segments(shape, dim):
        at = lax.broadcasted_iota(jnp.int32, shape, dim)
        seg = at + 8
        for k in range(5):
            res = res_ref[k]
            off = off_ref[k]
            length = jnp.where(res == 0, SMALL_LEN, jnp.where(res == 1, BIG_LEN, 0))
            seg = jnp.where((at >= off) & (at < off + length), k, seg)
        return seg

    allowed = segments((count, count), 0) == segments((count, count), 1)
    lane = lax.broadcasted_iota(jnp.int32, (1, 128), 1)
    masks = ((lane < HD).astype(F32).astype(BF), (lane >= HD).astype(F32).astype(BF))
    scale = HD**-0.5
    for p in range(HEADS // 2):
        lo = p * 128
        q = qkv_ref[:, lo : lo + 128]
        k = qkv_ref[:, 384 + lo : 512 + lo]
        v = qkv_ref[:, 768 + lo : 896 + lo]
        ctx = 0.0
        for hh in range(2):
            scores = dot_nt(q * masks[hh], k) * scale
            scores = jnp.where(allowed, scores, -1e30)
            expo = jnp.exp(scores - jnp.max(scores, axis=-1, keepdims=True))
            probs = expo / jnp.sum(expo, axis=-1, keepdims=True)
            probs_ref[2 * p + hh] = probs
            ctx = ctx + dot(probs.astype(BF), v * masks[hh])
        ctx_ref[:, lo : lo + 128] = ctx.astype(BF)
    ctx_pads = [
        dot_nt(ctx_ref[...], places_ref[place(s), :, 1152:]).astype(BF) for s in range(2)
    ]
    stream_mid = stream_in + (dot(ctx_pads[0], wat[:768, :]) + dot(ctx_pads[1], wat[768:, :]))
    n2, r2 = norm_parts(stream_mid)
    y2 = (n2 * g2 + s2).astype(BF)

    cot = cot_ref[...]
    right = jnp.where(half == 0, y2, cot)
    out = stream_mid
    d_y2 = 0.0
    for k in range(4):
        wu = wup[k * 384 : (k + 1) * 384, :]
        wd = wdn[k * 384 : (k + 1) * 384, :]
        pre = dot_nt(y2, wu)
        cdf = 0.5 * (1.0 + lax.erf(pre * (2.0**-0.5)))
        hidden = (pre * cdf).astype(BF)
        slope = cdf + pre * (jnp.exp(-0.5 * pre * pre) * ((2.0 * math.pi) ** -0.5))
        d_pre = (slope * dot_nt(cot, wd)).astype(BF)
        out = out + dot(hidden, wd)
        d_y2 = d_y2 + dot(d_pre, wu)
        grad = dot_tn(jnp.where(half == 0, d_pre, hidden), right).reshape(8, GROUP, 384)
        at = (k % 2) * 8
        if k < 2:
            keep_ref[at : at + 8] = grad.astype(BF)
        else:
            send_ref[at : at + 8] = grad.astype(BF)
    result_ref[...] = out.astype(BF)
    gain2 = jnp.sum(d_y2 * n2, axis=0, keepdims=True)
    shift2 = jnp.sum(d_y2, axis=0, keepdims=True)
    d_mid = cot.astype(F32) + norm_back(d_y2, n2, r2, g2)

    d_attn = d_mid.astype(BF)
    d_ctx = 0.0
    for s in range(2):
        pad = dot_nt(d_attn, wat[s * 768 : (s + 1) * 768, :]).astype(BF)
        d_ctx = d_ctx + dot(pad, places_ref[place(s), :, 1152:])
    d_ctx = d_ctx.astype(BF)
    for p in range(HEADS // 2):
        lo = p * 128
        q = qkv_ref[:, lo : lo + 128]
        k = qkv_ref[:, 384 + lo : 512 + lo]
        v = qkv_ref[:, 768 + lo : 896 + lo]
        dc = d_ctx[:, lo : lo + 128]
        dq, dk, dv = 0.0, 0.0, 0.0
        for hh in range(2):
            probs = probs_ref[2 * p + hh]
            dcm = dc * masks[hh]
            d_probs = dot_nt(dcm, v)
            inner = jnp.sum(probs * d_probs, axis=-1, keepdims=True)
            d_scores = (probs * (d_probs - inner)).astype(BF)
            dq = dq + dot(d_scores, k * masks[hh])
            dk = dk + dot_tn(d_scores, q * masks[hh])
            dv = dv + dot_tn(probs.astype(BF), dcm)
        dqkv_ref[:, lo : lo + 128] = (dq * scale).astype(BF)
        dqkv_ref[:, 384 + lo : 512 + lo] = (dk * scale).astype(BF)
        dqkv_ref[:, 768 + lo : 896 + lo] = dv.astype(BF)
    d_pads = [
        dot_nt(dqkv_ref[...], places_ref[place(s), :, :1152]).astype(BF) for s in range(2)
    ]
    d_y1 = dot(d_pads[0], wat[:768, :]) + dot(d_pads[1], wat[768:, :])
    in_grad = d_mid + norm_back(d_y1, n1, r1, g1)
    in_grad_ref[...] = in_grad

    i0, i1 = halves(in_grad)
    pos_grad = dot(hits, i0) + dot(hits, i1)
    gain1 = jnp.sum(d_y1 * n1, axis=0, keepdims=True)
    shift1 = jnp.sum(d_y1, axis=0, keepdims=True)
    row = lax.broadcasted_iota(jnp.int32, (64, 384), 0)
    for at, value in ((50, gain1), (51, shift1), (52, gain2), (53, shift2)):
        pos_grad = jnp.where(row == at, jnp.broadcast_to(value, (64, 384)), pos_grad)
    small = dot(small_ref[...], jnp.where(half == 0, pos_grad, 0.0).astype(BF))
    right = jnp.where(half == 0, d_attn, y1)
    for s in range(2):
        left = jnp.where(half == 0, ctx_pads[s], d_pads[s])
        grad = (dot_tn(left, right) + small).reshape(16, GROUP, 384)
        if s == 0:
            keep_ref[16:] = grad.astype(BF)
        else:
            send_ref[16:] = grad.astype(BF)


def run_layer(where, res_ids, offsets, tokens, cotangent, table, norms, pos, own, other):
    count = tokens.shape[0]
    places = jnp.asarray(unit_places(), BF)
    small = jnp.asarray(small_places(), BF)
    smem = pl.BlockSpec(memory_space=pltpu.SMEM)
    vmem = pl.BlockSpec(memory_space=pltpu.VMEM)
    return pl.pallas_call(
        layer_kernel,
        out_shape=(
            jax.ShapeDtypeStruct((count, D), BF),
            jax.ShapeDtypeStruct((count, D), F32),
            jax.ShapeDtypeStruct((32, GROUP, D), BF),
            jax.ShapeDtypeStruct((32, GROUP, D), BF),
        ),
        in_specs=[smem] * 3 + [vmem] * 9,
        out_specs=(vmem,) * 4,
        scratch_shapes=[
            pltpu.VMEM((1536, D), BF),
            pltpu.VMEM((1536, D), BF),
            pltpu.VMEM((1536, D), BF),
            pltpu.VMEM((HEADS, count, count), F32),
            pltpu.VMEM((count, 1152), BF),
            pltpu.VMEM((count, D), BF),
            pltpu.VMEM((count, 1152), BF),
        ],
        compiler_params=pltpu.CompilerParams(vmem_limit_bytes=VMEM),
        cost_estimate=pl.CostEstimate(
            flops=6_000_000_000, bytes_accessed=16_000_000, transcendentals=2_000_000
        ),
        name="layer",
    )(where, res_ids, offsets, tokens, cotangent, table, norms, pos, own, other, places, small)


def product(a, b):
    (ah, al), (bh, bl) = a, b
    return dot(ah, bh) + (dot(ah, bl) + dot(al, bh))


def call(kernel, name, outs, args, scalars=0, scratch=(), flops=0, moved=0):
    smem = pl.BlockSpec(memory_space=pltpu.SMEM)
    vmem = pl.BlockSpec(memory_space=pltpu.VMEM)
    return pl.pallas_call(
        kernel,
        out_shape=tuple(jax.ShapeDtypeStruct(shape, dtype) for shape, dtype in outs),
        in_specs=[smem] * scalars + [vmem] * (len(args) - scalars),
        out_specs=(vmem,) * len(outs),
        scratch_shapes=scratch,
        compiler_params=pltpu.CompilerParams(vmem_limit_bytes=VMEM),
        cost_estimate=pl.CostEstimate(flops=flops, bytes_accessed=moved, transcendentals=0),
        name=name,
    )(*args)


def prepare_kernel(qkv_ref, out_ref, up_ref, down_ref, qkv_m_ref, out_m_ref, up_m_ref, down_m_ref, rows_ref, old_ref):
    zeros = jnp.zeros((16, D), F32)
    rows = jnp.concatenate(
        [up_ref[...], down_ref[...], qkv_ref[...], out_ref[...], zeros[: SENT - 36]], axis=0
    ).astype(BF)
    rows_ref[...] = jnp.broadcast_to(rows[None], rows_ref.shape)
    old = (
        jnp.concatenate([up_m_ref[...], zeros[:4]], axis=0),
        jnp.concatenate([zeros[:9], out_m_ref[...], zeros[:4]], axis=0),
        jnp.concatenate([down_m_ref[...], zeros[:4]], axis=0),
        jnp.concatenate([qkv_m_ref[...], zeros[:7]], axis=0),
    )
    for z in range(4):
        old_ref[z * 16 : (z + 1) * 16] = jnp.broadcast_to(old[z].astype(BF)[None], (16, 16, D))


def valid_rows(is_out):
    row = lax.broadcasted_iota(jnp.int32, (GROUP, D), 0) % BLOCK
    return ((is_out == 0) | (row >= 9)).astype(F32)


def tell_kernel(where_ref, own_ref, oth_ref, piece_ref, small_ref, told_ref):
    is_out = where_ref[3]
    valid = valid_rows(is_out)
    total = jnp.zeros((GROUP, D), F32)
    for xy in range(16):
        for ref in (own_ref, oth_ref):
            g = ref[xy].astype(F32) * valid
            total = total + g * g
    small = dot_tn(small_ref[...], own_ref[...].reshape(768, D))
    squares = jnp.sum(total) + jnp.where(is_out == 1, jnp.sum(small * small), 0.0)
    squares = jnp.full((1, D), squares, F32)
    high = squares.astype(BF).astype(F32)
    mid = (squares - high).astype(BF).astype(F32)
    low = squares - high - mid
    for z in range(4):
        told_ref[z] = jnp.concatenate(
            [small, piece_ref[z * BLOCK : (z + 1) * BLOCK, :], high, mid, low, jnp.zeros((1, D), F32)],
            axis=0,
        ).astype(BF)


def clip(told_ref):
    total = jnp.zeros((1, 1), F32)
    for z in range(4):
        for k in range(3):
            total = total + told_ref[z, 76 + k : 77 + k, :].astype(F32)[:, :1]
    grad_norm = jnp.sqrt(total)
    return grad_norm, jnp.minimum(1.0, CLIP_LIMIT / (grad_norm + 1e-06))


def gram_kernel(where_ref, g_own_ref, g_oth_ref, o_own_ref, o_oth_ref, gram_ref, both_ref):
    valid = valid_rows(where_ref[3])

    def fill(xy, _):
        for s, (g, o) in enumerate(((g_own_ref, o_own_ref), (g_oth_ref, o_oth_ref))):
            at = pl.ds(pl.multiple_of(s * 768 + xy * GROUP, 16), GROUP)
            both_ref[at, :D] = group_rows(o, 0, xy).astype(BF)
            both_ref[at, D:] = (g[xy].astype(F32) * valid).astype(BF)
        return 0

    lax.fori_loop(0, 16, fill, 0)
    both = both_ref[...]
    gram_ref[...] = dot_tn(both, both)


def orth_kernel(where_ref, told_ref, gram_ref, o_own_ref, piece_ref, out_ref):
    xy = where_ref[2]
    valid = valid_rows(where_ref[3])
    factor = clip(told_ref)[1]
    gram = (
        (MOMENTUM * MOMENTUM) * gram_ref[:D, :D]
        + (MOMENTUM * factor) * (gram_ref[:D, D:] + gram_ref[D:, :D])
        + (factor * factor) * gram_ref[D:, D:]
    )
    eye = (
        lax.broadcasted_iota(jnp.int32, (D, D), 0) == lax.broadcasted_iota(jnp.int32, (D, D), 1)
    ).astype(F32)
    inv = 1.0 / (jnp.sqrt(jnp.sum(gram * eye)) + 1e-07)
    gram = gram * (inv * inv)
    run = None
    for step in range(NS_STEPS):
        parts = halves(gram)
        poly = COEF_A * eye + COEF_B * gram + COEF_C * product(parts, parts)
        poly_parts = halves(poly)
        run = poly if run is None else product(poly_parts, halves(run))
        if step < NS_STEPS - 1:
            gram = product(halves(product(poly_parts, parts)), poly_parts)
    mine = MOMENTUM * group_rows(o_own_ref, 0, xy) + factor * (piece_ref[...] * valid)
    orth = product(halves(mine * inv), halves(run))
    for z in range(4):
        out_ref[z] = jnp.concatenate(
            [orth[z * BLOCK : (z + 1) * BLOCK], jnp.zeros((4, D), F32)], axis=0
        ).astype(BF)


def step_rate(rows_count, cols_count):
    return math.sqrt(max(rows_count, cols_count) / rows_count)


def update_kernel(
    told_ref,
    back_ref,
    qkv_ref,
    out_ref,
    up_ref,
    down_ref,
    qkv_m_ref,
    out_m_ref,
    up_m_ref,
    down_m_ref,
    norms_ref,
    norm_m_ref,
    table_ref,
    pos_m_ref,
    grad_norm_ref,
    qkv_m_next,
    qkv_next,
    out_m_next,
    out_next,
    up_m_next,
    up_next,
    down_m_next,
    down_next,
    norm_m_next,
    norms_next,
    pos_m_next,
    table_next,
):
    grad_norm, factor = clip(told_ref)
    grad_norm_ref[...] = grad_norm
    for z, first, last, rate, w_ref, m_ref, w_next, m_next in (
        (3, 0, 9, step_rate(D, 3 * D), qkv_ref, qkv_m_ref, qkv_next, qkv_m_next),
        (1, 9, 12, step_rate(D, D), out_ref, out_m_ref, out_next, out_m_next),
        (0, 0, 12, step_rate(D, FF), up_ref, up_m_ref, up_next, up_m_next),
        (2, 0, 12, step_rate(FF, D), down_ref, down_m_ref, down_next, down_m_next),
    ):
        grad = told_ref[z].astype(F32)[64 + first : 64 + last]
        orth = back_ref[z].astype(F32)[first:last]
        m_next[...] = MOMENTUM * m_ref[...] + factor * grad
        w_next[...] = w_ref[...] - rate * orth
    small = told_ref[1].astype(F32)
    norm_fresh = MOMENTUM * norm_m_ref[...] + factor * small[50:54]
    norm_m_next[...] = norm_fresh
    norms_next[...] = norms_ref[...] - NORM_RATE * norm_fresh
    pos_fresh = MOMENTUM * pos_m_ref[...] + factor * small[:50]
    pos_m_next[...] = pos_fresh
    table_next[...] = table_ref[...] - SMALL_RATE * pos_fresh


def swapped(value):
    return lax.ppermute(value, "c", [(0, 1), (1, 0)])


def exchanged(value, axes):
    return lax.all_to_all(value, axes, 0, 0, tiled=True)


def everywhere(value, axes):
    peers = lax.axis_size(axes)
    return exchanged(jnp.broadcast_to(value[None], (peers, *value.shape)), axes)


def shards(
    tokens,
    cotangent,
    pos_table,
    norm_params,
    qkv_weight,
    out_weight,
    up_weight,
    down_weight,
    qkv_moment,
    out_moment,
    up_moment,
    down_moment,
    norm_moment,
    pos_moment,
    res_ids,
    offsets,
    pos_index,
):
    is_out = (lax.axis_index(COLUMN) == 1).astype(jnp.int32)
    where = jnp.stack(
        [lax.axis_index("c"), lax.axis_index("zh"), lax.axis_index(PLANE), is_out]
    ).astype(jnp.int32)
    weights = (qkv_weight.T, out_weight, up_weight.T, down_weight)
    moments = (qkv_moment.T, out_moment, up_moment.T, down_moment)

    rows, old = call(
        prepare_kernel,
        "prepare",
        (((64, SENT, D), BF), ((64, 16, D), BF)),
        weights + moments,
        moved=4_000_000,
    )
    own = exchanged(rows, CHIPS)
    own, old = lax.optimization_barrier((own, old))
    other = swapped(own)
    old = exchanged(old, CHIPS)

    result, in_grad, keep, send = run_layer(
        where,
        res_ids,
        offsets,
        tokens,
        cotangent,
        jnp.pad(pos_table, ((0, 14), (0, 0))),
        norm_params,
        pos_index.reshape(1, -1),
        own,
        other,
    )
    keep, send, old = lax.optimization_barrier((keep, send, old))
    old_other = swapped(old)
    pair = (keep.astype(F32) + swapped(send).astype(F32)).astype(BF)
    piece = jnp.sum(exchanged(pair, HALF).astype(F32), axis=0)
    grads = everywhere(piece.astype(BF), PLANE)
    grads_other = swapped(grads)

    small = jnp.asarray(small_places(), BF)
    (told,) = call(
        tell_kernel,
        "tell",
        (((4, 80, D), BF),),
        (where, grads, grads_other, piece, small),
        scalars=1,
        moved=2_000_000,
    )
    told = exchanged(told, COLUMN)
    (gram,) = call(
        gram_kernel,
        "gram",
        (((2 * D, 2 * D), F32),),
        (where, grads, grads_other, old, old_other),
        scalars=1,
        scratch=[pltpu.VMEM((1536, 2 * D), BF)],
        flops=3_000_000_000,
        moved=5_000_000,
    )
    (orth,) = call(
        orth_kernel,
        "orth",
        (((4, 16, D), BF),),
        (where, told, gram, old, piece),
        scalars=1,
        flops=8_000_000_000,
        moved=4_000_000,
    )
    back = exchanged(orth, COLUMN)
    like = lambda a: (a.shape, F32)
    grad_norm, *news = call(
        update_kernel,
        "update",
        (
            ((1, 1), F32),
            *(like(a) for pair_of in zip(moments, weights) for a in pair_of),
            like(norm_moment),
            like(norm_params),
            like(pos_moment),
            like(pos_table),
        ),
        (told, back, *weights, *moments, norm_params, norm_moment, pos_table, pos_moment),
        moved=2_000_000,
    )
    for k in (0, 1, 4, 5):
        news[k] = news[k].T
    return (result, in_grad, grad_norm.reshape(()), *news)


def solution(mesh):
    finer = Mesh(
        mesh.devices.reshape(2, 4, 4, 2, mesh.shape["tensor"]), ("zl", "x", "y", "c", "zh")
    )
    columns = P(None, ROWS)
    rows = P(ROWS, None)
    return jax.shard_map(
        shards,
        mesh=finer,
        in_specs=(
            P(DP, None),
            P(DP, None),
            P(),
            P(),
            columns,
            rows,
            columns,
            rows,
            columns,
            rows,
            columns,
            rows,
            P(),
            P(),
            P(DP),
            P(DP),
            P(DP),
        ),
        out_specs=(
            P(DP, None),
            P(DP, None),
            P(),
            columns,
            columns,
            rows,
            rows,
            columns,
            columns,
            rows,
            rows,
            P(),
            P(),
            P(),
            P(),
        ),
        check_vma=False,
    )
```

```python
import math

import jax
import jax.numpy as jnp
import numpy as np
from jax import lax
from jax.experimental import pallas as pl
from jax.experimental.pallas import tpu as pltpu
from jax.sharding import Mesh
from jax.sharding import PartitionSpec as P

D = 384
HEADS = 6
HD = 64
FF = 1536
SMALL_LEN = 50
BIG_LEN = 145
NS_STEPS = 5
COEF_A = 3.4445
COEF_B = -4.775
COEF_C = 2.0315
NORM_EPS = 1e-06
CLIP_LIMIT = 1.0
MOMENTUM = 0.5
SMALL_RATE = 10.0
NORM_RATE = 40.0

DP = ("zl", "x", "y", "c")
ROWS = ("zh",) + DP
COLUMN = ("zh", "zl")
PLANE = ("x", "y")
HALF = ("zl", "x", "y")
COLUMN_CORES = ("zh", "zl", "c")
AXES = ("zl", "x", "y", "c", "zh")

BF = jnp.bfloat16
F32 = jnp.float32
BLOCK = 12
GROUP = 48
SENT = 40
VMEM = 60 << 20
LAYER_VMEM = 60 << 20


def unit_places():
    places = np.zeros((2, 768, 1536), np.float32)
    for core in range(2):
        for xy in range(16):
            for z in range(4):
                block = (z * 16 + xy) * 2 + core
                for r in range(BLOCK):
                    row = xy * GROUP + z * BLOCK + r
                    if r < 9:
                        head, rest = divmod(block * 9 + r, 192)
                        part, e = divmod(rest, 64)
                        places[core, row, part * 384 + head * 64 + e] = 1
                    else:
                        places[core, row, 1152 + block * 3 + r - 9] = 1
    return places


def small_places():
    places = np.zeros((768, 64), np.float32)
    for n in range(64):
        places[(n // 4) * GROUP + (n % 4) * BLOCK, n] = 1
    return places


def dot(a, b):
    return lax.dot_general(a, b, (((1,), (0,)), ((), ())), preferred_element_type=F32)


def dot_nt(a, b):
    return lax.dot_general(a, b, (((1,), (1,)), ((), ())), preferred_element_type=F32)


def dot_tn(a, b):
    return lax.dot_general(a, b, (((0,), (0,)), ((), ())), preferred_element_type=F32)


def halves(a):
    high = a.astype(BF)
    return high, (a - high.astype(F32)).astype(BF)


def norm_parts(v):
    cen = v - jnp.mean(v, axis=-1, keepdims=True)
    var = jnp.mean(cen * cen, axis=-1, keepdims=True)
    r = lax.rsqrt(var + NORM_EPS)
    return cen * r, r


def norm_back(dy, n, r, gain):
    e = dy * gain
    return r * (
        e - jnp.mean(e, axis=-1, keepdims=True) - n * jnp.mean(e * n, axis=-1, keepdims=True)
    )


def device(x, y, z, core):
    x, y, z = x % 4, y % 4, z % 4
    return ((((z % 2) * 4 + x) * 4 + y) * 2 + core) * 2 + z // 2


def devices():
    return [(x, y, z, c) for x in range(4) for y in range(4) for z in range(4) for c in range(2)]


def column_step(step):
    return [(device(x, y, z + step, c), device(x, y, z, c)) for x, y, z, c in devices()]


def colour_groups():
    return [
        [device(x, y, x + 2 * y - colour, core) for x in range(4) for y in range(4)]
        for colour in range(4)
        for core in range(2)
    ]


def colour_step(step):
    sources = {
        1: ((1, 0, 0), (0, 0, -1)),
        2: ((0, 1, 0), (0, -1, 0)),
        3: ((-1, 0, 0), (0, 0, 1)),
    }[step]
    return [
        (device(x + sources[c][0], y + sources[c][1], z + sources[c][2], c), device(x, y, z, c))
        for x, y, z, c in devices()
    ]


def layer_kernel(
    where_ref,
    res_ref,
    off_ref,
    tok_hbm,
    cot_hbm,
    table_hbm,
    norms_ref,
    pos_ref,
    own0,
    own1,
    own2,
    own3,
    oth0,
    oth1,
    oth2,
    oth3,
    places_hbm,
    small_ref,
    result_ref,
    in_grad_ref,
    keep_ref,
    send_ref,
    wup,
    wdn,
    wat,
    probs_ref,
    qkv_ref,
    ctx_ref,
    dqkv_ref,
    places_ref,
    tok_ref,
    cot_ref,
    table_ref,
    sems,
):
    core = where_ref[0]
    half = where_ref[1]
    colour = where_ref[4]
    count = tok_ref.shape[0]
    loads = [
        pltpu.make_async_copy(src, dst, sems.at[k])
        for k, (src, dst) in enumerate(
            ((tok_hbm, tok_ref), (places_hbm, places_ref), (cot_hbm, cot_ref))
        )
    ]
    for load in loads:
        load.start()
    table_ref[...] = jnp.zeros(table_ref.shape, F32)
    table_ref[: table_hbm.shape[0]] = table_hbm[...]

    for here in range(4):

        @pl.when(colour == here)
        def _(here=here):
            for s, refs in enumerate(((own0, own1, own2, own3), (oth0, oth1, oth2, oth3))):
                for xy in range(16):
                    ahead = xy // 4 + 2 * (xy % 4) - here
                    blocks = [refs[(ahead - z) % 4][xy].astype(F32) for z in range(4)]
                    at = s * 768 + xy * GROUP
                    for first, dst in ((0, wup), (12, wdn), (24, wat)):
                        dst[at : at + GROUP] = jnp.concatenate(
                            [block[first : first + BLOCK] for block in blocks], axis=0
                        ).astype(BF)

    for load in loads:
        load.wait()

    def place(s):
        return core if s == 0 else 1 - core

    hits = (
        lax.broadcasted_iota(jnp.int32, (64, count), 0) == jnp.broadcast_to(pos_ref[...], (64, count))
    ).astype(BF)
    table = table_ref[...]
    t0, t_rest = halves(table)
    t1, t2 = halves(table - t0.astype(F32))
    stream_in = tok_ref[...].astype(F32) + ((dot_tn(hits, t2) + dot_tn(hits, t1)) + dot_tn(hits, t0))
    g1, s1, g2, s2 = (norms_ref[k : k + 1, :] for k in range(4))
    n1, r1 = norm_parts(stream_in)
    y1 = (n1 * g1 + s1).astype(BF)
    qkv = 0.0
    for s in range(2):
        pad = dot_nt(y1, wat[s * 768 : (s + 1) * 768, :]).astype(BF)
        qkv = qkv + dot(pad, places_ref[place(s), :, :1152])
    qkv_ref[...] = qkv.astype(BF)

    def segments(shape, dim):
        at = lax.broadcasted_iota(jnp.int32, shape, dim)
        seg = at + 8
        for k in range(5):
            res = res_ref[k]
            off = off_ref[k]
            length = jnp.where(res == 0, SMALL_LEN, jnp.where(res == 1, BIG_LEN, 0))
            seg = jnp.where((at >= off) & (at < off + length), k, seg)
        return seg

    allowed = segments((count, count), 0) == segments((count, count), 1)
    lane = lax.broadcasted_iota(jnp.int32, (1, 128), 1)
    masks = ((lane < HD).astype(F32).astype(BF), (lane >= HD).astype(F32).astype(BF))
    scale = HD**-0.5
    for p in range(HEADS // 2):
        lo = p * 128
        q = qkv_ref[:, lo : lo + 128]
        k = qkv_ref[:, 384 + lo : 512 + lo]
        v = qkv_ref[:, 768 + lo : 896 + lo]
        ctx = 0.0
        for hh in range(2):
            scores = dot_nt(q * masks[hh], k) * scale
            scores = jnp.where(allowed, scores, -1e30)
            expo = jnp.exp(scores - jnp.max(scores, axis=-1, keepdims=True))
            probs = expo / jnp.sum(expo, axis=-1, keepdims=True)
            probs_ref[2 * p + hh] = probs
            ctx = ctx + dot(probs.astype(BF), v * masks[hh])
        ctx_ref[:, lo : lo + 128] = ctx.astype(BF)
    ctx_pads = [
        dot_nt(ctx_ref[...], places_ref[place(s), :, 1152:]).astype(BF) for s in range(2)
    ]
    stream_mid = stream_in + (dot(ctx_pads[0], wat[:768, :]) + dot(ctx_pads[1], wat[768:, :]))
    n2, r2 = norm_parts(stream_mid)
    y2 = (n2 * g2 + s2).astype(BF)

    cot = cot_ref[...]
    right = jnp.where(half == 0, y2, cot)
    out = stream_mid
    d_y2 = 0.0
    for k in range(4):
        wu = wup[k * 384 : (k + 1) * 384, :]
        wd = wdn[k * 384 : (k + 1) * 384, :]
        pre = dot_nt(y2, wu)
        cdf = 0.5 * (1.0 + lax.erf(pre * (2.0**-0.5)))
        hidden = (pre * cdf).astype(BF)
        slope = cdf + pre * (jnp.exp(-0.5 * pre * pre) * ((2.0 * math.pi) ** -0.5))
        d_pre = (slope * dot_nt(cot, wd)).astype(BF)
        out = out + dot(hidden, wd)
        d_y2 = d_y2 + dot(d_pre, wu)
        grad = dot_tn(jnp.where(half == 0, d_pre, hidden), right).reshape(8, GROUP, 384)
        at = (k % 2) * 8
        if k < 2:
            keep_ref[at : at + 8] = grad.astype(BF)
        else:
            send_ref[at : at + 8] = grad.astype(BF)
    result_ref[...] = out.astype(BF)
    gain2 = jnp.sum(d_y2 * n2, axis=0, keepdims=True)
    shift2 = jnp.sum(d_y2, axis=0, keepdims=True)
    d_mid = cot.astype(F32) + norm_back(d_y2, n2, r2, g2)

    d_attn = d_mid.astype(BF)
    d_ctx = 0.0
    for s in range(2):
        pad = dot_nt(d_attn, wat[s * 768 : (s + 1) * 768, :]).astype(BF)
        d_ctx = d_ctx + dot(pad, places_ref[place(s), :, 1152:])
    d_ctx = d_ctx.astype(BF)
    for p in range(HEADS // 2):
        lo = p * 128
        q = qkv_ref[:, lo : lo + 128]
        k = qkv_ref[:, 384 + lo : 512 + lo]
        v = qkv_ref[:, 768 + lo : 896 + lo]
        dc = d_ctx[:, lo : lo + 128]
        dq, dk, dv = 0.0, 0.0, 0.0
        for hh in range(2):
            probs = probs_ref[2 * p + hh]
            dcm = dc * masks[hh]
            d_probs = dot_nt(dcm, v)
            inner = jnp.sum(probs * d_probs, axis=-1, keepdims=True)
            d_scores = (probs * (d_probs - inner)).astype(BF)
            dq = dq + dot(d_scores, k * masks[hh])
            dk = dk + dot_tn(d_scores, q * masks[hh])
            dv = dv + dot_tn(probs.astype(BF), dcm)
        dqkv_ref[:, lo : lo + 128] = (dq * scale).astype(BF)
        dqkv_ref[:, 384 + lo : 512 + lo] = (dk * scale).astype(BF)
        dqkv_ref[:, 768 + lo : 896 + lo] = dv.astype(BF)
    d_pads = [
        dot_nt(dqkv_ref[...], places_ref[place(s), :, :1152]).astype(BF) for s in range(2)
    ]
    d_y1 = dot(d_pads[0], wat[:768, :]) + dot(d_pads[1], wat[768:, :])
    in_grad = d_mid + norm_back(d_y1, n1, r1, g1)
    in_grad_ref[...] = in_grad

    i0, i1 = halves(in_grad)
    pos_grad = dot(hits, i0) + dot(hits, i1)
    gain1 = jnp.sum(d_y1 * n1, axis=0, keepdims=True)
    shift1 = jnp.sum(d_y1, axis=0, keepdims=True)
    row = lax.broadcasted_iota(jnp.int32, (64, 384), 0)
    for at, value in ((50, gain1), (51, shift1), (52, gain2), (53, shift2)):
        pos_grad = jnp.where(row == at, jnp.broadcast_to(value, (64, 384)), pos_grad)
    small = dot(small_ref[...], jnp.where(half == 0, pos_grad, 0.0).astype(BF))
    right = jnp.where(half == 0, d_attn, y1)
    for s in range(2):
        left = jnp.where(half == 0, ctx_pads[s], d_pads[s])
        grad = (dot_tn(left, right) + small).reshape(16, GROUP, 384)
        if s == 0:
            keep_ref[16:] = grad.astype(BF)
        else:
            send_ref[16:] = grad.astype(BF)


def run_layer(where, res_ids, offsets, tokens, cotangent, table, norms, pos, weights):
    count = tokens.shape[0]
    places = jnp.asarray(unit_places(), BF)
    small = jnp.asarray(small_places(), BF)
    smem = pl.BlockSpec(memory_space=pltpu.SMEM)
    vmem = pl.BlockSpec(memory_space=pltpu.VMEM)
    hbm = pl.BlockSpec(memory_space=pl.ANY)
    return pl.pallas_call(
        layer_kernel,
        out_shape=(
            jax.ShapeDtypeStruct((count, D), BF),
            jax.ShapeDtypeStruct((count, D), F32),
            jax.ShapeDtypeStruct((32, GROUP, D), BF),
            jax.ShapeDtypeStruct((32, GROUP, D), BF),
        ),
        in_specs=[smem] * 3 + [hbm] * 2 + [vmem] * 11 + [hbm, vmem],
        out_specs=(vmem,) * 4,
        scratch_shapes=[
            pltpu.VMEM((1536, D), BF),
            pltpu.VMEM((1536, D), BF),
            pltpu.VMEM((1536, D), BF),
            pltpu.VMEM((HEADS, count, count), F32),
            pltpu.VMEM((count, 1152), BF),
            pltpu.VMEM((count, D), BF),
            pltpu.VMEM((count, 1152), BF),
            pltpu.VMEM((2, 768, 1536), BF),
            pltpu.VMEM((count, D), BF),
            pltpu.VMEM((count, D), BF),
            pltpu.VMEM((64, D), F32),
            pltpu.SemaphoreType.DMA((3,)),
        ],
        compiler_params=pltpu.CompilerParams(vmem_limit_bytes=LAYER_VMEM),
        cost_estimate=pl.CostEstimate(
            flops=0, bytes_accessed=0, transcendentals=0
        ),
        name="layer",
    )(
        where, res_ids, offsets, tokens, cotangent, table, norms, pos, *weights, places, small
    )


def product(a, b):
    (ah, al), (bh, bl) = a, b
    return dot(ah, bh) + (dot(ah, bl) + dot(al, bh))


def call(kernel, name, outs, args, scalars=0, scratch=(), flops=0, moved=0):
    smem = pl.BlockSpec(memory_space=pltpu.SMEM)
    vmem = pl.BlockSpec(memory_space=pltpu.VMEM)
    return pl.pallas_call(
        kernel,
        out_shape=tuple(jax.ShapeDtypeStruct(shape, dtype) for shape, dtype in outs),
        in_specs=[smem] * scalars + [vmem] * (len(args) - scalars),
        out_specs=(vmem,) * len(outs),
        scratch_shapes=scratch,
        compiler_params=pltpu.CompilerParams(vmem_limit_bytes=VMEM),
        cost_estimate=pl.CostEstimate(flops=flops, bytes_accessed=moved, transcendentals=0),
        name=name,
    )(*args)


def prepare_kernel(
    where_ref,
    qkv_ref,
    out_ref,
    up_ref,
    down_ref,
    qkv_m_ref,
    out_m_ref,
    up_m_ref,
    down_m_ref,
    rows_ref,
    *old_refs,
):
    zeros = jnp.zeros((16, D), F32)
    rows = jnp.concatenate(
        [up_ref[...], down_ref[...], qkv_ref[...], out_ref[...], zeros[: SENT - 36]], axis=0
    ).astype(BF)
    rows_ref[...] = jnp.broadcast_to(rows[None], rows_ref.shape)
    old = (
        up_m_ref[...],
        jnp.concatenate([zeros[:9], out_m_ref[...]], axis=0),
        down_m_ref[...],
        jnp.concatenate([qkv_m_ref[...], zeros[:3]], axis=0),
    )
    for z in range(4):

        @pl.when(where_ref[3] == z)
        def _(z=z):
            for step, ref in enumerate(old_refs):
                ref[...] = old[(z - step) % 4].astype(BF)


def join_kernel(where_ref, *refs):
    *sources, joined_ref = refs
    for z in range(4):

        @pl.when(where_ref[3] == z)
        def _(z=z):
            joined_ref[...] = jnp.concatenate(
                [sources[(at - z) % 4][...].astype(F32) for at in range(4)], axis=0
            ).astype(BF)


def valid_rows(is_out):
    row = lax.broadcasted_iota(jnp.int32, (GROUP, D), 0) % BLOCK
    return (jnp.logical_not(is_out) | (row >= 9)).astype(F32)


def tell_kernel(where_ref, own_ref, piece_ref, small_ref, told_ref):
    is_out = where_ref[3] == 1
    valid = valid_rows(is_out)
    total = jnp.zeros((GROUP, D), F32)
    for xy in range(16):
        g = own_ref[xy].astype(F32) * valid
        total = total + g * g
    small = dot(small_ref[...], own_ref[...].reshape(768, D))
    counted = jnp.where(is_out & (where_ref[0] == 0), 1.0, 0.0)
    squares = jnp.sum(total) + counted * jnp.sum(small * small)
    squares = jnp.full((1, D), squares, F32)
    high = squares.astype(BF).astype(F32)
    mid = (squares - high).astype(BF).astype(F32)
    low = squares - high - mid
    for z in range(4):
        rows = jnp.concatenate(
            [small, piece_ref[z * BLOCK : (z + 1) * BLOCK, :], high, mid, low, jnp.zeros((1, D), F32)],
            axis=0,
        ).astype(BF)
        told_ref[2 * z] = rows
        told_ref[2 * z + 1] = rows


def clip(told_ref):
    total = jnp.zeros((1, 1), F32)
    for k in range(8):
        last = told_ref[k, 64:, :].astype(F32)
        total = total + (last[12:13, :1] + last[13:14, :1] + last[14:15, :1])
    grad_norm = jnp.sqrt(total)
    return grad_norm, jnp.minimum(1.0, CLIP_LIMIT / (grad_norm + 1e-06))


def gram_kernel(where_ref, own_ref, oth_ref, old_own_ref, old_oth_ref, gram_ref, grad_ref, old_ref):
    valid = valid_rows(where_ref[3] == 1)
    for s, (g_ref, o_ref) in enumerate(((own_ref, old_own_ref), (oth_ref, old_oth_ref))):
        for xy in range(16):
            at = s * 768 + xy * GROUP
            grad_ref[at : at + GROUP] = (g_ref[xy].astype(F32) * valid).astype(BF)
        old_ref[s * 768 : (s + 1) * 768] = o_ref[...].reshape(768, D)
    grad = grad_ref[...]
    old = old_ref[...]
    cross = dot_tn(grad, old)
    gram_ref[0] = dot_tn(old, old)
    gram_ref[1] = cross + cross.T
    gram_ref[2] = dot_tn(grad, grad)


def left_parts(parts):
    return jnp.concatenate([parts[0], parts[0], parts[1]], axis=1)


def right_parts(parts):
    return jnp.concatenate([parts[0], parts[1], parts[0]], axis=0)


def orth_kernel(where_ref, told_ref, gram_ref, old_ref, piece_ref, out_ref):
    valid = valid_rows(where_ref[3] == 1)
    factor = clip(told_ref)[1]
    gram = (
        (MOMENTUM * MOMENTUM) * gram_ref[0]
        + (MOMENTUM * factor) * gram_ref[1]
        + (factor * factor) * gram_ref[2]
    )
    eye = (
        lax.broadcasted_iota(jnp.int32, (D, D), 0) == lax.broadcasted_iota(jnp.int32, (D, D), 1)
    ).astype(F32)
    inv = 1.0 / (jnp.sqrt(jnp.sum(gram * eye)) + 1e-07)
    gram = gram * (inv * inv)
    mine = (MOMENTUM * old_ref[...].astype(F32) + factor * (piece_ref[...] * valid)) * inv
    for step in range(NS_STEPS):
        parts = halves(gram)
        right = right_parts(parts)
        poly = halves(COEF_A * eye + COEF_B * gram + COEF_C * dot(left_parts(parts), right))
        if step < NS_STEPS - 1:
            turned = halves(dot(left_parts(poly), right))
            left = jnp.concatenate([left_parts(turned), left_parts(halves(mine))], axis=0)
            both = dot(left, right_parts(poly))
            gram, mine = both[:D], both[D:]
        else:
            mine = dot(left_parts(halves(mine)), right_parts(poly))
    for z in range(4):
        out_ref[z] = jnp.concatenate(
            [mine[z * BLOCK : (z + 1) * BLOCK], jnp.zeros((4, D), F32)], axis=0
        ).astype(BF)


def step_rate(rows_count, cols_count):
    return math.sqrt(max(rows_count, cols_count) / rows_count)


def update_kernel(
    where_ref,
    told_ref,
    back_ref,
    qkv_ref,
    out_ref,
    up_ref,
    down_ref,
    qkv_m_ref,
    out_m_ref,
    up_m_ref,
    down_m_ref,
    norms_ref,
    norm_m_ref,
    table_ref,
    pos_m_ref,
    grad_norm_ref,
    qkv_m_next,
    qkv_next,
    out_m_next,
    out_next,
    up_m_next,
    up_next,
    down_m_next,
    down_next,
    norm_m_next,
    norms_next,
    pos_m_next,
    table_next,
):
    grad_norm, factor = clip(told_ref)
    grad_norm_ref[...] = grad_norm
    for z, first, last, rate, w_ref, m_ref, w_next, m_next in (
        (3, 0, 9, step_rate(D, 3 * D), qkv_ref, qkv_m_ref, qkv_next, qkv_m_next),
        (1, 9, 12, step_rate(D, D), out_ref, out_m_ref, out_next, out_m_next),
        (0, 0, 12, step_rate(D, FF), up_ref, up_m_ref, up_next, up_m_next),
        (2, 0, 12, step_rate(FF, D), down_ref, down_m_ref, down_next, down_m_next),
    ):
        grad = told_ref[2 * z + where_ref[0], 64:, :].astype(F32)[first:last]
        orth = back_ref[z].astype(F32)[first:last]
        m_next[...] = MOMENTUM * m_ref[...] + factor * grad
        w_next[...] = w_ref[...] - rate * orth
    small = told_ref[2, :64, :].astype(F32)
    norm_fresh = MOMENTUM * norm_m_ref[...] + factor * small[50:54]
    norm_m_next[...] = norm_fresh
    norms_next[...] = norms_ref[...] - NORM_RATE * norm_fresh
    pos_fresh = MOMENTUM * pos_m_ref[...] + factor * small[:50]
    pos_m_next[...] = pos_fresh
    table_next[...] = table_ref[...] - SMALL_RATE * pos_fresh


def swapped(value):
    return lax.ppermute(value, "c", [(0, 1), (1, 0)])


def exchanged(value, axes):
    return lax.all_to_all(value, axes, 0, 0, tiled=True)


def everywhere(value, axes):
    peers = lax.axis_size(axes)
    return exchanged(jnp.broadcast_to(value[None], (peers, *value.shape)), axes)


def shards(
    tokens,
    cotangent,
    pos_table,
    norm_params,
    qkv_weight,
    out_weight,
    up_weight,
    down_weight,
    qkv_moment,
    out_moment,
    up_moment,
    down_moment,
    norm_moment,
    pos_moment,
    res_ids,
    offsets,
    pos_index,
):
    z = lax.axis_index(COLUMN)
    colour = (lax.axis_index("x") + 2 * lax.axis_index("y") - z) % 4
    where = jnp.stack(
        [lax.axis_index("c"), lax.axis_index("zh"), lax.axis_index(PLANE), z, colour]
    ).astype(jnp.int32)
    weights = (qkv_weight.T, out_weight, up_weight.T, down_weight)
    moments = (qkv_moment.T, out_moment, up_moment.T, down_moment)

    rows, *old = call(
        prepare_kernel,
        "prepare",
        (((16, SENT, D), BF), *(((BLOCK, D), BF) for _ in range(4))),
        (where, *weights, *moments),
        scalars=1,
        moved=4_000_000,
    )
    old = [old[0]] + [lax.ppermute(old[k], AXES, column_step(k)) for k in (1, 2, 3)]
    (old,) = call(join_kernel, "join", (((GROUP, D), BF),), (where, *old), scalars=1)

    own = [lax.all_to_all(rows, AXES, 0, 0, axis_index_groups=colour_groups(), tiled=True)]
    own[0], old = lax.optimization_barrier((own[0], old))
    own += [lax.ppermute(own[0], AXES, colour_step(step)) for step in (1, 2, 3)]
    other = [swapped(value) for value in own]
    old_own = everywhere(old, PLANE)

    result, in_grad, keep, send = run_layer(
        where,
        res_ids,
        offsets,
        tokens,
        cotangent,
        pos_table,
        norm_params,
        pos_index.reshape(1, -1),
        (*own, *other),
    )
    keep, send, old_own = lax.optimization_barrier((keep, send, old_own))
    old_other = swapped(old_own)
    pair = (keep.astype(F32) + swapped(send).astype(F32)).astype(BF)
    piece = jnp.sum(exchanged(pair, HALF).astype(F32), axis=0)
    grads = everywhere(piece.astype(BF), PLANE)
    grads_other = swapped(grads)

    (told,) = call(
        tell_kernel,
        "tell",
        (((8, 80, D), BF),),
        (where, grads, piece, jnp.asarray(small_places().T, BF)),
        scalars=1,
        moved=2_000_000,
    )
    told = exchanged(told, COLUMN_CORES)
    (gram,) = call(
        gram_kernel,
        "gram",
        (((3, D, D), F32),),
        (where, grads, grads_other, old_own, old_other),
        scalars=1,
        scratch=[pltpu.VMEM((1536, D), BF), pltpu.VMEM((1536, D), BF)],
        flops=3_000_000_000,
        moved=5_000_000,
    )
    (orth,) = call(
        orth_kernel,
        "orth",
        (((4, 16, D), BF),),
        (where, told, gram, old, piece),
        scalars=1,
        flops=8_000_000_000,
        moved=4_000_000,
    )
    back = exchanged(orth, COLUMN)
    like = lambda a: (a.shape, F32)
    grad_norm, *news = call(
        update_kernel,
        "update",
        (
            ((1, 1), F32),
            *(like(a) for pair_of in zip(moments, weights) for a in pair_of),
            like(norm_moment),
            like(norm_params),
            like(pos_moment),
            like(pos_table),
        ),
        (where, told, back, *weights, *moments, norm_params, norm_moment, pos_table, pos_moment),
        scalars=1,
        moved=2_000_000,
    )
    for k in (0, 1, 4, 5):
        news[k] = news[k].T
    return (result, in_grad, grad_norm.reshape(()), *news)


def solution(mesh):
    finer = Mesh(
        mesh.devices.reshape(2, 4, 4, 2, mesh.shape["tensor"]), ("zl", "x", "y", "c", "zh")
    )
    columns = P(None, ROWS)
    rows = P(ROWS, None)
    return jax.shard_map(
        shards,
        mesh=finer,
        in_specs=(
            P(DP, None),
            P(DP, None),
            P(),
            P(),
            columns,
            rows,
            columns,
            rows,
            columns,
            rows,
            columns,
            rows,
            P(),
            P(),
            P(DP),
            P(DP),
            P(DP),
        ),
        out_specs=(
            P(DP, None),
            P(DP, None),
            P(),
            columns,
            columns,
            rows,
            rows,
            columns,
            columns,
            rows,
            rows,
            P(),
            P(),
            P(),
            P(),
        ),
        check_vma=False,
    )
```

```python
import math

import jax
import jax.numpy as jnp
import numpy as np
from jax import lax
from jax.experimental import pallas as pl
from jax.experimental.pallas import tpu as pltpu
from jax.sharding import Mesh
from jax.sharding import PartitionSpec as P

D = 384
HEADS = 6
HD = 64
FF = 1536
SMALL_LEN = 50
BIG_LEN = 145
NS_STEPS = 5
COEF_A = 3.4445
COEF_B = -4.775
COEF_C = 2.0315
NORM_EPS = 1e-06
CLIP_LIMIT = 1.0
MOMENTUM = 0.5
SMALL_RATE = 10.0
NORM_RATE = 40.0

DP = ("zl", "x", "y", "c")
ROWS = ("zh",) + DP
COLUMN = ("zh", "zl")
PLANE = ("x", "y")
HALF = ("zl", "x", "y")
COLUMN_CORES = ("zh", "zl", "c")
AXES = ("zl", "x", "y", "c", "zh")

BF = jnp.bfloat16
F32 = jnp.float32
BLOCK = 12
GROUP = 48
SENT = 40
VMEM = 24 << 20
ALL_VMEM = 60 << 20
LAYER_VMEM = 60 << 20


def qkv_pieces(block):
    pieces = []
    row = block * 9
    while row < block * 9 + 9:
        head, rest = divmod(row, 3 * HD)
        part, e = divmod(rest, HD)
        count = min(HD - e, block * 9 + 9 - row)
        pieces.append((row - block * 9, count, part * HEADS * HD + head * HD + e))
        row += count
    return pieces


def blocks_of_rows():
    return [
        (core, xy * GROUP + z * BLOCK, (z * 16 + xy) * 2 + core)
        for core in range(2)
        for xy in range(16)
        for z in range(4)
    ]


def small_places():
    places = np.zeros((2, 64, 768), np.float32)
    for n in range(64):
        at = (n // 4) * GROUP + (n % 4) * BLOCK
        places[0, n, at] = 1
        places[1, n, at + 9] = 1
    return places


def dot(a, b):
    return lax.dot_general(a, b, (((1,), (0,)), ((), ())), preferred_element_type=F32)


def dot_nt(a, b):
    return lax.dot_general(a, b, (((1,), (1,)), ((), ())), preferred_element_type=F32)


def dot_tn(a, b):
    return lax.dot_general(a, b, (((0,), (0,)), ((), ())), preferred_element_type=F32)


def halves(a):
    high = a.astype(BF)
    return high, (a - high.astype(F32)).astype(BF)


def norm_parts(v):
    cen = v - jnp.mean(v, axis=-1, keepdims=True)
    var = jnp.mean(cen * cen, axis=-1, keepdims=True)
    r = lax.rsqrt(var + NORM_EPS)
    return cen * r, r


def norm_back(dy, n, r, gain):
    e = dy * gain
    return r * (
        e - jnp.mean(e, axis=-1, keepdims=True) - n * jnp.mean(e * n, axis=-1, keepdims=True)
    )


def device(x, y, z, core):
    x, y, z = x % 4, y % 4, z % 4
    return ((((z % 2) * 4 + x) * 4 + y) * 2 + core) * 2 + z // 2


def devices():
    return [(x, y, z, c) for x in range(4) for y in range(4) for z in range(4) for c in range(2)]


def column_step(step):
    return [(device(x, y, z + step, c), device(x, y, z, c)) for x, y, z, c in devices()]


def colour_groups():
    return [
        [device(x, y, x + 2 * y - colour, core) for x in range(4) for y in range(4)]
        for colour in range(4)
        for core in range(2)
    ]


def colour_step(step):
    sources = {
        1: ((1, 0, 0), (0, 0, -1)),
        2: ((0, 1, 0), (0, -1, 0)),
        3: ((-1, 0, 0), (0, 0, 1)),
    }[step]
    return [
        (device(x + sources[c][0], y + sources[c][1], z + sources[c][2], c), device(x, y, z, c))
        for x, y, z, c in devices()
    ]


def embed_kernel(tok_ref, cot_ref, table_ref, pos_ref, stream_ref, cot_out_ref, padded_ref):
    count = tok_ref.shape[0]
    padded_ref[...] = jnp.zeros(padded_ref.shape, F32)
    padded_ref[: table_ref.shape[0]] = table_ref[...]
    t0, t_rest = halves(padded_ref[...])
    t1, t2 = halves(padded_ref[...] - t0.astype(F32))
    hits = hits_of(pos_ref, count)
    stream_ref[...] = tok_ref[...].astype(F32) + (
        (dot_tn(hits, t2) + dot_tn(hits, t1)) + dot_tn(hits, t0)
    )
    cot_out_ref[...] = cot_ref[...]


def hits_of(pos_ref, count):
    return (
        lax.broadcasted_iota(jnp.int32, (64, count), 0) == jnp.broadcast_to(pos_ref[...], (64, count))
    ).astype(BF)


def layer_kernel(
    where_ref,
    res_ref,
    off_ref,
    norms_ref,
    pos_ref,
    stream_hbm,
    cot_hbm,
    own0,
    own1,
    own2,
    own3,
    oth0,
    oth1,
    oth2,
    oth3,
    result_hbm,
    in_grad_hbm,
    keep_hbm,
    send_hbm,
    wup,
    wdn,
    wqkv,
    wout,
    mixed,
    sorted_qkv,
    sorted_out,
    message,
    probs_ref,
    qkv_ref,
    ctx_ref,
    dqkv_ref,
    small_ref,
    weights_ref,
    stream_ref,
    cot_ref,
    result_ref,
    in_grad_ref,
    kept,
    sent,
    in_sems,
    out_sems,
):
    core = where_ref[0]
    half = where_ref[1]
    colour = where_ref[4]
    count = cot_ref.shape[0]
    loads = [
        pltpu.make_async_copy(source, weights_ref.at[k], in_sems.at[k])
        for k, source in enumerate((own0, own1, own2, own3, oth0, oth1, oth2, oth3))
    ]
    loads.append(pltpu.make_async_copy(stream_hbm, stream_ref, in_sems.at[8]))
    loads.append(pltpu.make_async_copy(cot_hbm, cot_ref, in_sems.at[9]))
    for load in loads:
        load.start()

    for s in range(2):
        for load in loads[4 * s : 4 * s + 4]:
            load.wait()
        for here in range(4):

            @pl.when(colour == here)
            def _(s=s, here=here):
                for xy in range(16):
                    ahead = xy // 4 + 2 * (xy % 4) - here
                    blocks = [weights_ref[4 * s + (ahead - z) % 4, xy].astype(F32) for z in range(4)]
                    at = s * 768 + xy * GROUP
                    groups = [
                        jnp.concatenate([block[k : k + BLOCK] for block in blocks], axis=0)
                        for k in (0, 12, 24)
                    ]
                    wup[at : at + GROUP] = groups[0].astype(BF)
                    wdn[at : at + GROUP] = groups[1].astype(BF)
                    mixed[core if s == 0 else 1 - core, xy * GROUP : (xy + 1) * GROUP] = groups[2]

    for load in loads[8:]:
        load.wait()

    for at_core, at, block in blocks_of_rows():
        for first, length, to in qkv_pieces(block):
            sorted_qkv[to : to + length] = mixed[at_core, at + first : at + first + length]
        sorted_out[block * 3 : block * 3 + 3] = mixed[at_core, at + 9 : at + 12]
    wqkv[...] = sorted_qkv[...].astype(BF)
    wout[...] = sorted_out[...].astype(BF)


    stream_in = stream_ref[...]
    g1, s1, g2, s2 = (norms_ref[k : k + 1, :] for k in range(4))
    n1, r1 = norm_parts(stream_in)
    y1 = (n1 * g1 + s1).astype(BF)
    qkv_ref[...] = dot_nt(y1, wqkv[...]).astype(BF)

    def segments(shape, dim):
        at = lax.broadcasted_iota(jnp.int32, shape, dim)
        seg = at + 8
        for k in range(5):
            res = res_ref[k]
            off = off_ref[k]
            length = jnp.where(res == 0, SMALL_LEN, jnp.where(res == 1, BIG_LEN, 0))
            seg = jnp.where((at >= off) & (at < off + length), k, seg)
        return seg

    allowed = segments((count, count), 0) == segments((count, count), 1)
    lane = lax.broadcasted_iota(jnp.int32, (1, 128), 1)
    masks = ((lane < HD).astype(F32).astype(BF), (lane >= HD).astype(F32).astype(BF))
    scale = HD**-0.5
    for p in range(HEADS // 2):
        lo = p * 128
        q = qkv_ref[:, lo : lo + 128]
        k = qkv_ref[:, 384 + lo : 512 + lo]
        v = qkv_ref[:, 768 + lo : 896 + lo]
        ctx = 0.0
        for hh in range(2):
            scores = dot_nt(q * masks[hh], k) * scale
            scores = jnp.where(allowed, scores, -1e30)
            expo = jnp.exp(scores - jnp.max(scores, axis=-1, keepdims=True))
            probs = expo / jnp.sum(expo, axis=-1, keepdims=True)
            probs_ref[2 * p + hh] = probs
            ctx = ctx + dot(probs.astype(BF), v * masks[hh])
        ctx_ref[:, lo : lo + 128] = ctx.astype(BF)
    stream_mid = stream_in + dot(ctx_ref[...], wout[...])
    n2, r2 = norm_parts(stream_mid)
    y2 = (n2 * g2 + s2).astype(BF)

    cot = cot_ref[...]
    right = jnp.where(half == 0, y2, cot)
    out = stream_mid
    d_y2 = 0.0
    for k in range(4):
        wu = wup[k * 384 : (k + 1) * 384, :]
        wd = wdn[k * 384 : (k + 1) * 384, :]
        pre = dot_nt(y2, wu)
        cdf = 0.5 * (1.0 + lax.erf(pre * (2.0**-0.5)))
        hidden = (pre * cdf).astype(BF)
        slope = cdf + pre * (jnp.exp(-0.5 * pre * pre) * ((2.0 * math.pi) ** -0.5))
        d_pre = (slope * dot_nt(cot, wd)).astype(BF)
        out = out + dot(hidden, wd)
        d_y2 = d_y2 + dot(d_pre, wu)
        grad = dot_tn(jnp.where(half == 0, d_pre, hidden), right).reshape(8, GROUP, 384)
        at = (k % 2) * 8
        if k < 2:
            kept[at : at + 8] = grad.astype(BF)
        else:
            sent[at : at + 8] = grad.astype(BF)
    result_ref[...] = out.astype(BF)
    stores = [
        pltpu.make_async_copy(
            source.at[pl.ds(16 * k, 16)], target.at[pl.ds(16 * k, 16)], out_sems.at[2 * k + j]
        )
        for k in range(2)
        for j, (source, target) in enumerate(((sent, send_hbm), (kept, keep_hbm)))
    ]
    stores.append(pltpu.make_async_copy(result_ref, result_hbm, out_sems.at[4]))
    stores.append(pltpu.make_async_copy(in_grad_ref, in_grad_hbm, out_sems.at[5]))
    for k in (0, 1, 4):
        stores[k].start()
    gain2 = jnp.sum(d_y2 * n2, axis=0, keepdims=True)
    shift2 = jnp.sum(d_y2, axis=0, keepdims=True)
    d_mid = cot.astype(F32) + norm_back(d_y2, n2, r2, g2)

    d_attn = d_mid.astype(BF)
    d_ctx = dot_nt(d_attn, wout[...]).astype(BF)
    for p in range(HEADS // 2):
        lo = p * 128
        q = qkv_ref[:, lo : lo + 128]
        k = qkv_ref[:, 384 + lo : 512 + lo]
        v = qkv_ref[:, 768 + lo : 896 + lo]
        dc = d_ctx[:, lo : lo + 128]
        dq, dk, dv = 0.0, 0.0, 0.0
        for hh in range(2):
            probs = probs_ref[2 * p + hh]
            dcm = dc * masks[hh]
            d_probs = dot_nt(dcm, v)
            inner = jnp.sum(probs * d_probs, axis=-1, keepdims=True)
            d_scores = (probs * (d_probs - inner)).astype(BF)
            dq = dq + dot(d_scores, k * masks[hh])
            dk = dk + dot_tn(d_scores, q * masks[hh])
            dv = dv + dot_tn(probs.astype(BF), dcm)
        dqkv_ref[:, lo : lo + 128] = (dq * scale).astype(BF)
        dqkv_ref[:, 384 + lo : 512 + lo] = (dk * scale).astype(BF)
        dqkv_ref[:, 768 + lo : 896 + lo] = dv.astype(BF)
    d_y1 = dot(dqkv_ref[...], wqkv[...])
    in_grad = d_mid + norm_back(d_y1, n1, r1, g1)
    in_grad_ref[...] = in_grad
    stores[5].start()

    hits = hits_of(pos_ref, count)
    i0, i1 = halves(in_grad)
    pos_grad = dot(hits, i0) + dot(hits, i1)
    gain1 = jnp.sum(d_y1 * n1, axis=0, keepdims=True)
    shift1 = jnp.sum(d_y1, axis=0, keepdims=True)
    row = lax.broadcasted_iota(jnp.int32, (64, 384), 0)
    for at, value in ((50, gain1), (51, shift1), (52, gain2), (53, shift2)):
        pos_grad = jnp.where(row == at, jnp.broadcast_to(value, (64, 384)), pos_grad)
    sorted_out[...] = dot_tn(ctx_ref[...], d_attn)
    sorted_qkv[...] = dot_tn(dqkv_ref[...], y1)
    small_ref[...] = pos_grad

    @pl.when(half == 0)
    def _():
        zeros = jnp.zeros((8, D), F32)
        for at_core in range(2):
            for xy in range(16):
                rows = []
                for z in range(4):
                    block = (z * 16 + xy) * 2 + at_core
                    rows += [
                        small_ref[xy * 4 + z : xy * 4 + z + 1],
                        zeros,
                        sorted_out[block * 3 : block * 3 + 3],
                    ]
                message[at_core, xy] = jnp.concatenate(rows, axis=0).astype(BF)

    @pl.when(half == 1)
    def _():
        zeros = jnp.zeros((2, D), F32)
        for at_core in range(2):
            for xy in range(16):
                rows = []
                for z in range(4):
                    rows += [
                        sorted_qkv[to : to + length]
                        for _, length, to in qkv_pieces((z * 16 + xy) * 2 + at_core)
                    ]
                    rows += [small_ref[xy * 4 + z : xy * 4 + z + 1], zeros]
                message[at_core, xy] = jnp.concatenate(rows, axis=0).astype(BF)

    sent[16:] = message[1 - core]
    stores[2].start()
    kept[16:] = message[core]
    stores[3].start()
    for store in stores:
        store.wait()


def run_layer(where, res_ids, offsets, stream, cotangent, norms, pos, weights):
    count = stream.shape[0]
    smem = pl.BlockSpec(memory_space=pltpu.SMEM)
    vmem = pl.BlockSpec(memory_space=pltpu.VMEM)
    hbm = pl.BlockSpec(memory_space=pl.ANY)
    return pl.pallas_call(
        layer_kernel,
        out_shape=(
            jax.ShapeDtypeStruct((count, D), BF),
            jax.ShapeDtypeStruct((count, D), F32),
            jax.ShapeDtypeStruct((32, GROUP, D), BF),
            jax.ShapeDtypeStruct((32, GROUP, D), BF),
        ),
        in_specs=[smem] * 3 + [vmem] * 2 + [hbm] * 10,
        out_specs=(hbm,) * 4,
        scratch_shapes=[
            pltpu.VMEM((1536, D), BF),
            pltpu.VMEM((1536, D), BF),
            pltpu.VMEM((1152, D), BF),
            pltpu.VMEM((D, D), BF),
            pltpu.VMEM((2, 768, D), F32),
            pltpu.VMEM((1152, D), F32),
            pltpu.VMEM((D, D), F32),
            pltpu.VMEM((2, 16, GROUP, D), BF),
            pltpu.VMEM((HEADS, count, count), F32),
            pltpu.VMEM((count, 1152), BF),
            pltpu.VMEM((count, D), BF),
            pltpu.VMEM((count, 1152), BF),
            pltpu.VMEM((64, D), F32),
            pltpu.VMEM((8, 16, SENT, D), BF),
            pltpu.VMEM((count, D), F32),
            pltpu.VMEM((count, D), BF),
            pltpu.VMEM((count, D), BF),
            pltpu.VMEM((count, D), F32),
            pltpu.VMEM((32, GROUP, D), BF),
            pltpu.VMEM((32, GROUP, D), BF),
            pltpu.SemaphoreType.DMA((10,)),
            pltpu.SemaphoreType.DMA((6,)),
        ],
        compiler_params=pltpu.CompilerParams(vmem_limit_bytes=LAYER_VMEM),
        cost_estimate=pl.CostEstimate(
            flops=0, bytes_accessed=0, transcendentals=0
        ),
        name="layer",
    )(
        where, res_ids, offsets, norms, pos, stream, cotangent, *weights
    )


def product(a, b):
    (ah, al), (bh, bl) = a, b
    first = jnp.concatenate([ah, al], axis=1)
    return dot(first, jnp.concatenate([bh, bh], axis=0)) + dot(ah, bl)


def call(kernel, name, outs, args, scalars=0, scratch=(), flops=0, moved=0, vmem_bytes=VMEM):
    smem = pl.BlockSpec(memory_space=pltpu.SMEM)
    vmem = pl.BlockSpec(memory_space=pltpu.VMEM)
    return pl.pallas_call(
        kernel,
        out_shape=tuple(jax.ShapeDtypeStruct(shape, dtype) for shape, dtype in outs),
        in_specs=[smem] * scalars + [vmem] * (len(args) - scalars),
        out_specs=(vmem,) * len(outs),
        scratch_shapes=scratch,
        compiler_params=pltpu.CompilerParams(vmem_limit_bytes=vmem_bytes),
        cost_estimate=pl.CostEstimate(flops=flops, bytes_accessed=moved, transcendentals=0),
        name=name,
    )(*args)


def prepare_kernel(
    where_ref,
    qkv_ref,
    out_ref,
    up_ref,
    down_ref,
    qkv_m_ref,
    out_m_ref,
    up_m_ref,
    down_m_ref,
    rows_ref,
    *old_refs,
):
    zeros = jnp.zeros((16, D), F32)
    rows = jnp.concatenate(
        [up_ref[...], down_ref[...], qkv_ref[...], out_ref[...], zeros[: SENT - 36]], axis=0
    ).astype(BF)
    rows_ref[...] = jnp.broadcast_to(rows[None], rows_ref.shape)
    old = (
        up_m_ref[...],
        jnp.concatenate([zeros[:9], out_m_ref[...]], axis=0),
        down_m_ref[...],
        jnp.concatenate([qkv_m_ref[...], zeros[:3]], axis=0),
    )
    for z in range(4):

        @pl.when(where_ref[3] == z)
        def _(z=z):
            for step, ref in enumerate(old_refs):
                ref[...] = old[(z - step) % 4].astype(BF)


def join_kernel(where_ref, *refs):
    *sources, joined_ref, sent_ref = refs
    for z in range(4):

        @pl.when(where_ref[3] == z)
        def _(z=z):
            joined = jnp.concatenate(
                [sources[(at - z) % 4][...].astype(F32) for at in range(4)], axis=0
            ).astype(BF)
            joined_ref[...] = joined
            sent_ref[...] = jnp.broadcast_to(joined[None], sent_ref.shape)


def sum_kernel(parts_ref, piece_ref, sent_ref):
    total = parts_ref[0].astype(F32)
    for k in range(1, parts_ref.shape[0]):
        total = total + parts_ref[k].astype(F32)
    piece_ref[...] = total
    sent_ref[...] = jnp.broadcast_to(total.astype(BF)[None], sent_ref.shape)


def valid_rows(z):
    row = lax.broadcasted_iota(jnp.int32, (GROUP, D), 0) % BLOCK
    return jnp.where(z == 1, (row >= 9).astype(F32), jnp.where(z == 3, (row < 9).astype(F32), 1.0))


def tell_kernel(where_ref, own_ref, piece_ref, places_ref, told_ref, small_ref):
    z = where_ref[3]
    valid = valid_rows(z)
    total = jnp.zeros((GROUP, D), F32)
    for xy in range(16):
        g = own_ref[xy].astype(F32) * valid
        total = total + g * g
    small = dot(places_ref[where_ref[1]], own_ref[...].reshape(768, D))
    small_ref[...] = small.astype(BF)
    counted = jnp.where((z == 1) & (where_ref[0] == 0), 1.0, 0.0)
    squares = jnp.sum(total) + counted * jnp.sum(small * small)
    squares = jnp.full((1, D), squares, F32)
    high = squares.astype(BF).astype(F32)
    mid = (squares - high).astype(BF).astype(F32)
    low = squares - high - mid
    for to in range(4):
        rows = jnp.concatenate(
            [piece_ref[to * BLOCK : (to + 1) * BLOCK, :], high, mid, low, jnp.zeros((1, D), F32)],
            axis=0,
        ).astype(BF)
        told_ref[2 * to] = rows
        told_ref[2 * to + 1] = rows


def clip(told_ref):
    total = jnp.zeros((1, 1), F32)
    for k in range(8):
        last = told_ref[k].astype(F32)
        total = total + (last[12:13, :1] + last[13:14, :1] + last[14:15, :1])
    grad_norm = jnp.sqrt(total)
    return grad_norm, jnp.minimum(1.0, CLIP_LIMIT / (grad_norm + 1e-06))


def orth_kernel(
    where_ref,
    told_ref,
    own_ref,
    oth_ref,
    old_own_ref,
    old_oth_ref,
    old_ref,
    piece_ref,
    out_ref,
    whole_ref,
):
    valid = valid_rows(where_ref[3])
    factor = clip(told_ref)[1]
    scaled = factor * valid
    for s, (grad_ref, before_ref) in enumerate(((own_ref, old_own_ref), (oth_ref, old_oth_ref))):
        for xy in range(16):
            at = s * 768 + xy * GROUP
            whole_ref[at : at + GROUP] = (
                MOMENTUM * before_ref[xy].astype(F32) + scaled * grad_ref[xy].astype(F32)
            ).astype(BF)
    whole = whole_ref[...]
    gram = dot_tn(whole, whole)
    eye = (
        lax.broadcasted_iota(jnp.int32, (D, D), 0) == lax.broadcasted_iota(jnp.int32, (D, D), 1)
    ).astype(F32)
    inv = 1.0 / (jnp.sqrt(jnp.sum(gram * eye)) + 1e-07)
    gram = gram * (inv * inv)
    mine = (MOMENTUM * old_ref[...].astype(F32) + scaled * piece_ref[...]) * inv
    for step in range(NS_STEPS):
        parts = halves(gram)
        if step in (0, 1, NS_STEPS - 1):
            square = dot(parts[0], parts[0])
        else:
            square = product(parts, parts)
        poly = COEF_A * eye + COEF_B * gram + COEF_C * square
        if step == NS_STEPS - 1:
            mine = dot(mine.astype(BF), poly.astype(BF))
        else:
            poly = halves(poly)
            gram = product(halves(product(poly, parts)), poly)
            mine = product(halves(mine), poly)
    for z in range(4):
        out_ref[z] = jnp.concatenate(
            [mine[z * BLOCK : (z + 1) * BLOCK], jnp.zeros((4, D), F32)], axis=0
        ).astype(BF)


def step_rate(rows_count, cols_count):
    return math.sqrt(max(rows_count, cols_count) / rows_count)


def update_kernel(
    where_ref,
    told_ref,
    small_own_ref,
    small_near_ref,
    back_ref,
    qkv_ref,
    out_ref,
    up_ref,
    down_ref,
    qkv_m_ref,
    out_m_ref,
    up_m_ref,
    down_m_ref,
    norms_ref,
    norm_m_ref,
    table_ref,
    pos_m_ref,
    grad_norm_ref,
    qkv_m_next,
    qkv_next,
    out_m_next,
    out_next,
    up_m_next,
    up_next,
    down_m_next,
    down_next,
    norm_m_next,
    norms_next,
    pos_m_next,
    table_next,
):
    grad_norm, factor = clip(told_ref)
    grad_norm_ref[...] = grad_norm
    for z, first, last, rate, w_ref, m_ref, w_next, m_next in (
        (3, 0, 9, step_rate(D, 3 * D), qkv_ref, qkv_m_ref, qkv_next, qkv_m_next),
        (1, 9, 12, step_rate(D, D), out_ref, out_m_ref, out_next, out_m_next),
        (0, 0, 12, step_rate(D, FF), up_ref, up_m_ref, up_next, up_m_next),
        (2, 0, 12, step_rate(FF, D), down_ref, down_m_ref, down_next, down_m_next),
    ):
        grad = told_ref[2 * z + where_ref[0]].astype(F32)[first:last]
        orth = back_ref[z].astype(F32)[first:last]
        m_next[...] = MOMENTUM * m_ref[...] + factor * grad
        w_next[...] = w_ref[...] - rate * orth
    near = (where_ref[3] % 2 == 0).astype(F32)
    small = near * small_near_ref[...].astype(F32) + (1.0 - near) * small_own_ref[...].astype(F32)
    norm_fresh = MOMENTUM * norm_m_ref[...] + factor * small[50:54]
    norm_m_next[...] = norm_fresh
    norms_next[...] = norms_ref[...] - NORM_RATE * norm_fresh
    pos_fresh = MOMENTUM * pos_m_ref[...] + factor * small[:50]
    pos_m_next[...] = pos_fresh
    table_next[...] = table_ref[...] - SMALL_RATE * pos_fresh


def swapped(value):
    return lax.ppermute(value, "c", [(0, 1), (1, 0)])


def exchanged(value, axes):
    return lax.all_to_all(value, axes, 0, 0, tiled=True)


def everywhere(value, axes):
    peers = lax.axis_size(axes)
    return exchanged(jnp.broadcast_to(value[None], (peers, *value.shape)), axes)


def shards(
    tokens,
    cotangent,
    pos_table,
    norm_params,
    qkv_weight,
    out_weight,
    up_weight,
    down_weight,
    qkv_moment,
    out_moment,
    up_moment,
    down_moment,
    norm_moment,
    pos_moment,
    res_ids,
    offsets,
    pos_index,
):
    z = lax.axis_index(COLUMN)
    colour = (lax.axis_index("x") + 2 * lax.axis_index("y") - z) % 4
    where = jnp.stack(
        [lax.axis_index("c"), lax.axis_index("zh"), lax.axis_index(PLANE), z, colour]
    ).astype(jnp.int32)
    weights = (qkv_weight.T, out_weight, up_weight.T, down_weight)
    moments = (qkv_moment.T, out_moment, up_moment.T, down_moment)

    rows, *old = call(
        prepare_kernel,
        "prepare",
        (((16, SENT, D), BF), *(((BLOCK, D), BF) for _ in range(4))),
        (where, *weights, *moments),
        scalars=1,
        moved=4_000_000,
        vmem_bytes=ALL_VMEM,
    )
    old = [old[0]] + [lax.ppermute(old[k], AXES, column_step(k)) for k in (1, 2, 3)]
    pos = pos_index.reshape(1, -1)
    stream, cotangent = call(
        embed_kernel,
        "embed",
        ((tokens.shape, F32), (tokens.shape, BF)),
        (tokens, cotangent, pos_table, pos),
        scratch=[pltpu.VMEM((64, D), F32)],
        vmem_bytes=ALL_VMEM,
    )

    own = [lax.all_to_all(rows, AXES, 0, 0, axis_index_groups=colour_groups(), tiled=True)]
    own[0], stream, cotangent, *old = lax.optimization_barrier(
        (own[0], stream, cotangent, *old)
    )
    old, old_sent = call(
        join_kernel,
        "join",
        (((GROUP, D), BF), ((16, GROUP, D), BF)),
        (where, *old),
        scalars=1,
    )
    own += [lax.ppermute(own[0], AXES, colour_step(step)) for step in (1, 2, 3)]
    other = [swapped(value) for value in own]
    old_own = exchanged(old_sent, PLANE)

    result, in_grad, keep, send = run_layer(
        where,
        res_ids,
        offsets,
        stream,
        cotangent,
        norm_params,
        pos,
        (*own, *other),
    )
    keep, send, old_own = lax.optimization_barrier((keep, send, old_own))
    old_other = swapped(old_own)
    pair = (keep.astype(F32) + swapped(send).astype(F32)).astype(BF)
    piece, sent = call(
        sum_kernel, "sum", (((GROUP, D), F32), ((16, GROUP, D), BF)), (exchanged(pair, HALF),)
    )
    grads = exchanged(sent, PLANE)
    grads_other = swapped(grads)

    told, small = call(
        tell_kernel,
        "tell",
        (((8, 16, D), BF), ((64, D), BF)),
        (where, grads, piece, jnp.asarray(small_places(), BF)),
        scalars=1,
        moved=2_000_000,
    )
    told = exchanged(told, COLUMN_CORES)
    small_near = lax.ppermute(small, "zl", [(1, 0)])
    (orth,) = call(
        orth_kernel,
        "orth",
        (((4, 16, D), BF),),
        (where, told, grads, grads_other, old_own, old_other, old, piece),
        scalars=1,
        scratch=[pltpu.VMEM((1536, D), BF)],
        flops=8_000_000_000,
        moved=4_000_000,
    )
    back = exchanged(orth, COLUMN)
    like = lambda a: (a.shape, F32)
    grad_norm, *news = call(
        update_kernel,
        "update",
        (
            ((1, 1), F32),
            *(like(a) for pair_of in zip(moments, weights) for a in pair_of),
            like(norm_moment),
            like(norm_params),
            like(pos_moment),
            like(pos_table),
        ),
        (where, told, small, small_near, back, *weights, *moments, norm_params, norm_moment, pos_table, pos_moment),
        scalars=1,
        moved=2_000_000,
    )
    for k in (0, 1, 4, 5):
        news[k] = news[k].T
    return (result, in_grad, grad_norm.reshape(()), *news)


def solution(mesh):
    finer = Mesh(
        mesh.devices.reshape(2, 4, 4, 2, mesh.shape["tensor"]), ("zl", "x", "y", "c", "zh")
    )
    columns = P(None, ROWS)
    rows = P(ROWS, None)
    return jax.shard_map(
        shards,
        mesh=finer,
        in_specs=(
            P(DP, None),
            P(DP, None),
            P(),
            P(),
            columns,
            rows,
            columns,
            rows,
            columns,
            rows,
            columns,
            rows,
            P(),
            P(),
            P(DP),
            P(DP),
            P(DP),
        ),
        out_specs=(
            P(DP, None),
            P(DP, None),
            P(),
            columns,
            columns,
            rows,
            rows,
            columns,
            columns,
            rows,
            rows,
            P(),
            P(),
            P(),
            P(),
        ),
        check_vma=False,
    )
```

```python
import math

import jax
import jax.numpy as jnp
import numpy as np
from jax import lax
from jax.experimental import pallas as pl
from jax.experimental.pallas import tpu as pltpu
from jax.sharding import Mesh
from jax.sharding import PartitionSpec as P

D = 384
HEADS = 6
HD = 64
FF = 1536
SMALL_LEN = 50
BIG_LEN = 145
NS_STEPS = 5
COEF_A = 3.4445
COEF_B = -4.775
COEF_C = 2.0315
NORM_EPS = 1e-06
CLIP_LIMIT = 1.0
MOMENTUM = 0.5
SMALL_RATE = 10.0
NORM_RATE = 40.0

DP = ("zl", "x", "y", "c")
ROWS = ("zh",) + DP
COLUMN = ("zh", "zl")
PLANE = ("x", "y")
HALF = ("zl", "x", "y")
COLUMN_CORES = ("zh", "zl", "c")
AXES = ("zl", "x", "y", "c", "zh")

BF = jnp.bfloat16
F32 = jnp.float32
BLOCK = 12
GROUP = 48
SENT = 40
VMEM = 24 << 20
ALL_VMEM = 60 << 20
LAYER_VMEM = 60 << 20


def qkv_pieces(block):
    pieces = []
    row = block * 9
    while row < block * 9 + 9:
        head, rest = divmod(row, 3 * HD)
        part, e = divmod(rest, HD)
        count = min(HD - e, block * 9 + 9 - row)
        pieces.append((row - block * 9, count, part * HEADS * HD + head * HD + e))
        row += count
    return pieces


def blocks_of_rows():
    return [
        (core, xy * GROUP + z * BLOCK, (z * 16 + xy) * 2 + core)
        for core in range(2)
        for xy in range(16)
        for z in range(4)
    ]


def small_places():
    places = np.zeros((2, 64, 768), np.float32)
    for n in range(64):
        at = (n // 4) * GROUP + (n % 4) * BLOCK
        places[0, n, at] = 1
        places[1, n, at + 9] = 1
    return places


def dot(a, b):
    return lax.dot_general(a, b, (((1,), (0,)), ((), ())), preferred_element_type=F32)


def dot_nt(a, b):
    return lax.dot_general(a, b, (((1,), (1,)), ((), ())), preferred_element_type=F32)


def dot_tn(a, b):
    return lax.dot_general(a, b, (((0,), (0,)), ((), ())), preferred_element_type=F32)


def halves(a):
    high = a.astype(BF)
    return high, (a - high.astype(F32)).astype(BF)


def norm_parts(v):
    cen = v - jnp.mean(v, axis=-1, keepdims=True)
    var = jnp.mean(cen * cen, axis=-1, keepdims=True)
    r = lax.rsqrt(var + NORM_EPS)
    return cen * r, r


def norm_back(dy, n, r, gain):
    e = dy * gain
    return r * (
        e - jnp.mean(e, axis=-1, keepdims=True) - n * jnp.mean(e * n, axis=-1, keepdims=True)
    )


def device(x, y, z, core):
    x, y, z = x % 4, y % 4, z % 4
    return ((((z % 2) * 4 + x) * 4 + y) * 2 + core) * 2 + z // 2


def devices():
    return [(x, y, z, c) for x in range(4) for y in range(4) for z in range(4) for c in range(2)]


def column_step(step):
    return [(device(x, y, z + step, c), device(x, y, z, c)) for x, y, z, c in devices()]


def colour_groups():
    return [
        [device(x, y, x + 2 * y - colour, core) for x in range(4) for y in range(4)]
        for colour in range(4)
        for core in range(2)
    ]


def colour_step(step):
    sources = {
        1: ((1, 0, 0), (0, 0, -1)),
        2: ((0, 1, 0), (0, -1, 0)),
        3: ((-1, 0, 0), (0, 0, 1)),
    }[step]
    return [
        (device(x + sources[c][0], y + sources[c][1], z + sources[c][2], c), device(x, y, z, c))
        for x, y, z, c in devices()
    ]


def embed_kernel(tok_ref, cot_ref, table_ref, pos_ref, stream_ref, cot_out_ref, padded_ref):
    count = tok_ref.shape[0]
    padded_ref[...] = jnp.zeros(padded_ref.shape, F32)
    padded_ref[: table_ref.shape[0]] = table_ref[...]
    t0, t_rest = halves(padded_ref[...])
    t1, t2 = halves(padded_ref[...] - t0.astype(F32))
    hits = hits_of(pos_ref, count)
    stream_ref[...] = tok_ref[...].astype(F32) + (
        (dot_tn(hits, t2) + dot_tn(hits, t1)) + dot_tn(hits, t0)
    )
    cot_out_ref[...] = cot_ref[...]


def hits_of(pos_ref, count):
    return (
        lax.broadcasted_iota(jnp.int32, (64, count), 0) == jnp.broadcast_to(pos_ref[...], (64, count))
    ).astype(BF)


def layer_kernel(
    where_ref,
    res_ref,
    off_ref,
    norms_ref,
    pos_ref,
    stream_hbm,
    cot_hbm,
    own0,
    own1,
    own2,
    own3,
    oth0,
    oth1,
    oth2,
    oth3,
    result_hbm,
    in_grad_hbm,
    keep_hbm,
    send_hbm,
    wup,
    wdn,
    wqkv,
    wout,
    mixed,
    sorted_qkv,
    sorted_out,
    message,
    probs_ref,
    qkv_ref,
    ctx_ref,
    dqkv_ref,
    small_ref,
    weights_ref,
    stream_ref,
    cot_ref,
    result_ref,
    in_grad_ref,
    kept,
    sent,
    in_sems,
    out_sems,
):
    core = where_ref[0]
    half = where_ref[1]
    colour = where_ref[4]
    count = cot_ref.shape[0]
    loads = [
        pltpu.make_async_copy(source, weights_ref.at[k], in_sems.at[k])
        for k, source in enumerate((own0, own1, own2, own3, oth0, oth1, oth2, oth3))
    ]
    loads.append(pltpu.make_async_copy(stream_hbm, stream_ref, in_sems.at[8]))
    loads.append(pltpu.make_async_copy(cot_hbm, cot_ref, in_sems.at[9]))
    for load in loads[8:] + loads[:8]:
        load.start()

    def grouped(s, xy, first):
        ahead = xy // 4 + 2 * (xy % 4) - colour + 4
        return jnp.concatenate(
            [
                weights_ref[4 * s + ((ahead - z) & 3), xy].astype(F32)[first : first + BLOCK]
                for z in range(4)
            ],
            axis=0,
        )

    for load in loads[8:]:
        load.wait()
    stream_in = stream_ref[...]
    g1, s1, g2, s2 = (norms_ref[k : k + 1, :] for k in range(4))
    n1, r1 = norm_parts(stream_in)
    y1 = (n1 * g1 + s1).astype(BF)
    for s, at_core in ((0, core), (1, 1 - core)):
        for load in loads[4 * s : 4 * s + 4]:
            load.wait()
        for xy in range(16):
            mixed[at_core, xy * GROUP : (xy + 1) * GROUP] = grouped(s, xy, 24)
    for at_core, at, block in blocks_of_rows():
        for first, length, to in qkv_pieces(block):
            sorted_qkv[to : to + length] = mixed[at_core, at + first : at + first + length]
        sorted_out[block * 3 : block * 3 + 3] = mixed[at_core, at + 9 : at + 12]
    wqkv[...] = sorted_qkv[...].astype(BF)
    wout[...] = sorted_out[...].astype(BF)


    qkv_ref[...] = dot_nt(y1, wqkv[...]).astype(BF)

    def segments(shape, dim):
        at = lax.broadcasted_iota(jnp.int32, shape, dim)
        seg = at + 8
        for k in range(5):
            res = res_ref[k]
            off = off_ref[k]
            length = jnp.where(res == 0, SMALL_LEN, jnp.where(res == 1, BIG_LEN, 0))
            seg = jnp.where((at >= off) & (at < off + length), k, seg)
        return seg

    allowed = segments((count, count), 0) == segments((count, count), 1)
    lane = lax.broadcasted_iota(jnp.int32, (1, 128), 1)
    masks = ((lane < HD).astype(F32).astype(BF), (lane >= HD).astype(F32).astype(BF))
    scale = HD**-0.5
    for p in range(HEADS // 2):
        lo = p * 128
        q = qkv_ref[:, lo : lo + 128]
        k = qkv_ref[:, 384 + lo : 512 + lo]
        v = qkv_ref[:, 768 + lo : 896 + lo]
        ctx = 0.0
        for hh in range(2):
            scores = dot_nt(q * masks[hh], k) * scale
            scores = jnp.where(allowed, scores, -1e30)
            expo = jnp.exp(scores - jnp.max(scores, axis=-1, keepdims=True))
            probs = expo / jnp.sum(expo, axis=-1, keepdims=True)
            probs_ref[2 * p + hh] = probs
            ctx = ctx + dot(probs.astype(BF), v * masks[hh])
        ctx_ref[:, lo : lo + 128] = ctx.astype(BF)
    stream_mid = stream_in + dot(ctx_ref[...], wout[...])
    n2, r2 = norm_parts(stream_mid)
    y2 = (n2 * g2 + s2).astype(BF)

    cot = cot_ref[...]
    right = jnp.where(half == 0, y2, cot)
    out = stream_mid
    d_y2 = 0.0
    for k in range(4):
        for xy in range(8):
            at = k * 384 + xy * GROUP
            wup[at : at + GROUP] = grouped(k // 2, (k % 2) * 8 + xy, 0).astype(BF)
            wdn[at : at + GROUP] = grouped(k // 2, (k % 2) * 8 + xy, 12).astype(BF)
        wu = wup[k * 384 : (k + 1) * 384, :]
        wd = wdn[k * 384 : (k + 1) * 384, :]
        pre = dot_nt(y2, wu)
        cdf = 0.5 * (1.0 + lax.erf(pre * (2.0**-0.5)))
        hidden = (pre * cdf).astype(BF)
        slope = cdf + pre * (jnp.exp(-0.5 * pre * pre) * ((2.0 * math.pi) ** -0.5))
        d_pre = (slope * dot_nt(cot, wd)).astype(BF)
        out = out + dot(hidden, wd)
        d_y2 = d_y2 + dot(d_pre, wu)
        grad = dot_tn(jnp.where(half == 0, d_pre, hidden), right).reshape(8, GROUP, 384)
        at = (k % 2) * 8
        if k < 2:
            kept[at : at + 8] = grad.astype(BF)
        else:
            sent[at : at + 8] = grad.astype(BF)
    result_ref[...] = out.astype(BF)
    stores = [
        pltpu.make_async_copy(
            source.at[pl.ds(16 * k, 16)], target.at[pl.ds(16 * k, 16)], out_sems.at[2 * k + j]
        )
        for k in range(2)
        for j, (source, target) in enumerate(((sent, send_hbm), (kept, keep_hbm)))
    ]
    stores.append(pltpu.make_async_copy(result_ref, result_hbm, out_sems.at[4]))
    stores.append(pltpu.make_async_copy(in_grad_ref, in_grad_hbm, out_sems.at[5]))
    for k in (0, 1, 4):
        stores[k].start()
    gain2 = jnp.sum(d_y2 * n2, axis=0, keepdims=True)
    shift2 = jnp.sum(d_y2, axis=0, keepdims=True)
    d_mid = cot.astype(F32) + norm_back(d_y2, n2, r2, g2)

    d_attn = d_mid.astype(BF)
    d_ctx = dot_nt(d_attn, wout[...]).astype(BF)
    for p in range(HEADS // 2):
        lo = p * 128
        q = qkv_ref[:, lo : lo + 128]
        k = qkv_ref[:, 384 + lo : 512 + lo]
        v = qkv_ref[:, 768 + lo : 896 + lo]
        dc = d_ctx[:, lo : lo + 128]
        dq, dk, dv = 0.0, 0.0, 0.0
        for hh in range(2):
            probs = probs_ref[2 * p + hh]
            dcm = dc * masks[hh]
            d_probs = dot_nt(dcm, v)
            inner = jnp.sum(probs * d_probs, axis=-1, keepdims=True)
            d_scores = (probs * (d_probs - inner)).astype(BF)
            dq = dq + dot(d_scores, k * masks[hh])
            dk = dk + dot_tn(d_scores, q * masks[hh])
            dv = dv + dot_tn(probs.astype(BF), dcm)
        dqkv_ref[:, lo : lo + 128] = (dq * scale).astype(BF)
        dqkv_ref[:, 384 + lo : 512 + lo] = (dk * scale).astype(BF)
        dqkv_ref[:, 768 + lo : 896 + lo] = dv.astype(BF)
    d_y1 = dot(dqkv_ref[...], wqkv[...])
    in_grad = d_mid + norm_back(d_y1, n1, r1, g1)
    in_grad_ref[...] = in_grad
    stores[5].start()

    hits = hits_of(pos_ref, count)
    i0, i1 = halves(in_grad)
    pos_grad = dot(hits, i0) + dot(hits, i1)
    gain1 = jnp.sum(d_y1 * n1, axis=0, keepdims=True)
    shift1 = jnp.sum(d_y1, axis=0, keepdims=True)
    row = lax.broadcasted_iota(jnp.int32, (64, 384), 0)
    for at, value in ((50, gain1), (51, shift1), (52, gain2), (53, shift2)):
        pos_grad = jnp.where(row == at, jnp.broadcast_to(value, (64, 384)), pos_grad)
    sorted_out[...] = dot_tn(ctx_ref[...], d_attn)
    sorted_qkv[...] = dot_tn(dqkv_ref[...], y1)
    small_ref[...] = pos_grad

    @pl.when(half == 0)
    def _():
        zeros = jnp.zeros((8, D), F32)
        for at_core in range(2):
            for xy in range(16):
                rows = []
                for z in range(4):
                    block = (z * 16 + xy) * 2 + at_core
                    rows += [
                        small_ref[xy * 4 + z : xy * 4 + z + 1],
                        zeros,
                        sorted_out[block * 3 : block * 3 + 3],
                    ]
                message[at_core, xy] = jnp.concatenate(rows, axis=0).astype(BF)

    @pl.when(half == 1)
    def _():
        zeros = jnp.zeros((2, D), F32)
        for at_core in range(2):
            for xy in range(16):
                rows = []
                for z in range(4):
                    rows += [
                        sorted_qkv[to : to + length]
                        for _, length, to in qkv_pieces((z * 16 + xy) * 2 + at_core)
                    ]
                    rows += [small_ref[xy * 4 + z : xy * 4 + z + 1], zeros]
                message[at_core, xy] = jnp.concatenate(rows, axis=0).astype(BF)

    sent[16:] = message[1 - core]
    stores[2].start()
    kept[16:] = message[core]
    stores[3].start()
    for store in stores:
        store.wait()


def run_layer(where, res_ids, offsets, stream, cotangent, norms, pos, weights):
    count = stream.shape[0]
    smem = pl.BlockSpec(memory_space=pltpu.SMEM)
    vmem = pl.BlockSpec(memory_space=pltpu.VMEM)
    hbm = pl.BlockSpec(memory_space=pl.ANY)
    return pl.pallas_call(
        layer_kernel,
        out_shape=(
            jax.ShapeDtypeStruct((count, D), BF),
            jax.ShapeDtypeStruct((count, D), F32),
            jax.ShapeDtypeStruct((32, GROUP, D), BF),
            jax.ShapeDtypeStruct((32, GROUP, D), BF),
        ),
        in_specs=[smem] * 3 + [vmem] * 2 + [hbm] * 10,
        out_specs=(hbm,) * 4,
        scratch_shapes=[
            pltpu.VMEM((1536, D), BF),
            pltpu.VMEM((1536, D), BF),
            pltpu.VMEM((1152, D), BF),
            pltpu.VMEM((D, D), BF),
            pltpu.VMEM((2, 768, D), F32),
            pltpu.VMEM((1152, D), F32),
            pltpu.VMEM((D, D), F32),
            pltpu.VMEM((2, 16, GROUP, D), BF),
            pltpu.VMEM((HEADS, count, count), F32),
            pltpu.VMEM((count, 1152), BF),
            pltpu.VMEM((count, D), BF),
            pltpu.VMEM((count, 1152), BF),
            pltpu.VMEM((64, D), F32),
            pltpu.VMEM((8, 16, SENT, D), BF),
            pltpu.VMEM((count, D), F32),
            pltpu.VMEM((count, D), BF),
            pltpu.VMEM((count, D), BF),
            pltpu.VMEM((count, D), F32),
            pltpu.VMEM((32, GROUP, D), BF),
            pltpu.VMEM((32, GROUP, D), BF),
            pltpu.SemaphoreType.DMA((10,)),
            pltpu.SemaphoreType.DMA((6,)),
        ],
        compiler_params=pltpu.CompilerParams(vmem_limit_bytes=LAYER_VMEM),
        cost_estimate=pl.CostEstimate(
            flops=0, bytes_accessed=0, transcendentals=0
        ),
        name="layer",
    )(
        where, res_ids, offsets, norms, pos, stream, cotangent, *weights
    )


def product(a, b):
    (ah, al), (bh, bl) = a, b
    first = jnp.concatenate([ah, al], axis=1)
    return dot(first, jnp.concatenate([bh, bh], axis=0)) + dot(ah, bl)


def call(kernel, name, outs, args, scalars=0, scratch=(), flops=0, moved=0, vmem_bytes=VMEM):
    smem = pl.BlockSpec(memory_space=pltpu.SMEM)
    vmem = pl.BlockSpec(memory_space=pltpu.VMEM)
    return pl.pallas_call(
        kernel,
        out_shape=tuple(jax.ShapeDtypeStruct(shape, dtype) for shape, dtype in outs),
        in_specs=[smem] * scalars + [vmem] * (len(args) - scalars),
        out_specs=(vmem,) * len(outs),
        scratch_shapes=scratch,
        compiler_params=pltpu.CompilerParams(vmem_limit_bytes=vmem_bytes),
        cost_estimate=pl.CostEstimate(flops=flops, bytes_accessed=moved, transcendentals=0),
        name=name,
    )(*args)


def weights_kernel(qkv_ref, out_ref, up_ref, down_ref, rows_ref):
    rows = jnp.concatenate(
        [up_ref[...], down_ref[...], qkv_ref[...], out_ref[...], jnp.zeros((SENT - 36, D), F32)],
        axis=0,
    ).astype(BF)
    rows_ref[...] = jnp.broadcast_to(rows[None], rows_ref.shape)


def moments_kernel(where_ref, qkv_ref, out_ref, up_ref, down_ref, *old_refs):
    zeros = jnp.zeros((9, D), F32)
    old = (
        up_ref[...],
        jnp.concatenate([zeros, out_ref[...]], axis=0),
        down_ref[...],
        jnp.concatenate([qkv_ref[...], zeros[:3]], axis=0),
    )
    for z in range(4):

        @pl.when(where_ref[3] == z)
        def _(z=z):
            for step, ref in enumerate(old_refs):
                ref[...] = old[(z - step) % 4].astype(BF)


def join_kernel(where_ref, *refs):
    *sources, joined_ref, sent_ref = refs
    for z in range(4):

        @pl.when(where_ref[3] == z)
        def _(z=z):
            joined = jnp.concatenate(
                [sources[(at - z) % 4][...].astype(F32) for at in range(4)], axis=0
            ).astype(BF)
            joined_ref[...] = joined
            sent_ref[...] = jnp.broadcast_to(joined[None], sent_ref.shape)


def hold_kernel(keep_ref, held_ref):
    held_ref[...] = keep_ref[...]


def sum_kernel(parts_ref, piece_ref, sent_ref):
    total = parts_ref[0].astype(F32)
    for k in range(1, parts_ref.shape[0]):
        total = total + parts_ref[k].astype(F32)
    piece_ref[...] = total
    sent_ref[...] = jnp.broadcast_to(total.astype(BF)[None], sent_ref.shape)


def valid_rows(z):
    row = lax.broadcasted_iota(jnp.int32, (GROUP, D), 0) % BLOCK
    return jnp.where(z == 1, (row >= 9).astype(F32), jnp.where(z == 3, (row < 9).astype(F32), 1.0))


def tell_kernel(where_ref, own_ref, piece_ref, told_ref):
    z = where_ref[3]
    counts_all = (z == 1) & (where_ref[0] == 0)
    valid = jnp.where(counts_all, 1.0, valid_rows(z))
    total = jnp.zeros((GROUP, D), F32)
    for xy in range(16):
        g = own_ref[xy].astype(F32)
        total = total + g * g
    squares = jnp.full((1, D), jnp.sum(total * valid), F32)
    high = squares.astype(BF).astype(F32)
    mid = (squares - high).astype(BF).astype(F32)
    low = squares - high - mid
    for to in range(4):
        rows = jnp.concatenate(
            [piece_ref[to * BLOCK : (to + 1) * BLOCK, :], high, mid, low, jnp.zeros((1, D), F32)],
            axis=0,
        ).astype(BF)
        told_ref[2 * to] = rows
        told_ref[2 * to + 1] = rows


def small_kernel(where_ref, own_ref, places_ref, small_ref):
    small_ref[...] = dot(places_ref[where_ref[1]], own_ref[...].reshape(768, D)).astype(BF)


def clip(told_ref):
    total = jnp.zeros((1, 1), F32)
    for k in range(8):
        last = told_ref[k].astype(F32)
        total = total + (last[12:13, :1] + last[13:14, :1] + last[14:15, :1])
    grad_norm = jnp.sqrt(total)
    return grad_norm, jnp.minimum(1.0, CLIP_LIMIT / (grad_norm + 1e-06))


def orth_kernel(
    where_ref,
    told_ref,
    own_ref,
    oth_ref,
    old_own_ref,
    old_oth_ref,
    old_ref,
    piece_ref,
    out_ref,
    whole_ref,
):
    valid = valid_rows(where_ref[3])
    factor = clip(told_ref)[1]
    scaled = factor * valid
    for s, (grad_ref, before_ref) in enumerate(((own_ref, old_own_ref), (oth_ref, old_oth_ref))):
        for xy in range(16):
            at = s * 768 + xy * GROUP
            whole_ref[at : at + GROUP] = (
                MOMENTUM * before_ref[xy].astype(F32) + scaled * grad_ref[xy].astype(F32)
            ).astype(BF)
    whole = whole_ref[...]
    gram = dot_tn(whole, whole)
    eye = (
        lax.broadcasted_iota(jnp.int32, (D, D), 0) == lax.broadcasted_iota(jnp.int32, (D, D), 1)
    ).astype(F32)
    inv = 1.0 / (jnp.sqrt(jnp.sum(gram * eye)) + 1e-07)
    gram = gram * (inv * inv)
    mine = (MOMENTUM * old_ref[...].astype(F32) + scaled * piece_ref[...]) * inv
    for step in range(NS_STEPS - 2):
        parts = halves(gram)
        poly = halves(COEF_A * eye + COEF_B * gram + COEF_C * dot(parts[0], parts[0]))
        gram = product(halves(product(poly, parts)), poly)
        mine = product(halves(mine), poly)
    parts = halves(gram)
    poly = (COEF_A * eye + COEF_B * gram + COEF_C * product(parts, parts)).astype(BF)
    turned = dot(poly, parts[0]).astype(BF)
    both = dot(jnp.concatenate([turned, mine.astype(BF)], axis=0), poly)
    gram, mine = both[:D], both[D:]
    low = gram.astype(BF)
    poly = COEF_A * eye + COEF_B * gram + COEF_C * dot(low, low)
    mine = dot(mine.astype(BF), poly.astype(BF))
    for z in range(4):
        out_ref[z] = jnp.concatenate(
            [mine[z * BLOCK : (z + 1) * BLOCK], jnp.zeros((4, D), F32)], axis=0
        ).astype(BF)


def step_rate(rows_count, cols_count):
    return math.sqrt(max(rows_count, cols_count) / rows_count)


def moment_kernel(
    where_ref,
    told_ref,
    small_own_ref,
    small_near_ref,
    qkv_m_ref,
    out_m_ref,
    up_m_ref,
    down_m_ref,
    norms_ref,
    norm_m_ref,
    table_ref,
    pos_m_ref,
    grad_norm_ref,
    qkv_m_next,
    out_m_next,
    up_m_next,
    down_m_next,
    norm_m_next,
    norms_next,
    pos_m_next,
    table_next,
):
    grad_norm, factor = clip(told_ref)
    grad_norm_ref[...] = grad_norm
    for z, first, last, m_ref, m_next in (
        (3, 0, 9, qkv_m_ref, qkv_m_next),
        (1, 9, 12, out_m_ref, out_m_next),
        (0, 0, 12, up_m_ref, up_m_next),
        (2, 0, 12, down_m_ref, down_m_next),
    ):
        grad = told_ref[2 * z + where_ref[0]].astype(F32)[first:last]
        m_next[...] = MOMENTUM * m_ref[...] + factor * grad
    near = (where_ref[3] % 2 == 0).astype(F32)
    small = near * small_near_ref[...].astype(F32) + (1.0 - near) * small_own_ref[...].astype(F32)
    norm_fresh = MOMENTUM * norm_m_ref[...] + factor * small[50:54]
    norm_m_next[...] = norm_fresh
    norms_next[...] = norms_ref[...] - NORM_RATE * norm_fresh
    pos_fresh = MOMENTUM * pos_m_ref[...] + factor * small[:50]
    pos_m_next[...] = pos_fresh
    table_next[...] = table_ref[...] - SMALL_RATE * pos_fresh


def update_kernel(
    back_ref, qkv_ref, out_ref, up_ref, down_ref, qkv_next, out_next, up_next, down_next
):
    for z, first, last, rate, w_ref, w_next in (
        (3, 0, 9, step_rate(D, 3 * D), qkv_ref, qkv_next),
        (1, 9, 12, step_rate(D, D), out_ref, out_next),
        (0, 0, 12, step_rate(D, FF), up_ref, up_next),
        (2, 0, 12, step_rate(FF, D), down_ref, down_next),
    ):
        w_next[...] = w_ref[...] - rate * back_ref[z].astype(F32)[first:last]


def swapped(value):
    return lax.ppermute(value, "c", [(0, 1), (1, 0)])


def exchanged(value, axes):
    return lax.all_to_all(value, axes, 0, 0, tiled=True)


def everywhere(value, axes):
    peers = lax.axis_size(axes)
    return exchanged(jnp.broadcast_to(value[None], (peers, *value.shape)), axes)


def shards(
    tokens,
    cotangent,
    pos_table,
    norm_params,
    qkv_weight,
    out_weight,
    up_weight,
    down_weight,
    qkv_moment,
    out_moment,
    up_moment,
    down_moment,
    norm_moment,
    pos_moment,
    res_ids,
    offsets,
    pos_index,
):
    z = lax.axis_index(COLUMN)
    colour = (lax.axis_index("x") + 2 * lax.axis_index("y") - z) % 4
    where = jnp.stack(
        [lax.axis_index("c"), lax.axis_index("zh"), lax.axis_index(PLANE), z, colour]
    ).astype(jnp.int32)
    weights = (qkv_weight.T, out_weight, up_weight.T, down_weight)
    moments = (qkv_moment.T, out_moment, up_moment.T, down_moment)

    (rows,) = call(
        weights_kernel, "weights", (((16, SENT, D), BF),), weights, vmem_bytes=ALL_VMEM
    )
    old = call(
        moments_kernel,
        "moments",
        (((BLOCK, D), BF),) * 4,
        (where, *moments),
        scalars=1,
        vmem_bytes=ALL_VMEM,
    )
    old = [old[0]] + [lax.ppermute(old[k], AXES, column_step(k)) for k in (1, 2, 3)]
    pos = pos_index.reshape(1, -1)
    stream, cotangent = call(
        embed_kernel,
        "embed",
        ((tokens.shape, F32), (tokens.shape, BF)),
        (tokens, cotangent, pos_table, pos),
        scratch=[pltpu.VMEM((64, D), F32)],
        vmem_bytes=ALL_VMEM,
    )

    own = [lax.all_to_all(rows, AXES, 0, 0, axis_index_groups=colour_groups(), tiled=True)]
    own[0], stream, cotangent, *old = lax.optimization_barrier(
        (own[0], stream, cotangent, *old)
    )
    old, old_sent = call(
        join_kernel,
        "join",
        (((GROUP, D), BF), ((16, GROUP, D), BF)),
        (where, *old),
        scalars=1,
    )
    own += [lax.ppermute(own[0], AXES, colour_step(step)) for step in (1, 2, 3)]
    other = [swapped(value) for value in own]
    old_sent, other[0] = lax.optimization_barrier((old_sent, other[0]))
    old_own = exchanged(old_sent, PLANE)

    result, in_grad, keep, send = run_layer(
        where,
        res_ids,
        offsets,
        stream,
        cotangent,
        norm_params,
        pos,
        (*own, *other),
    )
    keep, send, old_own = lax.optimization_barrier((keep, send, old_own))
    old_other = swapped(old_own)
    (keep,) = call(hold_kernel, "hold", ((keep.shape, BF),), (keep,))
    pair = (keep.astype(F32) + swapped(send).astype(F32)).astype(BF)
    piece, sent = call(
        sum_kernel, "sum", (((GROUP, D), F32), ((16, GROUP, D), BF)), (exchanged(pair, HALF),)
    )
    grads = exchanged(sent, PLANE)
    (told,) = call(
        tell_kernel, "tell", (((8, 16, D), BF),), (where, grads, piece), scalars=1
    )
    told, grads_sent = lax.optimization_barrier((told, grads))
    told = exchanged(told, COLUMN_CORES)
    grads_other = swapped(grads_sent)
    (small,) = call(
        small_kernel,
        "small",
        (((64, D), BF),),
        (where, grads_sent, jnp.asarray(small_places(), BF)),
        scalars=1,
    )
    small_near = lax.ppermute(small, "zl", [(1, 0)])
    (orth,) = call(
        orth_kernel,
        "orth",
        (((4, 16, D), BF),),
        (where, told, grads, grads_other, old_own, old_other, old, piece),
        scalars=1,
        scratch=[pltpu.VMEM((1536, D), BF)],
        flops=8_000_000_000,
        moved=4_000_000,
    )
    back = exchanged(orth, COLUMN)
    like = lambda a: (a.shape, F32)
    grad_norm, *fresh = call(
        moment_kernel,
        "moment",
        (
            ((1, 1), F32),
            *(like(a) for a in moments),
            like(norm_moment),
            like(norm_params),
            like(pos_moment),
            like(pos_table),
        ),
        (where, told, small, small_near, *moments, norm_params, norm_moment, pos_table, pos_moment),
        scalars=1,
    )
    news = call(update_kernel, "update", [like(a) for a in weights], (back, *weights))
    return (
        result,
        in_grad,
        grad_norm.reshape(()),
        fresh[0].T,
        news[0].T,
        fresh[1],
        news[1],
        fresh[2].T,
        news[2].T,
        fresh[3],
        news[3],
        *fresh[4:],
    )


def solution(mesh):
    finer = Mesh(
        mesh.devices.reshape(2, 4, 4, 2, mesh.shape["tensor"]), ("zl", "x", "y", "c", "zh")
    )
    columns = P(None, ROWS)
    rows = P(ROWS, None)
    return jax.shard_map(
        shards,
        mesh=finer,
        in_specs=(
            P(DP, None),
            P(DP, None),
            P(),
            P(),
            columns,
            rows,
            columns,
            rows,
            columns,
            rows,
            columns,
            rows,
            P(),
            P(),
            P(DP),
            P(DP),
            P(DP),
        ),
        out_specs=(
            P(DP, None),
            P(DP, None),
            P(),
            columns,
            columns,
            rows,
            rows,
            columns,
            columns,
            rows,
            rows,
            P(),
            P(),
            P(),
            P(),
        ),
        check_vma=False,
    )
```

```python
import math

import jax
import jax.numpy as jnp
import numpy as np
from jax import lax
from jax.experimental import pallas as pl
from jax.experimental.pallas import tpu as pltpu
from jax.sharding import Mesh
from jax.sharding import PartitionSpec as P

D = 384
HEADS = 6
HD = 64
FF = 1536
SMALL_LEN = 50
BIG_LEN = 145
NS_STEPS = 5
COEF_A = 3.4445
COEF_B = -4.775
COEF_C = 2.0315
NORM_EPS = 1e-06
CLIP_LIMIT = 1.0
MOMENTUM = 0.5
SMALL_RATE = 10.0
NORM_RATE = 40.0

DP = ("zl", "x", "y", "c")
ROWS = ("zh",) + DP
COLUMN = ("zh", "zl")
PLANE = ("x", "y")
HALF = ("zl", "x", "y")
COLUMN_CORES = ("zh", "zl", "c")
AXES = ("zl", "x", "y", "c", "zh")

BF = jnp.bfloat16
F32 = jnp.float32
BLOCK = 12
GROUP = 48
SENT = 40
VMEM = 24 << 20
ALL_VMEM = 60 << 20
LAYER_VMEM = 60 << 20


def qkv_pieces(block):
    pieces = []
    row = block * 9
    while row < block * 9 + 9:
        head, rest = divmod(row, 3 * HD)
        part, e = divmod(rest, HD)
        count = min(HD - e, block * 9 + 9 - row)
        pieces.append((row - block * 9, count, part * HEADS * HD + head * HD + e))
        row += count
    return pieces


def blocks_of_rows():
    return [
        (core, xy * GROUP + z * BLOCK, (z * 16 + xy) * 2 + core)
        for core in range(2)
        for xy in range(16)
        for z in range(4)
    ]


def small_places():
    places = np.zeros((2, 64, 768), np.float32)
    for n in range(64):
        at = (n // 4) * GROUP + (n % 4) * BLOCK
        places[0, n, at] = 1
        places[1, n, at + 9] = 1
    return places


def dot(a, b):
    return lax.dot_general(a, b, (((1,), (0,)), ((), ())), preferred_element_type=F32)


def dot_nt(a, b):
    return lax.dot_general(a, b, (((1,), (1,)), ((), ())), preferred_element_type=F32)


def dot_tn(a, b):
    return lax.dot_general(a, b, (((0,), (0,)), ((), ())), preferred_element_type=F32)


def halves(a):
    high = a.astype(BF)
    return high, (a - high.astype(F32)).astype(BF)


def norm_parts(v):
    cen = v - jnp.mean(v, axis=-1, keepdims=True)
    var = jnp.mean(cen * cen, axis=-1, keepdims=True)
    r = lax.rsqrt(var + NORM_EPS)
    return cen * r, r


def norm_back(dy, n, r, gain):
    e = dy * gain
    return r * (
        e - jnp.mean(e, axis=-1, keepdims=True) - n * jnp.mean(e * n, axis=-1, keepdims=True)
    )


def device(x, y, z, core):
    x, y, z = x % 4, y % 4, z % 4
    return ((((z % 2) * 4 + x) * 4 + y) * 2 + core) * 2 + z // 2


def chip_z():
    return 2 * lax.axis_index("zh") + lax.axis_index("zl")


def devices():
    return [(x, y, z, c) for x in range(4) for y in range(4) for z in range(4) for c in range(2)]


def column_step(step):
    return [(device(x, y, z + step, c), device(x, y, z, c)) for x, y, z, c in devices()]


def colour_groups():
    return [
        [device(x, y, x + 2 * y + colour, core) for x in range(4) for y in range(4)]
        for colour in range(4)
        for core in range(2)
    ]


def colour_step(step):
    sources = {
        1: ((-1, 0, 0), (0, 0, 1)),
        2: ((0, 1, 0), (0, -1, 0)),
        3: ((1, 0, 0), (0, 0, -1)),
    }[step]
    return [
        (device(x + sources[c][0], y + sources[c][1], z + sources[c][2], c), device(x, y, z, c))
        for x, y, z, c in devices()
    ]


def embed_kernel(tok_ref, cot_ref, table_ref, pos_ref, stream_ref, cot_out_ref, padded_ref):
    count = tok_ref.shape[0]
    padded_ref[...] = jnp.zeros(padded_ref.shape, F32)
    padded_ref[: table_ref.shape[0]] = table_ref[...]
    t0, t_rest = halves(padded_ref[...])
    t1, t2 = halves(padded_ref[...] - t0.astype(F32))
    hits = hits_of(pos_ref, count)
    stream_ref[...] = tok_ref[...].astype(F32) + (
        (dot_tn(hits, t2) + dot_tn(hits, t1)) + dot_tn(hits, t0)
    )
    cot_out_ref[...] = cot_ref[...]


def hits_of(pos_ref, count):
    return (
        lax.broadcasted_iota(jnp.int32, (64, count), 0) == jnp.broadcast_to(pos_ref[...], (64, count))
    ).astype(BF)


def layer_kernel(
    where_ref,
    res_ref,
    off_ref,
    norms_ref,
    pos_ref,
    stream_hbm,
    cot_hbm,
    own0,
    own1,
    own2,
    own3,
    oth0,
    oth1,
    oth2,
    oth3,
    result_hbm,
    in_grad_hbm,
    keep_hbm,
    send_hbm,
    wup,
    wdn,
    wqkv,
    wout,
    mixed,
    sorted_qkv,
    sorted_out,
    message,
    probs_ref,
    qkv_ref,
    ctx_ref,
    dqkv_ref,
    small_ref,
    weights_ref,
    stream_ref,
    cot_ref,
    result_ref,
    in_grad_ref,
    kept,
    sent,
    in_sems,
    out_sems,
):
    core = where_ref[0]
    half = where_ref[1]
    colour = where_ref[2]
    count = cot_ref.shape[0]
    loads = [
        pltpu.make_async_copy(source, weights_ref.at[k], in_sems.at[k])
        for k, source in enumerate((own0, own1, own2, own3, oth0, oth1, oth2, oth3))
    ]
    loads.append(pltpu.make_async_copy(stream_hbm, stream_ref, in_sems.at[8]))
    loads.append(pltpu.make_async_copy(cot_hbm, cot_ref, in_sems.at[9]))
    for load in loads[8:] + loads[:8]:
        load.start()

    def grouped(s, xy, first):
        behind = xy // 4 + 2 * (xy % 4) + colour
        return jnp.concatenate(
            [
                weights_ref[4 * s + ((z + 12 - behind) & 3), xy].astype(F32)[first : first + BLOCK]
                for z in range(4)
            ],
            axis=0,
        )

    for load in loads[8:]:
        load.wait()
    stream_in = stream_ref[...]
    g1, s1, g2, s2 = (norms_ref[k : k + 1, :] for k in range(4))
    n1, r1 = norm_parts(stream_in)
    y1 = (n1 * g1 + s1).astype(BF)
    for s, at_core in ((0, core), (1, 1 - core)):
        for load in loads[4 * s : 4 * s + 4]:
            load.wait()
        for xy in range(16):
            mixed[at_core, xy * GROUP : (xy + 1) * GROUP] = grouped(s, xy, 24)
    for at_core, at, block in blocks_of_rows():
        for first, length, to in qkv_pieces(block):
            sorted_qkv[to : to + length] = mixed[at_core, at + first : at + first + length]
        sorted_out[block * 3 : block * 3 + 3] = mixed[at_core, at + 9 : at + 12]
    wqkv[...] = sorted_qkv[...].astype(BF)
    wout[...] = sorted_out[...].astype(BF)


    qkv_ref[...] = dot_nt(y1, wqkv[...]).astype(BF)

    def segments(shape, dim):
        at = lax.broadcasted_iota(jnp.int32, shape, dim)
        seg = at + 8
        for k in range(5):
            res = res_ref[k]
            off = off_ref[k]
            length = jnp.where(res == 0, SMALL_LEN, jnp.where(res == 1, BIG_LEN, 0))
            seg = jnp.where((at >= off) & (at < off + length), k, seg)
        return seg

    allowed = segments((count, count), 0) == segments((count, count), 1)
    lane = lax.broadcasted_iota(jnp.int32, (1, 128), 1)
    masks = ((lane < HD).astype(F32).astype(BF), (lane >= HD).astype(F32).astype(BF))
    scale = HD**-0.5
    for p in range(HEADS // 2):
        lo = p * 128
        q = qkv_ref[:, lo : lo + 128]
        k = qkv_ref[:, 384 + lo : 512 + lo]
        v = qkv_ref[:, 768 + lo : 896 + lo]
        ctx = 0.0
        for hh in range(2):
            scores = dot_nt(q * masks[hh], k) * scale
            scores = jnp.where(allowed, scores, -1e30)
            expo = jnp.exp(scores - jnp.max(scores, axis=-1, keepdims=True))
            probs = expo / jnp.sum(expo, axis=-1, keepdims=True)
            probs_ref[2 * p + hh] = probs
            ctx = ctx + dot(probs.astype(BF), v * masks[hh])
        ctx_ref[:, lo : lo + 128] = ctx.astype(BF)
    stream_mid = stream_in + dot(ctx_ref[...], wout[...])
    n2, r2 = norm_parts(stream_mid)
    y2 = (n2 * g2 + s2).astype(BF)

    cot = cot_ref[...]
    right = jnp.where(half == 0, y2, cot)
    out = stream_mid
    d_y2 = 0.0
    for k in range(4):
        for xy in range(8):
            at = k * 384 + xy * GROUP
            wup[at : at + GROUP] = grouped(k // 2, (k % 2) * 8 + xy, 0).astype(BF)
            wdn[at : at + GROUP] = grouped(k // 2, (k % 2) * 8 + xy, 12).astype(BF)
        wu = wup[k * 384 : (k + 1) * 384, :]
        wd = wdn[k * 384 : (k + 1) * 384, :]
        pre = dot_nt(y2, wu)
        cdf = 0.5 * (1.0 + lax.erf(pre * (2.0**-0.5)))
        hidden = (pre * cdf).astype(BF)
        slope = cdf + pre * (jnp.exp(-0.5 * pre * pre) * ((2.0 * math.pi) ** -0.5))
        d_pre = (slope * dot_nt(cot, wd)).astype(BF)
        out = out + dot(hidden, wd)
        d_y2 = d_y2 + dot(d_pre, wu)
        grad = dot_tn(jnp.where(half == 0, d_pre, hidden), right).reshape(8, GROUP, 384)
        at = (k % 2) * 8
        if k < 2:
            kept[at : at + 8] = grad.astype(BF)
        else:
            sent[at : at + 8] = grad.astype(BF)
    result_ref[...] = out.astype(BF)
    stores = [
        pltpu.make_async_copy(
            source.at[pl.ds(16 * k, 16)], target.at[pl.ds(16 * k, 16)], out_sems.at[2 * k + j]
        )
        for k in range(2)
        for j, (source, target) in enumerate(((sent, send_hbm), (kept, keep_hbm)))
    ]
    stores.append(pltpu.make_async_copy(result_ref, result_hbm, out_sems.at[4]))
    stores.append(pltpu.make_async_copy(in_grad_ref, in_grad_hbm, out_sems.at[5]))
    for k in (0, 1, 4):
        stores[k].start()
    gain2 = jnp.sum(d_y2 * n2, axis=0, keepdims=True)
    shift2 = jnp.sum(d_y2, axis=0, keepdims=True)
    d_mid = cot.astype(F32) + norm_back(d_y2, n2, r2, g2)

    d_attn = d_mid.astype(BF)
    d_ctx = dot_nt(d_attn, wout[...]).astype(BF)
    for p in range(HEADS // 2):
        lo = p * 128
        q = qkv_ref[:, lo : lo + 128]
        k = qkv_ref[:, 384 + lo : 512 + lo]
        v = qkv_ref[:, 768 + lo : 896 + lo]
        dc = d_ctx[:, lo : lo + 128]
        dq, dk, dv = 0.0, 0.0, 0.0
        for hh in range(2):
            probs = probs_ref[2 * p + hh]
            dcm = dc * masks[hh]
            d_probs = dot_nt(dcm, v)
            inner = jnp.sum(probs * d_probs, axis=-1, keepdims=True)
            d_scores = (probs * (d_probs - inner)).astype(BF)
            dq = dq + dot(d_scores, k * masks[hh])
            dk = dk + dot_tn(d_scores, q * masks[hh])
            dv = dv + dot_tn(probs.astype(BF), dcm)
        dqkv_ref[:, lo : lo + 128] = (dq * scale).astype(BF)
        dqkv_ref[:, 384 + lo : 512 + lo] = (dk * scale).astype(BF)
        dqkv_ref[:, 768 + lo : 896 + lo] = dv.astype(BF)
    d_y1 = dot(dqkv_ref[...], wqkv[...])
    in_grad = d_mid + norm_back(d_y1, n1, r1, g1)
    in_grad_ref[...] = in_grad
    stores[5].start()

    hits = hits_of(pos_ref, count)
    i0, i1 = halves(in_grad)
    pos_grad = dot(hits, i0) + dot(hits, i1)
    gain1 = jnp.sum(d_y1 * n1, axis=0, keepdims=True)
    shift1 = jnp.sum(d_y1, axis=0, keepdims=True)
    row = lax.broadcasted_iota(jnp.int32, (64, 384), 0)
    for at, value in ((50, gain1), (51, shift1), (52, gain2), (53, shift2)):
        pos_grad = jnp.where(row == at, jnp.broadcast_to(value, (64, 384)), pos_grad)
    sorted_out[...] = dot_tn(ctx_ref[...], d_attn)
    sorted_qkv[...] = dot_tn(dqkv_ref[...], y1)
    small_ref[...] = pos_grad

    @pl.when(half == 0)
    def _():
        zeros = jnp.zeros((8, D), F32)
        for at_core in range(2):
            for xy in range(16):
                rows = []
                for z in range(4):
                    block = (z * 16 + xy) * 2 + at_core
                    rows += [
                        small_ref[xy * 4 + z : xy * 4 + z + 1],
                        zeros,
                        sorted_out[block * 3 : block * 3 + 3],
                    ]
                message[at_core, xy] = jnp.concatenate(rows, axis=0).astype(BF)

    @pl.when(half == 1)
    def _():
        zeros = jnp.zeros((2, D), F32)
        for at_core in range(2):
            for xy in range(16):
                rows = []
                for z in range(4):
                    rows += [
                        sorted_qkv[to : to + length]
                        for _, length, to in qkv_pieces((z * 16 + xy) * 2 + at_core)
                    ]
                    rows += [small_ref[xy * 4 + z : xy * 4 + z + 1], zeros]
                message[at_core, xy] = jnp.concatenate(rows, axis=0).astype(BF)

    sent[16:] = message[1 - core]
    stores[2].start()
    kept[16:] = message[core]
    stores[3].start()
    for store in stores:
        store.wait()


def run_layer(where, res_ids, offsets, stream, cotangent, norms, pos, weights):
    count = stream.shape[0]
    smem = pl.BlockSpec(memory_space=pltpu.SMEM)
    vmem = pl.BlockSpec(memory_space=pltpu.VMEM)
    hbm = pl.BlockSpec(memory_space=pl.ANY)
    return pl.pallas_call(
        layer_kernel,
        out_shape=(
            jax.ShapeDtypeStruct((count, D), BF),
            jax.ShapeDtypeStruct((count, D), F32),
            jax.ShapeDtypeStruct((32, GROUP, D), BF),
            jax.ShapeDtypeStruct((32, GROUP, D), BF),
        ),
        in_specs=[smem] * 3 + [vmem] * 2 + [hbm] * 10,
        out_specs=(hbm,) * 4,
        scratch_shapes=[
            pltpu.VMEM((1536, D), BF),
            pltpu.VMEM((1536, D), BF),
            pltpu.VMEM((1152, D), BF),
            pltpu.VMEM((D, D), BF),
            pltpu.VMEM((2, 768, D), F32),
            pltpu.VMEM((1152, D), F32),
            pltpu.VMEM((D, D), F32),
            pltpu.VMEM((2, 16, GROUP, D), BF),
            pltpu.VMEM((HEADS, count, count), F32),
            pltpu.VMEM((count, 1152), BF),
            pltpu.VMEM((count, D), BF),
            pltpu.VMEM((count, 1152), BF),
            pltpu.VMEM((64, D), F32),
            pltpu.VMEM((8, 16, SENT, D), BF),
            pltpu.VMEM((count, D), F32),
            pltpu.VMEM((count, D), BF),
            pltpu.VMEM((count, D), BF),
            pltpu.VMEM((count, D), F32),
            pltpu.VMEM((32, GROUP, D), BF),
            pltpu.VMEM((32, GROUP, D), BF),
            pltpu.SemaphoreType.DMA((10,)),
            pltpu.SemaphoreType.DMA((6,)),
        ],
        compiler_params=pltpu.CompilerParams(vmem_limit_bytes=LAYER_VMEM),
        cost_estimate=pl.CostEstimate(
            flops=0, bytes_accessed=0, transcendentals=0
        ),
        name="layer",
    )(
        where, res_ids, offsets, norms, pos, stream, cotangent, *weights
    )


def product(a, b):
    (ah, al), (bh, bl) = a, b
    first = jnp.concatenate([ah, al], axis=1)
    return dot(first, jnp.concatenate([bh, bh], axis=0)) + dot(ah, bl)


def call(kernel, name, outs, args, scratch=(), flops=0, moved=0, vmem_bytes=VMEM):
    vmem = pl.BlockSpec(memory_space=pltpu.VMEM)
    return pl.pallas_call(
        kernel,
        out_shape=tuple(jax.ShapeDtypeStruct(shape, dtype) for shape, dtype in outs),
        in_specs=[vmem] * len(args),
        out_specs=(vmem,) * len(outs),
        scratch_shapes=scratch,
        compiler_params=pltpu.CompilerParams(vmem_limit_bytes=vmem_bytes),
        cost_estimate=pl.CostEstimate(flops=flops, bytes_accessed=moved, transcendentals=0),
        name=name,
    )(*args)


def weights_kernel(qkv_ref, out_ref, up_ref, down_ref, rows_ref):
    rows = jnp.concatenate(
        [up_ref[...], down_ref[...], qkv_ref[...], out_ref[...], jnp.zeros((SENT - 36, D), F32)],
        axis=0,
    ).astype(BF)
    rows_ref[...] = jnp.broadcast_to(rows[None], rows_ref.shape)


def moments_kernel(qkv_ref, out_ref, up_ref, down_ref, *old_refs):
    zeros = jnp.zeros((9, D), F32)
    old = (
        up_ref[...],
        jnp.concatenate([zeros, out_ref[...]], axis=0),
        down_ref[...],
        jnp.concatenate([qkv_ref[...], zeros[:3]], axis=0),
    )
    for z in range(4):

        @pl.when(chip_z() == z)
        def _(z=z):
            for step, ref in enumerate(old_refs):
                ref[...] = old[(z - step) % 4].astype(BF)


def join_kernel(*refs):
    *sources, joined_ref, sent_ref = refs
    for z in range(4):

        @pl.when(chip_z() == z)
        def _(z=z):
            joined = jnp.concatenate(
                [sources[(at - z) % 4][...].astype(F32) for at in range(4)], axis=0
            ).astype(BF)
            joined_ref[...] = joined
            sent_ref[...] = jnp.broadcast_to(joined[None], sent_ref.shape)


def hold_kernel(keep_ref, held_ref):
    held_ref[...] = keep_ref[...]


def sum_kernel(parts_ref, piece_ref, sent_ref):
    total = parts_ref[0].astype(F32)
    for k in range(1, parts_ref.shape[0]):
        total = total + parts_ref[k].astype(F32)
    piece_ref[...] = total
    sent_ref[...] = jnp.broadcast_to(total.astype(BF)[None], sent_ref.shape)


def valid_rows(z):
    row = lax.broadcasted_iota(jnp.int32, (GROUP, D), 0) % BLOCK
    return jnp.where(z == 1, (row >= 9).astype(F32), jnp.where(z == 3, (row < 9).astype(F32), 1.0))


def tell_kernel(own_ref, piece_ref, told_ref):
    z = chip_z()
    counts_all = (z == 1) & (lax.axis_index("c") == 0)
    valid = jnp.where(counts_all, 1.0, valid_rows(z))
    total = jnp.zeros((GROUP, D), F32)
    for xy in range(16):
        g = own_ref[xy].astype(F32)
        total = total + g * g
    squares = jnp.full((1, D), jnp.sum(total * valid), F32)
    high = squares.astype(BF).astype(F32)
    mid = (squares - high).astype(BF).astype(F32)
    low = squares - high - mid
    for to in range(4):
        rows = jnp.concatenate(
            [piece_ref[to * BLOCK : (to + 1) * BLOCK, :], high, mid, low, jnp.zeros((1, D), F32)],
            axis=0,
        ).astype(BF)
        told_ref[2 * to] = rows
        told_ref[2 * to + 1] = rows


def small_kernel(own_ref, places_ref, small_ref):
    small_ref[...] = dot(places_ref[lax.axis_index("zh")], own_ref[...].reshape(768, D)).astype(BF)


def clip(told_ref):
    total = jnp.zeros((1, 1), F32)
    for k in range(8):
        last = told_ref[k].astype(F32)
        total = total + (last[12:13, :1] + last[13:14, :1] + last[14:15, :1])
    grad_norm = jnp.sqrt(total)
    return grad_norm, jnp.minimum(1.0, CLIP_LIMIT / (grad_norm + 1e-06))


def orth_kernel(
    told_ref,
    own_ref,
    oth_ref,
    old_own_ref,
    old_oth_ref,
    old_ref,
    piece_ref,
    *refs,
):
    *out_refs, whole_ref = refs
    valid = valid_rows(chip_z())
    factor = clip(told_ref)[1]
    scaled = factor * valid
    for s, (grad_ref, before_ref) in enumerate(((own_ref, old_own_ref), (oth_ref, old_oth_ref))):
        for xy in range(16):
            at = s * 768 + xy * GROUP
            whole_ref[at : at + GROUP] = (
                MOMENTUM * before_ref[xy].astype(F32) + scaled * grad_ref[xy].astype(F32)
            ).astype(BF)
    whole = whole_ref[...]
    gram = dot_tn(whole, whole)
    eye = (
        lax.broadcasted_iota(jnp.int32, (D, D), 0) == lax.broadcasted_iota(jnp.int32, (D, D), 1)
    ).astype(F32)
    inv = 1.0 / (jnp.sqrt(jnp.sum(gram * eye)) + 1e-07)
    gram = gram * (inv * inv)
    mine = (MOMENTUM * old_ref[...].astype(F32) + scaled * piece_ref[...]) * inv
    for step in range(NS_STEPS - 2):
        parts = halves(gram)
        poly = halves(COEF_A * eye + COEF_B * gram + COEF_C * dot(parts[0], parts[0]))
        gram = product(halves(product(poly, parts)), poly)
        mine = product(halves(mine), poly)
    parts = halves(gram)
    poly = (COEF_A * eye + COEF_B * gram + COEF_C * product(parts, parts)).astype(BF)
    turned = dot(poly, parts[0]).astype(BF)
    both = dot(jnp.concatenate([turned, mine.astype(BF)], axis=0), poly)
    gram, mine = both[:D], both[D:]
    low = gram.astype(BF)
    poly = COEF_A * eye + COEF_B * gram + COEF_C * dot(low, low)
    mine = dot(mine.astype(BF), poly.astype(BF))
    for z in range(4):

        @pl.when(chip_z() == z)
        def _(z=z):
            for step, ref in enumerate(out_refs):
                to = (z - step) % 4
                ref[...] = mine[to * BLOCK : (to + 1) * BLOCK].astype(BF)


def step_rate(rows_count, cols_count):
    return math.sqrt(max(rows_count, cols_count) / rows_count)


def moment_kernel(
    told_ref,
    small_own_ref,
    small_near_ref,
    qkv_m_ref,
    out_m_ref,
    up_m_ref,
    down_m_ref,
    norms_ref,
    norm_m_ref,
    table_ref,
    pos_m_ref,
    grad_norm_ref,
    qkv_m_next,
    out_m_next,
    up_m_next,
    down_m_next,
    norm_m_next,
    norms_next,
    pos_m_next,
    table_next,
):
    grad_norm, factor = clip(told_ref)
    grad_norm_ref[...] = grad_norm
    for z, first, last, m_ref, m_next in (
        (3, 0, 9, qkv_m_ref, qkv_m_next),
        (1, 9, 12, out_m_ref, out_m_next),
        (0, 0, 12, up_m_ref, up_m_next),
        (2, 0, 12, down_m_ref, down_m_next),
    ):
        grad = told_ref[2 * z + lax.axis_index("c")].astype(F32)[first:last]
        m_next[...] = MOMENTUM * m_ref[...] + factor * grad
    near = (lax.axis_index("zl") == 0).astype(F32)
    small = near * small_near_ref[...].astype(F32) + (1.0 - near) * small_own_ref[...].astype(F32)
    norm_fresh = MOMENTUM * norm_m_ref[...] + factor * small[50:54]
    norm_m_next[...] = norm_fresh
    norms_next[...] = norms_ref[...] - NORM_RATE * norm_fresh
    pos_fresh = MOMENTUM * pos_m_ref[...] + factor * small[:50]
    pos_m_next[...] = pos_fresh
    table_next[...] = table_ref[...] - SMALL_RATE * pos_fresh


def update_kernel(
    orth0,
    orth1,
    orth2,
    orth3,
    qkv_ref,
    out_ref,
    up_ref,
    down_ref,
    qkv_next,
    out_next,
    up_next,
    down_next,
):
    here = chip_z()
    sources = [ref[...].astype(F32) for ref in (orth0, orth1, orth2, orth3)]
    for z, first, last, rate, w_ref, w_next in (
        (3, 0, 9, step_rate(D, 3 * D), qkv_ref, qkv_next),
        (1, 9, 12, step_rate(D, D), out_ref, out_next),
        (0, 0, 12, step_rate(D, FF), up_ref, up_next),
        (2, 0, 12, step_rate(FF, D), down_ref, down_next),
    ):
        orth = sources[z]
        for step in range(1, 4):
            orth = jnp.where(here == step, sources[(z - step) % 4], orth)
        w_next[...] = w_ref[...] - rate * orth[first:last]


def swapped(value):
    return lax.ppermute(value, "c", [(0, 1), (1, 0)])


def exchanged(value, axes):
    return lax.all_to_all(value, axes, 0, 0, tiled=True)


def everywhere(value, axes):
    peers = lax.axis_size(axes)
    return exchanged(jnp.broadcast_to(value[None], (peers, *value.shape)), axes)


def shards(
    tokens,
    cotangent,
    pos_table,
    norm_params,
    qkv_weight,
    out_weight,
    up_weight,
    down_weight,
    qkv_moment,
    out_moment,
    up_moment,
    down_moment,
    norm_moment,
    pos_moment,
    res_ids,
    offsets,
    pos_index,
):
    weights = (qkv_weight.T, out_weight, up_weight.T, down_weight)
    moments = (qkv_moment.T, out_moment, up_moment.T, down_moment)

    (rows,) = call(
        weights_kernel, "weights", (((16, SENT, D), BF),), weights, vmem_bytes=ALL_VMEM
    )
    old = call(
        moments_kernel,
        "moments",
        (((BLOCK, D), BF),) * 4,
        moments,
    )
    old = [old[0]] + [lax.ppermute(old[k], AXES, column_step(k)) for k in (1, 2, 3)]
    pos = pos_index.reshape(1, -1)
    stream, cotangent = call(
        embed_kernel,
        "embed",
        ((tokens.shape, F32), (tokens.shape, BF)),
        (tokens, cotangent, pos_table, pos),
        scratch=[pltpu.VMEM((64, D), F32)],
        vmem_bytes=ALL_VMEM,
    )

    own = [lax.all_to_all(rows, AXES, 0, 0, axis_index_groups=colour_groups(), tiled=True)]
    own[0], stream, cotangent, *old = lax.optimization_barrier(
        (own[0], stream, cotangent, *old)
    )
    old, old_sent = call(
        join_kernel,
        "join",
        (((GROUP, D), BF), ((16, GROUP, D), BF)),
        old,
    )
    own += [lax.ppermute(own[0], AXES, colour_step(step)) for step in (1, 2, 3)]
    other = [swapped(value) for value in own]
    old_sent, other[0] = lax.optimization_barrier((old_sent, other[0]))
    old_own = exchanged(old_sent, PLANE)

    colour = (chip_z() + 12 - lax.axis_index("x") - 2 * lax.axis_index("y")) & 3
    where = jnp.stack([lax.axis_index("c"), lax.axis_index("zh"), colour]).astype(jnp.int32)
    result, in_grad, keep, send = run_layer(
        where,
        res_ids,
        offsets,
        stream,
        cotangent,
        norm_params,
        pos,
        (*own, *other),
    )
    keep, send, old_own = lax.optimization_barrier((keep, send, old_own))
    old_other = swapped(old_own)
    (keep,) = call(hold_kernel, "hold", ((keep.shape, BF),), (keep,))
    pair = (keep.astype(F32) + swapped(send).astype(F32)).astype(BF)
    piece, sent = call(
        sum_kernel, "sum", (((GROUP, D), F32), ((16, GROUP, D), BF)), (exchanged(pair, HALF),)
    )
    grads = exchanged(sent, PLANE)
    (told,) = call(
        tell_kernel, "tell", (((8, 16, D), BF),), (grads, piece)
    )
    told, grads_sent = lax.optimization_barrier((told, grads))
    told = exchanged(told, COLUMN_CORES)
    grads_other = swapped(grads_sent)
    (small,) = call(
        small_kernel,
        "small",
        (((64, D), BF),),
        (grads_sent, jnp.asarray(small_places(), BF)),
    )
    small_near = lax.ppermute(small, "zl", [(1, 0)])
    orth = call(
        orth_kernel,
        "orth",
        (((BLOCK, D), BF),) * 4,
        (told, grads, grads_other, old_own, old_other, old, piece),
        scratch=[pltpu.VMEM((1536, D), BF)],
        flops=8_000_000_000,
        moved=4_000_000,
    )
    back = [orth[0]] + [lax.ppermute(orth[k], AXES, column_step(k)) for k in (1, 2, 3)]
    like = lambda a: (a.shape, F32)
    grad_norm, *fresh = call(
        moment_kernel,
        "moment",
        (
            ((1, 1), F32),
            *(like(a) for a in moments),
            like(norm_moment),
            like(norm_params),
            like(pos_moment),
            like(pos_table),
        ),
        (told, small, small_near, *moments, norm_params, norm_moment, pos_table, pos_moment),
    )
    news = call(
        update_kernel, "update", [like(a) for a in weights], (*back, *weights)
    )
    return (
        result,
        in_grad,
        grad_norm.reshape(()),
        fresh[0].T,
        news[0].T,
        fresh[1],
        news[1],
        fresh[2].T,
        news[2].T,
        fresh[3],
        news[3],
        *fresh[4:],
    )


def solution(mesh):
    finer = Mesh(
        mesh.devices.reshape(2, 4, 4, 2, mesh.shape["tensor"]), ("zl", "x", "y", "c", "zh")
    )
    columns = P(None, ROWS)
    rows = P(ROWS, None)
    return jax.shard_map(
        shards,
        mesh=finer,
        in_specs=(
            P(DP, None),
            P(DP, None),
            P(),
            P(),
            columns,
            rows,
            columns,
            rows,
            columns,
            rows,
            columns,
            rows,
            P(),
            P(),
            P(DP),
            P(DP),
            P(DP),
        ),
        out_specs=(
            P(DP, None),
            P(DP, None),
            P(),
            columns,
            columns,
            rows,
            rows,
            columns,
            columns,
            rows,
            rows,
            P(),
            P(),
            P(),
            P(),
        ),
        check_vma=False,
    )
```

```python
import math

import jax
import jax.numpy as jnp
import numpy as np
from jax import lax
from jax.experimental import pallas as pl
from jax.experimental.pallas import tpu as pltpu
from jax.sharding import Mesh
from jax.sharding import PartitionSpec as P

D = 384
HEADS = 6
HD = 64
FF = 1536
SMALL_LEN = 50
BIG_LEN = 145
NS_STEPS = 5
COEF_A = 3.4445
COEF_B = -4.775
COEF_C = 2.0315
NORM_EPS = 1e-06
CLIP_LIMIT = 1.0
MOMENTUM = 0.5
SMALL_RATE = 10.0
NORM_RATE = 40.0

DP = ("zl", "x", "y", "c")
ROWS = ("zh",) + DP
COLUMN = ("zh", "zl")
PLANE = ("x", "y")
HALF = ("zl", "x", "y")
COLUMN_CORES = ("zh", "zl", "c")
AXES = ("zl", "x", "y", "c", "zh")

BF = jnp.bfloat16
F32 = jnp.float32
BLOCK = 12
GROUP = 48
SENT = 40
VMEM = 24 << 20
ALL_VMEM = 60 << 20
LAYER_VMEM = 57 << 20


def qkv_pieces(block):
    pieces = []
    row = block * 9
    while row < block * 9 + 9:
        head, rest = divmod(row, 3 * HD)
        part, e = divmod(rest, HD)
        count = min(HD - e, block * 9 + 9 - row)
        pieces.append((row - block * 9, count, part * HEADS * HD + head * HD + e))
        row += count
    return pieces


def blocks_of_rows():
    return [
        (core, xy * GROUP + z * BLOCK, (z * 16 + xy) * 2 + core)
        for core in range(2)
        for xy in range(16)
        for z in range(4)
    ]


def small_places():
    places = np.zeros((2, 64, 768), np.float32)
    for n in range(64):
        at = (n // 4) * GROUP + (n % 4) * BLOCK
        places[0, n, at] = 1
        places[1, n, at + 9] = 1
    return places


def dot(a, b):
    return lax.dot_general(a, b, (((1,), (0,)), ((), ())), preferred_element_type=F32)


def dot_nt(a, b):
    return lax.dot_general(a, b, (((1,), (1,)), ((), ())), preferred_element_type=F32)


def dot_tn(a, b):
    return lax.dot_general(a, b, (((0,), (0,)), ((), ())), preferred_element_type=F32)


def halves(a):
    high = a.astype(BF)
    return high, (a - high.astype(F32)).astype(BF)


def norm_parts(v):
    cen = v - jnp.mean(v, axis=-1, keepdims=True)
    var = jnp.mean(cen * cen, axis=-1, keepdims=True)
    r = lax.rsqrt(var + NORM_EPS)
    return cen * r, r


def norm_back(dy, n, r, gain):
    e = dy * gain
    return r * (
        e - jnp.mean(e, axis=-1, keepdims=True) - n * jnp.mean(e * n, axis=-1, keepdims=True)
    )


def device(x, y, z, core):
    x, y, z = x % 4, y % 4, z % 4
    return ((((z % 2) * 4 + x) * 4 + y) * 2 + core) * 2 + z // 2


def chip_z():
    return 2 * lax.axis_index("zh") + lax.axis_index("zl")


def devices():
    return [(x, y, z, c) for x in range(4) for y in range(4) for z in range(4) for c in range(2)]


def column_step(step):
    return [(device(x, y, z + step, c), device(x, y, z, c)) for x, y, z, c in devices()]


def colour_groups():
    return [
        [device(x, y, x + 2 * y + colour, core) for x in range(4) for y in range(4)]
        for colour in range(4)
        for core in range(2)
    ]


def colour_step(step):
    sources = {
        1: ((-1, 0, 0), (0, 0, 1)),
        2: ((0, 1, 0), (0, -1, 0)),
        3: ((1, 0, 0), (0, 0, -1)),
    }[step]
    return [
        (device(x + sources[c][0], y + sources[c][1], z + sources[c][2], c), device(x, y, z, c))
        for x, y, z, c in devices()
    ]


def embed_kernel(tok_ref, cot_ref, table_ref, pos_ref, stream_ref, cot_out_ref, padded_ref):
    count = tok_ref.shape[0]
    padded_ref[...] = jnp.zeros(padded_ref.shape, F32)
    padded_ref[: table_ref.shape[0]] = table_ref[...]
    t0, t_rest = halves(padded_ref[...])
    t1, t2 = halves(padded_ref[...] - t0.astype(F32))
    hits = hits_of(pos_ref, count)
    stream_ref[...] = tok_ref[...].astype(F32) + (
        (dot_tn(hits, t2) + dot_tn(hits, t1)) + dot_tn(hits, t0)
    )
    cot_out_ref[...] = cot_ref[...]


def hits_of(pos_ref, count):
    return (
        lax.broadcasted_iota(jnp.int32, (64, count), 0) == jnp.broadcast_to(pos_ref[...], (64, count))
    ).astype(BF)


def layer_kernel(
    where_ref,
    res_ref,
    off_ref,
    norms_ref,
    pos_ref,
    stream_hbm,
    cot_hbm,
    own0,
    own1,
    own2,
    own3,
    oth0,
    oth1,
    oth2,
    oth3,
    result_hbm,
    in_grad_hbm,
    keep_hbm,
    send_hbm,
    wup,
    wdn,
    wqkv,
    wout,
    mixed,
    sorted_qkv,
    sorted_out,
    message,
    probs_ref,
    qkv_ref,
    ctx_ref,
    dqkv_ref,
    small_ref,
    stream_ref,
    cot_ref,
    result_ref,
    in_grad_ref,
    kept,
    sent,
    in_sems,
    out_sems,
):
    core = where_ref[0]
    half = where_ref[1]
    colour = where_ref[2]
    count = cot_ref.shape[0]
    parts = ((own0, own1, own2, own3), (oth0, oth1, oth2, oth3))
    loads = [
        pltpu.make_async_copy(stream_hbm, stream_ref, in_sems.at[0]),
        pltpu.make_async_copy(cot_hbm, cot_ref, in_sems.at[1]),
    ]
    for load in loads:
        load.start()

    for here in range(4):

        @pl.when(colour == here)
        def _(here=here):
            for s in range(2):
                for xy in range(16):
                    behind = xy // 4 + 2 * (xy % 4) + here
                    blocks = [parts[s][(z - behind) % 4][xy].astype(F32) for z in range(4)]
                    groups = [
                        jnp.concatenate([block[k : k + BLOCK] for block in blocks], axis=0)
                        for k in (0, 12, 24)
                    ]
                    at = s * 768 + xy * GROUP
                    wup[at : at + GROUP] = groups[0].astype(BF)
                    wdn[at : at + GROUP] = groups[1].astype(BF)
                    mixed[core if s == 0 else 1 - core, xy * GROUP : (xy + 1) * GROUP] = groups[2]

    for load in loads:
        load.wait()
    stream_in = stream_ref[...]
    g1, s1, g2, s2 = (norms_ref[k : k + 1, :] for k in range(4))
    n1, r1 = norm_parts(stream_in)
    y1 = (n1 * g1 + s1).astype(BF)
    for at_core, at, block in blocks_of_rows():
        for first, length, to in qkv_pieces(block):
            sorted_qkv[to : to + length] = mixed[at_core, at + first : at + first + length]
        sorted_out[block * 3 : block * 3 + 3] = mixed[at_core, at + 9 : at + 12]
    wqkv[...] = sorted_qkv[...].astype(BF)
    wout[...] = sorted_out[...].astype(BF)


    qkv_ref[...] = dot_nt(y1, wqkv[...]).astype(BF)

    def segments(shape, dim):
        at = lax.broadcasted_iota(jnp.int32, shape, dim)
        seg = at + 8
        for k in range(5):
            res = res_ref[k]
            off = off_ref[k]
            length = jnp.where(res == 0, SMALL_LEN, jnp.where(res == 1, BIG_LEN, 0))
            seg = jnp.where((at >= off) & (at < off + length), k, seg)
        return seg

    allowed = segments((count, count), 0) == segments((count, count), 1)
    lane = lax.broadcasted_iota(jnp.int32, (1, 128), 1)
    masks = ((lane < HD).astype(F32).astype(BF), (lane >= HD).astype(F32).astype(BF))
    scale = HD**-0.5
    for p in range(HEADS // 2):
        lo = p * 128
        q = qkv_ref[:, lo : lo + 128]
        k = qkv_ref[:, 384 + lo : 512 + lo]
        v = qkv_ref[:, 768 + lo : 896 + lo]
        ctx = 0.0
        for hh in range(2):
            scores = dot_nt(q * masks[hh], k) * scale
            scores = jnp.where(allowed, scores, -1e30)
            expo = jnp.exp(scores - jnp.max(scores, axis=-1, keepdims=True))
            probs = expo / jnp.sum(expo, axis=-1, keepdims=True)
            probs_ref[2 * p + hh] = probs
            ctx = ctx + dot(probs.astype(BF), v * masks[hh])
        ctx_ref[:, lo : lo + 128] = ctx.astype(BF)
    stream_mid = stream_in + dot(ctx_ref[...], wout[...])
    n2, r2 = norm_parts(stream_mid)
    y2 = (n2 * g2 + s2).astype(BF)

    cot = cot_ref[...]
    right = jnp.where(half == 0, y2, cot)
    out = stream_mid
    d_y2 = 0.0
    for k, target in enumerate((kept, sent)):
        wu = wup[k * 768 : (k + 1) * 768, :]
        wd = wdn[k * 768 : (k + 1) * 768, :]
        pre = dot_nt(y2, wu)
        cdf = 0.5 * (1.0 + lax.erf(pre * (2.0**-0.5)))
        hidden = (pre * cdf).astype(BF)
        slope = cdf + pre * (jnp.exp(-0.5 * pre * pre) * ((2.0 * math.pi) ** -0.5))
        d_pre = (slope * dot_nt(cot, wd)).astype(BF)
        out = out + dot(hidden, wd)
        d_y2 = d_y2 + dot(d_pre, wu)
        grad = dot_tn(jnp.where(half == 0, d_pre, hidden), right)
        target[...] = grad.astype(BF).reshape(16, GROUP, D)
    result_ref[...] = out.astype(BF)
    stores = [
        pltpu.make_async_copy(source, target.at[pl.ds(first, 16)], out_sems.at[k])
        for k, (source, target, first) in enumerate(
            (
                (sent, send_hbm, 0),
                (kept, keep_hbm, 0),
                (message.at[1 - core], send_hbm, 16),
                (message.at[core], keep_hbm, 16),
            )
        )
    ]
    stores.append(pltpu.make_async_copy(result_ref, result_hbm, out_sems.at[4]))
    stores.append(pltpu.make_async_copy(in_grad_ref, in_grad_hbm, out_sems.at[5]))
    for k in (0, 1, 4):
        stores[k].start()
    gain2 = jnp.sum(d_y2 * n2, axis=0, keepdims=True)
    shift2 = jnp.sum(d_y2, axis=0, keepdims=True)
    d_mid = cot.astype(F32) + norm_back(d_y2, n2, r2, g2)

    d_attn = d_mid.astype(BF)
    d_ctx = dot_nt(d_attn, wout[...]).astype(BF)
    for p in range(HEADS // 2):
        lo = p * 128
        q = qkv_ref[:, lo : lo + 128]
        k = qkv_ref[:, 384 + lo : 512 + lo]
        v = qkv_ref[:, 768 + lo : 896 + lo]
        dc = d_ctx[:, lo : lo + 128]
        dq, dk, dv = 0.0, 0.0, 0.0
        for hh in range(2):
            probs = probs_ref[2 * p + hh]
            dcm = dc * masks[hh]
            d_probs = dot_nt(dcm, v)
            inner = jnp.sum(probs * d_probs, axis=-1, keepdims=True)
            d_scores = (probs * (d_probs - inner)).astype(BF)
            dq = dq + dot(d_scores, k * masks[hh])
            dk = dk + dot_tn(d_scores, q * masks[hh])
            dv = dv + dot_tn(probs.astype(BF), dcm)
        dqkv_ref[:, lo : lo + 128] = (dq * scale).astype(BF)
        dqkv_ref[:, 384 + lo : 512 + lo] = (dk * scale).astype(BF)
        dqkv_ref[:, 768 + lo : 896 + lo] = dv.astype(BF)
    d_y1 = dot(dqkv_ref[...], wqkv[...])
    in_grad = d_mid + norm_back(d_y1, n1, r1, g1)
    in_grad_ref[...] = in_grad
    stores[5].start()

    hits = hits_of(pos_ref, count)
    i0, i1 = halves(in_grad)
    pos_grad = dot(hits, i0) + dot(hits, i1)
    gain1 = jnp.sum(d_y1 * n1, axis=0, keepdims=True)
    shift1 = jnp.sum(d_y1, axis=0, keepdims=True)
    row = lax.broadcasted_iota(jnp.int32, (64, 384), 0)
    for at, value in ((50, gain1), (51, shift1), (52, gain2), (53, shift2)):
        pos_grad = jnp.where(row == at, jnp.broadcast_to(value, (64, 384)), pos_grad)
    sorted_out[...] = dot_tn(ctx_ref[...], d_attn)
    sorted_qkv[...] = dot_tn(dqkv_ref[...], y1)
    small_ref[...] = pos_grad

    @pl.when(half == 0)
    def _():
        zeros = jnp.zeros((8, D), F32)
        for at_core in range(2):
            for xy in range(16):
                rows = []
                for z in range(4):
                    block = (z * 16 + xy) * 2 + at_core
                    rows += [
                        small_ref[xy * 4 + z : xy * 4 + z + 1],
                        zeros,
                        sorted_out[block * 3 : block * 3 + 3],
                    ]
                message[at_core, xy] = jnp.concatenate(rows, axis=0).astype(BF)

    @pl.when(half == 1)
    def _():
        zeros = jnp.zeros((2, D), F32)
        for at_core in range(2):
            for xy in range(16):
                rows = []
                for z in range(4):
                    rows += [
                        sorted_qkv[to : to + length]
                        for _, length, to in qkv_pieces((z * 16 + xy) * 2 + at_core)
                    ]
                    rows += [small_ref[xy * 4 + z : xy * 4 + z + 1], zeros]
                message[at_core, xy] = jnp.concatenate(rows, axis=0).astype(BF)

    stores[2].start()
    stores[3].start()
    for store in stores:
        store.wait()


def run_layer(where, res_ids, offsets, stream, cotangent, norms, pos, weights):
    count = stream.shape[0]
    smem = pl.BlockSpec(memory_space=pltpu.SMEM)
    vmem = pl.BlockSpec(memory_space=pltpu.VMEM)
    hbm = pl.BlockSpec(memory_space=pl.ANY)
    return pl.pallas_call(
        layer_kernel,
        out_shape=(
            jax.ShapeDtypeStruct((count, D), BF),
            jax.ShapeDtypeStruct((count, D), F32),
            jax.ShapeDtypeStruct((32, GROUP, D), BF),
            jax.ShapeDtypeStruct((32, GROUP, D), BF),
        ),
        in_specs=[smem] * 3 + [vmem] * 2 + [hbm] * 2 + [vmem] * 8,
        out_specs=(hbm,) * 4,
        scratch_shapes=[
            pltpu.VMEM((1536, D), BF),
            pltpu.VMEM((1536, D), BF),
            pltpu.VMEM((1152, D), BF),
            pltpu.VMEM((D, D), BF),
            pltpu.VMEM((2, 768, D), F32),
            pltpu.VMEM((1152, D), F32),
            pltpu.VMEM((D, D), F32),
            pltpu.VMEM((2, 16, GROUP, D), BF),
            pltpu.VMEM((HEADS, count, count), F32),
            pltpu.VMEM((count, 1152), BF),
            pltpu.VMEM((count, D), BF),
            pltpu.VMEM((count, 1152), BF),
            pltpu.VMEM((64, D), F32),
            pltpu.VMEM((count, D), F32),
            pltpu.VMEM((count, D), BF),
            pltpu.VMEM((count, D), BF),
            pltpu.VMEM((count, D), F32),
            pltpu.VMEM((16, GROUP, D), BF),
            pltpu.VMEM((16, GROUP, D), BF),
            pltpu.SemaphoreType.DMA((2,)),
            pltpu.SemaphoreType.DMA((6,)),
        ],
        compiler_params=pltpu.CompilerParams(vmem_limit_bytes=LAYER_VMEM),
        cost_estimate=pl.CostEstimate(
            flops=0, bytes_accessed=0, transcendentals=0
        ),
        name="layer",
    )(
        where, res_ids, offsets, norms, pos, stream, cotangent, *weights
    )


def product(a, b):
    (ah, al), (bh, bl) = a, b
    first = jnp.concatenate([ah, al], axis=1)
    return dot(first, jnp.concatenate([bh, bh], axis=0)) + dot(ah, bl)


def call(kernel, name, outs, args, scratch=(), flops=0, moved=0, vmem_bytes=VMEM):
    vmem = pl.BlockSpec(memory_space=pltpu.VMEM)
    return pl.pallas_call(
        kernel,
        out_shape=tuple(jax.ShapeDtypeStruct(shape, dtype) for shape, dtype in outs),
        in_specs=[vmem] * len(args),
        out_specs=(vmem,) * len(outs),
        scratch_shapes=scratch,
        compiler_params=pltpu.CompilerParams(vmem_limit_bytes=vmem_bytes),
        cost_estimate=pl.CostEstimate(flops=flops, bytes_accessed=moved, transcendentals=0),
        name=name,
    )(*args)


def weights_kernel(qkv_ref, out_ref, up_ref, down_ref, rows_ref):
    rows = jnp.concatenate(
        [up_ref[...], down_ref[...], qkv_ref[...], out_ref[...], jnp.zeros((SENT - 36, D), F32)],
        axis=0,
    ).astype(BF)
    rows_ref[...] = jnp.broadcast_to(rows[None], rows_ref.shape)


def moments_kernel(qkv_ref, out_ref, up_ref, down_ref, *old_refs):
    zeros = jnp.zeros((9, D), F32)
    old = (
        up_ref[...],
        jnp.concatenate([zeros, out_ref[...]], axis=0),
        down_ref[...],
        jnp.concatenate([qkv_ref[...], zeros[:3]], axis=0),
    )
    for z in range(4):

        @pl.when(chip_z() == z)
        def _(z=z):
            for step, ref in enumerate(old_refs):
                ref[...] = old[(z - step) % 4].astype(BF)


def join_kernel(*refs):
    *sources, joined_ref, sent_ref = refs
    for z in range(4):

        @pl.when(chip_z() == z)
        def _(z=z):
            joined = jnp.concatenate(
                [sources[(at - z) % 4][...].astype(F32) for at in range(4)], axis=0
            ).astype(BF)
            joined_ref[...] = joined
            sent_ref[...] = jnp.broadcast_to(joined[None], sent_ref.shape)


def hold_kernel(keep_ref, held_ref):
    held_ref[...] = keep_ref[...]


def sum_kernel(parts_ref, piece_ref, sent_ref):
    total = parts_ref[0].astype(F32)
    for k in range(1, parts_ref.shape[0]):
        total = total + parts_ref[k].astype(F32)
    piece_ref[...] = total
    sent_ref[...] = jnp.broadcast_to(total.astype(BF)[None], sent_ref.shape)


def valid_rows(z):
    row = lax.broadcasted_iota(jnp.int32, (GROUP, D), 0) % BLOCK
    return jnp.where(z == 1, (row >= 9).astype(F32), jnp.where(z == 3, (row < 9).astype(F32), 1.0))


def tell_kernel(own_ref, piece_ref, told_ref):
    z = chip_z()
    counts_all = (z == 1) & (lax.axis_index("c") == 0)
    valid = jnp.where(counts_all, 1.0, valid_rows(z))
    total = jnp.zeros((GROUP, D), F32)
    for xy in range(16):
        g = own_ref[xy].astype(F32)
        total = total + g * g
    squares = jnp.full((1, D), jnp.sum(total * valid), F32)
    high = squares.astype(BF).astype(F32)
    mid = (squares - high).astype(BF).astype(F32)
    low = squares - high - mid
    for to in range(4):
        rows = jnp.concatenate(
            [piece_ref[to * BLOCK : (to + 1) * BLOCK, :], high, mid, low, jnp.zeros((1, D), F32)],
            axis=0,
        ).astype(BF)
        told_ref[2 * to] = rows
        told_ref[2 * to + 1] = rows


def small_kernel(own_ref, places_ref, small_ref):
    small_ref[...] = dot(places_ref[lax.axis_index("zh")], own_ref[...].reshape(768, D)).astype(BF)


def clip(told_ref):
    total = jnp.zeros((1, 1), F32)
    for k in range(8):
        last = told_ref[k].astype(F32)
        total = total + (last[12:13, :1] + last[13:14, :1] + last[14:15, :1])
    grad_norm = jnp.sqrt(total)
    return grad_norm, jnp.minimum(1.0, CLIP_LIMIT / (grad_norm + 1e-06))


def orth_kernel(
    told_ref,
    own_ref,
    oth_ref,
    old_own_ref,
    old_oth_ref,
    old_ref,
    piece_ref,
    *refs,
):
    *out_refs, whole_ref = refs
    valid = valid_rows(chip_z())
    factor = clip(told_ref)[1]
    scaled = factor * valid
    for s, (grad_ref, before_ref) in enumerate(((own_ref, old_own_ref), (oth_ref, old_oth_ref))):
        for xy in range(16):
            at = s * 768 + xy * GROUP
            whole_ref[at : at + GROUP] = (
                MOMENTUM * before_ref[xy].astype(F32) + scaled * grad_ref[xy].astype(F32)
            ).astype(BF)
    whole = whole_ref[...]
    gram = dot_tn(whole, whole)
    eye = (
        lax.broadcasted_iota(jnp.int32, (D, D), 0) == lax.broadcasted_iota(jnp.int32, (D, D), 1)
    ).astype(F32)
    inv = 1.0 / (jnp.sqrt(jnp.sum(gram * eye)) + 1e-07)
    gram = gram * (inv * inv)
    mine = (MOMENTUM * old_ref[...].astype(F32) + scaled * piece_ref[...]) * inv
    turned = mine.T
    for step in range(NS_STEPS - 2):
        parts = halves(gram)
        poly = halves(COEF_A * eye + COEF_B * gram + COEF_C * dot(parts[0], parts[0]))
        inner = halves(product(poly, parts))
        more = halves(turned)
        both = product(
            poly, [jnp.concatenate([inner[k], more[k]], axis=1) for k in range(2)]
        )
        gram, turned = both[:, :D], both[:, D:]
    parts = halves(gram)
    poly = (COEF_A * eye + COEF_B * gram + COEF_C * product(parts, parts)).astype(BF)
    inner = dot(poly, parts[0]).astype(BF)
    both = dot(poly, jnp.concatenate([inner, turned.astype(BF)], axis=1))
    gram, turned = both[:, :D], both[:, D:]
    low = gram.astype(BF)
    poly = COEF_A * eye + COEF_B * gram + COEF_C * dot(low, low)
    mine = dot(poly.astype(BF), turned.astype(BF)).T
    for z in range(4):

        @pl.when(chip_z() == z)
        def _(z=z):
            for step, ref in enumerate(out_refs):
                to = (z - step) % 4
                ref[...] = mine[to * BLOCK : (to + 1) * BLOCK].astype(BF)


def step_rate(rows_count, cols_count):
    return math.sqrt(max(rows_count, cols_count) / rows_count)


def moment_kernel(
    told_ref,
    small_own_ref,
    small_near_ref,
    qkv_m_ref,
    out_m_ref,
    up_m_ref,
    down_m_ref,
    norms_ref,
    norm_m_ref,
    table_ref,
    pos_m_ref,
    grad_norm_ref,
    qkv_m_next,
    out_m_next,
    up_m_next,
    down_m_next,
    norm_m_next,
    norms_next,
    pos_m_next,
    table_next,
):
    grad_norm, factor = clip(told_ref)
    grad_norm_ref[...] = grad_norm
    for z, first, last, m_ref, m_next in (
        (3, 0, 9, qkv_m_ref, qkv_m_next),
        (1, 9, 12, out_m_ref, out_m_next),
        (0, 0, 12, up_m_ref, up_m_next),
        (2, 0, 12, down_m_ref, down_m_next),
    ):
        grad = told_ref[2 * z + lax.axis_index("c")].astype(F32)[first:last]
        m_next[...] = MOMENTUM * m_ref[...] + factor * grad
    near = (lax.axis_index("zl") == 0).astype(F32)
    small = near * small_near_ref[...].astype(F32) + (1.0 - near) * small_own_ref[...].astype(F32)
    norm_fresh = MOMENTUM * norm_m_ref[...] + factor * small[50:54]
    norm_m_next[...] = norm_fresh
    norms_next[...] = norms_ref[...] - NORM_RATE * norm_fresh
    pos_fresh = MOMENTUM * pos_m_ref[...] + factor * small[:50]
    pos_m_next[...] = pos_fresh
    table_next[...] = table_ref[...] - SMALL_RATE * pos_fresh


def update_kernel(
    orth0,
    orth1,
    orth2,
    orth3,
    qkv_ref,
    out_ref,
    up_ref,
    down_ref,
    qkv_next,
    out_next,
    up_next,
    down_next,
):
    here = chip_z()
    sources = [ref[...].astype(F32) for ref in (orth0, orth1, orth2, orth3)]
    for z, first, last, rate, w_ref, w_next in (
        (3, 0, 9, step_rate(D, 3 * D), qkv_ref, qkv_next),
        (1, 9, 12, step_rate(D, D), out_ref, out_next),
        (0, 0, 12, step_rate(D, FF), up_ref, up_next),
        (2, 0, 12, step_rate(FF, D), down_ref, down_next),
    ):
        orth = sources[z]
        for step in range(1, 4):
            orth = jnp.where(here == step, sources[(z - step) % 4], orth)
        w_next[...] = w_ref[...] - rate * orth[first:last]


def swapped(value):
    return lax.ppermute(value, "c", [(0, 1), (1, 0)])


def exchanged(value, axes):
    return lax.all_to_all(value, axes, 0, 0, tiled=True)


def everywhere(value, axes):
    peers = lax.axis_size(axes)
    return exchanged(jnp.broadcast_to(value[None], (peers, *value.shape)), axes)


def shards(
    tokens,
    cotangent,
    pos_table,
    norm_params,
    qkv_weight,
    out_weight,
    up_weight,
    down_weight,
    qkv_moment,
    out_moment,
    up_moment,
    down_moment,
    norm_moment,
    pos_moment,
    res_ids,
    offsets,
    pos_index,
):
    weights = (qkv_weight.T, out_weight, up_weight.T, down_weight)
    moments = (qkv_moment.T, out_moment, up_moment.T, down_moment)

    (rows,) = call(
        weights_kernel, "weights", (((16, SENT, D), BF),), weights, vmem_bytes=ALL_VMEM
    )
    old = call(
        moments_kernel,
        "moments",
        (((BLOCK, D), BF),) * 4,
        moments,
    )
    old = [old[0]] + [lax.ppermute(old[k], AXES, column_step(k)) for k in (1, 2, 3)]
    pos = pos_index.reshape(1, -1)
    stream, cotangent = call(
        embed_kernel,
        "embed",
        ((tokens.shape, F32), (tokens.shape, BF)),
        (tokens, cotangent, pos_table, pos),
        scratch=[pltpu.VMEM((64, D), F32)],
        vmem_bytes=ALL_VMEM,
    )

    own = [lax.all_to_all(rows, AXES, 0, 0, axis_index_groups=colour_groups(), tiled=True)]
    own[0], stream, cotangent, *old = lax.optimization_barrier(
        (own[0], stream, cotangent, *old)
    )
    old, old_sent = call(
        join_kernel,
        "join",
        (((GROUP, D), BF), ((16, GROUP, D), BF)),
        old,
    )
    own += [lax.ppermute(own[0], AXES, colour_step(step)) for step in (1, 2, 3)]
    other = [swapped(value) for value in own]
    old_sent, other[0] = lax.optimization_barrier((old_sent, other[0]))
    old_own = exchanged(old_sent, PLANE)

    colour = (chip_z() + 12 - lax.axis_index("x") - 2 * lax.axis_index("y")) & 3
    where = jnp.stack([lax.axis_index("c"), lax.axis_index("zh"), colour]).astype(jnp.int32)
    result, in_grad, keep, send = run_layer(
        where,
        res_ids,
        offsets,
        stream,
        cotangent,
        norm_params,
        pos,
        (*own, *other),
    )
    keep, send, old_own = lax.optimization_barrier((keep, send, old_own))
    old_other = swapped(old_own)
    (keep,) = call(hold_kernel, "hold", ((keep.shape, BF),), (keep,))
    pair = (keep.astype(F32) + swapped(send).astype(F32)).astype(BF)
    piece, sent = call(
        sum_kernel, "sum", (((GROUP, D), F32), ((16, GROUP, D), BF)), (exchanged(pair, HALF),)
    )
    grads = exchanged(sent, PLANE)
    (told,) = call(
        tell_kernel, "tell", (((8, 16, D), BF),), (grads, piece)
    )
    told, grads_sent = lax.optimization_barrier((told, grads))
    told = exchanged(told, COLUMN_CORES)
    grads_other = swapped(grads_sent)
    (small,) = call(
        small_kernel,
        "small",
        (((64, D), BF),),
        (grads_sent, jnp.asarray(small_places(), BF)),
    )
    small_near = lax.ppermute(small, "zl", [(1, 0)])
    orth = call(
        orth_kernel,
        "orth",
        (((BLOCK, D), BF),) * 4,
        (told, grads, grads_other, old_own, old_other, old, piece),
        scratch=[pltpu.VMEM((1536, D), BF)],
        flops=8_000_000_000,
        moved=4_000_000,
    )
    back = [orth[0]] + [lax.ppermute(orth[k], AXES, column_step(k)) for k in (1, 2, 3)]
    like = lambda a: (a.shape, F32)
    grad_norm, *fresh = call(
        moment_kernel,
        "moment",
        (
            ((1, 1), F32),
            *(like(a) for a in moments),
            like(norm_moment),
            like(norm_params),
            like(pos_moment),
            like(pos_table),
        ),
        (told, small, small_near, *moments, norm_params, norm_moment, pos_table, pos_moment),
    )
    news = call(
        update_kernel, "update", [like(a) for a in weights], (*back, *weights)
    )
    return (
        result,
        in_grad,
        grad_norm.reshape(()),
        fresh[0].T,
        news[0].T,
        fresh[1],
        news[1],
        fresh[2].T,
        news[2].T,
        fresh[3],
        news[3],
        *fresh[4:],
    )


def solution(mesh):
    finer = Mesh(
        mesh.devices.reshape(2, 4, 4, 2, mesh.shape["tensor"]), ("zl", "x", "y", "c", "zh")
    )
    columns = P(None, ROWS)
    rows = P(ROWS, None)
    return jax.shard_map(
        shards,
        mesh=finer,
        in_specs=(
            P(DP, None),
            P(DP, None),
            P(),
            P(),
            columns,
            rows,
            columns,
            rows,
            columns,
            rows,
            columns,
            rows,
            P(),
            P(),
            P(DP),
            P(DP),
            P(DP),
        ),
        out_specs=(
            P(DP, None),
            P(DP, None),
            P(),
            columns,
            columns,
            rows,
            rows,
            columns,
            columns,
            rows,
            rows,
            P(),
            P(),
            P(),
            P(),
        ),
        check_vma=False,
    )
```

```python
import math

import jax
import jax.numpy as jnp
import numpy as np
from jax import lax
from jax.experimental import pallas as pl
from jax.experimental.pallas import tpu as pltpu
from jax.sharding import Mesh
from jax.sharding import PartitionSpec as P

D = 384
HEADS = 6
HD = 64
FF = 1536
SMALL_LEN = 50
BIG_LEN = 145
NS_STEPS = 5
COEF_A = 3.4445
COEF_B = -4.775
COEF_C = 2.0315
NORM_EPS = 1e-06
CLIP_LIMIT = 1.0
MOMENTUM = 0.5
SMALL_RATE = 10.0
NORM_RATE = 40.0

DP = ("zl", "x", "y", "c")
ROWS = ("zh",) + DP
COLUMN = ("zh", "zl")
PLANE = ("x", "y")
HALF = ("zl", "x", "y")
COLUMN_CORES = ("zh", "zl", "c")
AXES = ("zl", "x", "y", "c", "zh")

BF = jnp.bfloat16
F32 = jnp.float32
BLOCK = 12
GROUP = 48
SENT = 40
VMEM = 24 << 20
ALL_VMEM = 60 << 20
LAYER_VMEM = 57 << 20


def qkv_pieces(block):
    pieces = []
    row = block * 9
    while row < block * 9 + 9:
        head, rest = divmod(row, 3 * HD)
        part, e = divmod(rest, HD)
        count = min(HD - e, block * 9 + 9 - row)
        pieces.append((row - block * 9, count, part * HEADS * HD + head * HD + e))
        row += count
    return pieces


def blocks_of_rows():
    return [
        (core, xy * GROUP + z * BLOCK, (z * 16 + xy) * 2 + core)
        for core in range(2)
        for xy in range(16)
        for z in range(4)
    ]


def small_places():
    places = np.zeros((2, 64, 768), np.float32)
    for n in range(64):
        at = (n // 4) * GROUP + (n % 4) * BLOCK
        places[0, n, at] = 1
        places[1, n, at + 9] = 1
    return places


def dot(a, b):
    return lax.dot_general(a, b, (((1,), (0,)), ((), ())), preferred_element_type=F32)


def dot_nt(a, b):
    return lax.dot_general(a, b, (((1,), (1,)), ((), ())), preferred_element_type=F32)


def dot_tn(a, b):
    return lax.dot_general(a, b, (((0,), (0,)), ((), ())), preferred_element_type=F32)


def halves(a):
    high = a.astype(BF)
    return high, (a - high.astype(F32)).astype(BF)


def norm_parts(v):
    cen = v - jnp.mean(v, axis=-1, keepdims=True)
    var = jnp.mean(cen * cen, axis=-1, keepdims=True)
    r = lax.rsqrt(var + NORM_EPS)
    return cen * r, r


def norm_back(dy, n, r, gain):
    e = dy * gain
    return r * (
        e - jnp.mean(e, axis=-1, keepdims=True) - n * jnp.mean(e * n, axis=-1, keepdims=True)
    )


def device(x, y, z, core):
    x, y, z = x % 4, y % 4, z % 4
    return ((((z % 2) * 4 + x) * 4 + y) * 2 + core) * 2 + z // 2


def chip_z():
    return 2 * lax.axis_index("zh") + lax.axis_index("zl")


def devices():
    return [(x, y, z, c) for x in range(4) for y in range(4) for z in range(4) for c in range(2)]


def column_step(step):
    return [(device(x, y, z + step, c), device(x, y, z, c)) for x, y, z, c in devices()]


def colour_groups():
    return [
        [device(x, y, x + 2 * y + colour, core) for x in range(4) for y in range(4)]
        for colour in range(4)
        for core in range(2)
    ]


def colour_step(step):
    sources = {
        1: ((-1, 0, 0), (0, 0, 1)),
        2: ((0, 1, 0), (0, -1, 0)),
        3: ((1, 0, 0), (0, 0, -1)),
    }[step]
    return [
        (device(x + sources[c][0], y + sources[c][1], z + sources[c][2], c), device(x, y, z, c))
        for x, y, z, c in devices()
    ]


def embed_kernel(tok_ref, cot_ref, table_ref, pos_ref, stream_ref, cot_out_ref, padded_ref):
    count = tok_ref.shape[0]
    padded_ref[...] = jnp.zeros(padded_ref.shape, F32)
    padded_ref[: table_ref.shape[0]] = table_ref[...]
    t0, t_rest = halves(padded_ref[...])
    t1, t2 = halves(padded_ref[...] - t0.astype(F32))
    hits = hits_of(pos_ref, count)
    stream_ref[...] = tok_ref[...].astype(F32) + (
        (dot_tn(hits, t2) + dot_tn(hits, t1)) + dot_tn(hits, t0)
    )
    cot_out_ref[...] = cot_ref[...]


def hits_of(pos_ref, count):
    return (
        lax.broadcasted_iota(jnp.int32, (64, count), 0) == jnp.broadcast_to(pos_ref[...], (64, count))
    ).astype(BF)


def layer_kernel(
    where_ref,
    res_ref,
    off_ref,
    norms_ref,
    pos_ref,
    stream_hbm,
    cot_hbm,
    own0,
    own1,
    own2,
    own3,
    oth0,
    oth1,
    oth2,
    oth3,
    result_hbm,
    in_grad_hbm,
    keep_hbm,
    send_hbm,
    wup,
    wdn,
    wqkv,
    wout,
    mixed,
    sorted_qkv,
    sorted_out,
    message,
    probs_ref,
    qkv_ref,
    ctx_ref,
    dqkv_ref,
    small_ref,
    stream_ref,
    cot_ref,
    result_ref,
    in_grad_ref,
    kept,
    sent,
    in_sems,
    out_sems,
):
    core = where_ref[0]
    half = where_ref[1]
    colour = where_ref[2]
    count = cot_ref.shape[0]
    parts = ((own0, own1, own2, own3), (oth0, oth1, oth2, oth3))
    loads = [
        pltpu.make_async_copy(stream_hbm, stream_ref, in_sems.at[0]),
        pltpu.make_async_copy(cot_hbm, cot_ref, in_sems.at[1]),
    ]
    for load in loads:
        load.start()

    for here in range(4):

        @pl.when(colour == here)
        def _(here=here):
            for s in range(2):
                for xy in range(16):
                    behind = xy // 4 + 2 * (xy % 4) + here
                    blocks = [parts[s][(z - behind) % 4][xy].astype(F32) for z in range(4)]
                    groups = [
                        jnp.concatenate([block[k : k + BLOCK] for block in blocks], axis=0)
                        for k in (0, 12, 24)
                    ]
                    at = s * 768 + xy * GROUP
                    wup[at : at + GROUP] = groups[0].astype(BF)
                    wdn[at : at + GROUP] = groups[1].astype(BF)
                    mixed[core if s == 0 else 1 - core, xy * GROUP : (xy + 1) * GROUP] = groups[2]

    for load in loads:
        load.wait()
    stream_in = stream_ref[...]
    g1, s1, g2, s2 = (norms_ref[k : k + 1, :] for k in range(4))
    n1, r1 = norm_parts(stream_in)
    y1 = (n1 * g1 + s1).astype(BF)
    for at_core, at, block in blocks_of_rows():
        for first, length, to in qkv_pieces(block):
            sorted_qkv[to : to + length] = mixed[at_core, at + first : at + first + length]
        sorted_out[block * 3 : block * 3 + 3] = mixed[at_core, at + 9 : at + 12]
    wqkv[...] = sorted_qkv[...].astype(BF)
    wout[...] = sorted_out[...].astype(BF)


    qkv_ref[...] = dot_nt(y1, wqkv[...]).astype(BF)

    def segments(shape, dim):
        at = lax.broadcasted_iota(jnp.int32, shape, dim)
        seg = at + 8
        for k in range(5):
            res = res_ref[k]
            off = off_ref[k]
            length = jnp.where(res == 0, SMALL_LEN, jnp.where(res == 1, BIG_LEN, 0))
            seg = jnp.where((at >= off) & (at < off + length), k, seg)
        return seg

    allowed = segments((count, count), 0) == segments((count, count), 1)
    lane = lax.broadcasted_iota(jnp.int32, (1, 128), 1)
    masks = ((lane < HD).astype(F32).astype(BF), (lane >= HD).astype(F32).astype(BF))
    scale = HD**-0.5
    scaled_masks = [mask * scale for mask in masks]
    for p in range(HEADS // 2):
        lo = p * 128
        q = qkv_ref[:, lo : lo + 128]
        k = qkv_ref[:, 384 + lo : 512 + lo]
        v = qkv_ref[:, 768 + lo : 896 + lo]
        ctx = 0.0
        for hh in range(2):
            scores = dot_nt(q * scaled_masks[hh], k)
            scores = jnp.where(allowed, scores, -1e30)
            expo = jnp.exp(scores - jnp.max(scores, axis=-1, keepdims=True))
            probs = expo * (1.0 / jnp.sum(expo, axis=-1, keepdims=True))
            probs_ref[2 * p + hh] = probs
            ctx = ctx + dot(probs.astype(BF), v * masks[hh])
        ctx_ref[:, lo : lo + 128] = ctx.astype(BF)
    stream_mid = stream_in + dot(ctx_ref[...], wout[...])
    n2, r2 = norm_parts(stream_mid)
    y2 = (n2 * g2 + s2).astype(BF)

    cot = cot_ref[...]
    right = jnp.where(half == 0, y2, cot)
    out = stream_mid
    d_y2 = 0.0
    for k, target in enumerate((kept, sent)):
        wu = wup[k * 768 : (k + 1) * 768, :]
        wd = wdn[k * 768 : (k + 1) * 768, :]
        pre = dot_nt(y2, wu)
        cdf = 0.5 * (1.0 + lax.erf(pre * (2.0**-0.5)))
        hidden = (pre * cdf).astype(BF)
        slope = cdf + pre * (jnp.exp(-0.5 * pre * pre) * ((2.0 * math.pi) ** -0.5))
        d_pre = (slope * dot_nt(cot, wd)).astype(BF)
        out = out + dot(hidden, wd)
        d_y2 = d_y2 + dot(d_pre, wu)
        grad = dot_tn(jnp.where(half == 0, d_pre, hidden), right)
        target[...] = grad.astype(BF).reshape(16, GROUP, D)
    result_ref[...] = out.astype(BF)
    stores = [
        pltpu.make_async_copy(source, target.at[pl.ds(first, 16)], out_sems.at[k])
        for k, (source, target, first) in enumerate(
            (
                (sent, send_hbm, 0),
                (kept, keep_hbm, 0),
                (message.at[1 - core], send_hbm, 16),
                (message.at[core], keep_hbm, 16),
            )
        )
    ]
    stores.append(pltpu.make_async_copy(result_ref, result_hbm, out_sems.at[4]))
    stores.append(pltpu.make_async_copy(in_grad_ref, in_grad_hbm, out_sems.at[5]))
    for k in (0, 1, 4):
        stores[k].start()
    gain2 = jnp.sum(d_y2 * n2, axis=0, keepdims=True)
    shift2 = jnp.sum(d_y2, axis=0, keepdims=True)
    d_mid = cot.astype(F32) + norm_back(d_y2, n2, r2, g2)

    d_attn = d_mid.astype(BF)
    d_ctx = dot_nt(d_attn, wout[...]).astype(BF)
    for p in range(HEADS // 2):
        lo = p * 128
        q = qkv_ref[:, lo : lo + 128]
        k = qkv_ref[:, 384 + lo : 512 + lo]
        v = qkv_ref[:, 768 + lo : 896 + lo]
        dc = d_ctx[:, lo : lo + 128]
        dq, dk, dv = 0.0, 0.0, 0.0
        for hh in range(2):
            probs = probs_ref[2 * p + hh]
            dcm = dc * masks[hh]
            d_probs = dot_nt(dcm, v)
            inner = jnp.sum(probs * d_probs, axis=-1, keepdims=True)
            d_scores = (probs * (d_probs - inner)).astype(BF)
            dq = dq + dot(d_scores, k * masks[hh])
            dk = dk + dot_tn(d_scores, q * masks[hh])
            dv = dv + dot_tn(probs.astype(BF), dcm)
        dqkv_ref[:, lo : lo + 128] = (dq * scale).astype(BF)
        dqkv_ref[:, 384 + lo : 512 + lo] = (dk * scale).astype(BF)
        dqkv_ref[:, 768 + lo : 896 + lo] = dv.astype(BF)
    d_y1 = dot(dqkv_ref[...], wqkv[...])
    in_grad = d_mid + norm_back(d_y1, n1, r1, g1)
    in_grad_ref[...] = in_grad
    stores[5].start()

    hits = hits_of(pos_ref, count)
    i0, i1 = halves(in_grad)
    pos_grad = dot(hits, i0) + dot(hits, i1)
    gain1 = jnp.sum(d_y1 * n1, axis=0, keepdims=True)
    shift1 = jnp.sum(d_y1, axis=0, keepdims=True)
    row = lax.broadcasted_iota(jnp.int32, (64, 384), 0)
    for at, value in ((50, gain1), (51, shift1), (52, gain2), (53, shift2)):
        pos_grad = jnp.where(row == at, jnp.broadcast_to(value, (64, 384)), pos_grad)
    sorted_out[...] = dot_tn(ctx_ref[...], d_attn)
    sorted_qkv[...] = dot_tn(dqkv_ref[...], y1)
    small_ref[...] = pos_grad

    @pl.when(half == 0)
    def _():
        zeros = jnp.zeros((8, D), F32)
        for at_core in range(2):
            for xy in range(16):
                rows = []
                for z in range(4):
                    block = (z * 16 + xy) * 2 + at_core
                    rows += [
                        small_ref[xy * 4 + z : xy * 4 + z + 1],
                        zeros,
                        sorted_out[block * 3 : block * 3 + 3],
                    ]
                message[at_core, xy] = jnp.concatenate(rows, axis=0).astype(BF)

    @pl.when(half == 1)
    def _():
        zeros = jnp.zeros((2, D), F32)
        for at_core in range(2):
            for xy in range(16):
                rows = []
                for z in range(4):
                    rows += [
                        sorted_qkv[to : to + length]
                        for _, length, to in qkv_pieces((z * 16 + xy) * 2 + at_core)
                    ]
                    rows += [small_ref[xy * 4 + z : xy * 4 + z + 1], zeros]
                message[at_core, xy] = jnp.concatenate(rows, axis=0).astype(BF)

    stores[2].start()
    stores[3].start()
    for store in stores:
        store.wait()


def run_layer(where, res_ids, offsets, stream, cotangent, norms, pos, weights):
    count = stream.shape[0]
    smem = pl.BlockSpec(memory_space=pltpu.SMEM)
    vmem = pl.BlockSpec(memory_space=pltpu.VMEM)
    hbm = pl.BlockSpec(memory_space=pl.ANY)
    return pl.pallas_call(
        layer_kernel,
        out_shape=(
            jax.ShapeDtypeStruct((count, D), BF),
            jax.ShapeDtypeStruct((count, D), F32),
            jax.ShapeDtypeStruct((32, GROUP, D), BF),
            jax.ShapeDtypeStruct((32, GROUP, D), BF),
        ),
        in_specs=[smem] * 3 + [vmem] * 2 + [hbm] * 2 + [vmem] * 8,
        out_specs=(hbm,) * 4,
        scratch_shapes=[
            pltpu.VMEM((1536, D), BF),
            pltpu.VMEM((1536, D), BF),
            pltpu.VMEM((1152, D), BF),
            pltpu.VMEM((D, D), BF),
            pltpu.VMEM((2, 768, D), F32),
            pltpu.VMEM((1152, D), F32),
            pltpu.VMEM((D, D), F32),
            pltpu.VMEM((2, 16, GROUP, D), BF),
            pltpu.VMEM((HEADS, count, count), F32),
            pltpu.VMEM((count, 1152), BF),
            pltpu.VMEM((count, D), BF),
            pltpu.VMEM((count, 1152), BF),
            pltpu.VMEM((64, D), F32),
            pltpu.VMEM((count, D), F32),
            pltpu.VMEM((count, D), BF),
            pltpu.VMEM((count, D), BF),
            pltpu.VMEM((count, D), F32),
            pltpu.VMEM((16, GROUP, D), BF),
            pltpu.VMEM((16, GROUP, D), BF),
            pltpu.SemaphoreType.DMA((2,)),
            pltpu.SemaphoreType.DMA((6,)),
        ],
        compiler_params=pltpu.CompilerParams(vmem_limit_bytes=LAYER_VMEM),
        cost_estimate=pl.CostEstimate(
            flops=0, bytes_accessed=0, transcendentals=0
        ),
        name="layer",
    )(
        where, res_ids, offsets, norms, pos, stream, cotangent, *weights
    )


def product(a, b):
    (ah, al), (bh, bl) = a, b
    first = jnp.concatenate([ah, al], axis=1)
    return dot(first, jnp.concatenate([bh, bh], axis=0)) + dot(ah, bl)


def call(kernel, name, outs, args, scratch=(), flops=0, moved=0, vmem_bytes=VMEM):
    vmem = pl.BlockSpec(memory_space=pltpu.VMEM)
    return pl.pallas_call(
        kernel,
        out_shape=tuple(jax.ShapeDtypeStruct(shape, dtype) for shape, dtype in outs),
        in_specs=[vmem] * len(args),
        out_specs=(vmem,) * len(outs),
        scratch_shapes=scratch,
        compiler_params=pltpu.CompilerParams(vmem_limit_bytes=vmem_bytes),
        cost_estimate=pl.CostEstimate(flops=flops, bytes_accessed=moved, transcendentals=0),
        name=name,
    )(*args)


def weights_kernel(qkv_ref, out_ref, up_ref, down_ref, rows_ref):
    rows = jnp.concatenate(
        [up_ref[...], down_ref[...], qkv_ref[...], out_ref[...], jnp.zeros((SENT - 36, D), F32)],
        axis=0,
    ).astype(BF)
    rows_ref[...] = jnp.broadcast_to(rows[None], rows_ref.shape)


def moments_kernel(qkv_ref, out_ref, up_ref, down_ref, *old_refs):
    zeros = jnp.zeros((9, D), F32)
    old = (
        up_ref[...],
        jnp.concatenate([zeros, out_ref[...]], axis=0),
        down_ref[...],
        jnp.concatenate([qkv_ref[...], zeros[:3]], axis=0),
    )
    for z in range(4):

        @pl.when(chip_z() == z)
        def _(z=z):
            for step, ref in enumerate(old_refs):
                ref[...] = old[(z - step) % 4].astype(BF)


def join_kernel(*refs):
    *sources, joined_ref, sent_ref = refs
    for z in range(4):

        @pl.when(chip_z() == z)
        def _(z=z):
            joined = jnp.concatenate(
                [sources[(at - z) % 4][...].astype(F32) for at in range(4)], axis=0
            ).astype(BF)
            joined_ref[...] = joined
            sent_ref[...] = jnp.broadcast_to(joined[None], sent_ref.shape)


def hold_kernel(keep_ref, held_ref):
    held_ref[...] = keep_ref[...]


def sum_kernel(parts_ref, piece_ref, sent_ref):
    total = parts_ref[0].astype(F32)
    for k in range(1, parts_ref.shape[0]):
        total = total + parts_ref[k].astype(F32)
    piece_ref[...] = total
    sent_ref[...] = jnp.broadcast_to(total.astype(BF)[None], sent_ref.shape)


def valid_rows(z):
    row = lax.broadcasted_iota(jnp.int32, (GROUP, D), 0) % BLOCK
    return jnp.where(z == 1, (row >= 9).astype(F32), jnp.where(z == 3, (row < 9).astype(F32), 1.0))


def tell_kernel(own_ref, piece_ref, told_ref):
    z = chip_z()
    counts_all = (z == 1) & (lax.axis_index("c") == 0)
    valid = jnp.where(counts_all, 1.0, valid_rows(z))
    total = jnp.zeros((GROUP, D), F32)
    for xy in range(16):
        g = own_ref[xy].astype(F32)
        total = total + g * g
    squares = jnp.full((1, D), jnp.sum(total * valid), F32)
    high = squares.astype(BF).astype(F32)
    mid = (squares - high).astype(BF).astype(F32)
    low = squares - high - mid
    for to in range(4):
        rows = jnp.concatenate(
            [piece_ref[to * BLOCK : (to + 1) * BLOCK, :], high, mid, low, jnp.zeros((1, D), F32)],
            axis=0,
        ).astype(BF)
        told_ref[2 * to] = rows
        told_ref[2 * to + 1] = rows


def small_kernel(own_ref, places_ref, small_ref):
    small_ref[...] = dot(places_ref[lax.axis_index("zh")], own_ref[...].reshape(768, D)).astype(BF)


def clip(told_ref):
    total = jnp.zeros((1, 1), F32)
    for k in range(8):
        last = told_ref[k].astype(F32)
        total = total + (last[12:13, :1] + last[13:14, :1] + last[14:15, :1])
    grad_norm = jnp.sqrt(total)
    return grad_norm, jnp.minimum(1.0, CLIP_LIMIT / (grad_norm + 1e-06))


def orth_kernel(
    told_ref,
    own_ref,
    oth_ref,
    old_own_ref,
    old_oth_ref,
    old_ref,
    piece_ref,
    *refs,
):
    out_refs = refs
    valid = valid_rows(chip_z())
    factor = clip(told_ref)[1]
    scaled = factor * valid
    gram = 0.0
    for grad_ref, before_ref in ((own_ref, old_own_ref), (oth_ref, old_oth_ref)):
        rows = jnp.concatenate(
            [
                (MOMENTUM * before_ref[xy].astype(F32) + scaled * grad_ref[xy].astype(F32)).astype(BF)
                for xy in range(16)
            ],
            axis=0,
        )
        gram = gram + dot_tn(rows, rows)
    eye = (
        lax.broadcasted_iota(jnp.int32, (D, D), 0) == lax.broadcasted_iota(jnp.int32, (D, D), 1)
    ).astype(F32)
    inv = 1.0 / (jnp.sqrt(jnp.sum(gram * eye)) + 1e-07)
    gram = gram * (inv * inv)
    mine = (MOMENTUM * old_ref[...].astype(F32) + scaled * piece_ref[...]) * inv
    turned = mine.T
    for step in range(NS_STEPS - 2):
        parts = halves(gram)
        poly = halves(COEF_A * eye + COEF_B * gram + COEF_C * dot(parts[0], parts[0]))
        inner = halves(product(poly, parts))
        more = halves(turned)
        both = product(
            poly, [jnp.concatenate([inner[k], more[k]], axis=1) for k in range(2)]
        )
        gram, turned = both[:, :D], both[:, D:]
    parts = halves(gram)
    poly = (COEF_A * eye + COEF_B * gram + COEF_C * product(parts, parts)).astype(BF)
    inner = dot(poly, parts[0]).astype(BF)
    both = dot(poly, jnp.concatenate([inner, turned.astype(BF)], axis=1))
    gram, turned = both[:, :D], both[:, D:]
    low = gram.astype(BF)
    poly = COEF_A * eye + COEF_B * gram + COEF_C * dot(low, low)
    mine = dot(poly.astype(BF), turned.astype(BF)).T
    for z in range(4):

        @pl.when(chip_z() == z)
        def _(z=z):
            for step, ref in enumerate(out_refs):
                to = (z - step) % 4
                ref[...] = mine[to * BLOCK : (to + 1) * BLOCK].astype(BF)


def step_rate(rows_count, cols_count):
    return math.sqrt(max(rows_count, cols_count) / rows_count)


def moment_kernel(
    told_ref,
    small_own_ref,
    small_near_ref,
    qkv_m_ref,
    out_m_ref,
    up_m_ref,
    down_m_ref,
    norms_ref,
    norm_m_ref,
    table_ref,
    pos_m_ref,
    grad_norm_ref,
    qkv_m_next,
    out_m_next,
    up_m_next,
    down_m_next,
    norm_m_next,
    norms_next,
    pos_m_next,
    table_next,
):
    grad_norm, factor = clip(told_ref)
    grad_norm_ref[...] = grad_norm
    for z, first, last, m_ref, m_next in (
        (3, 0, 9, qkv_m_ref, qkv_m_next),
        (1, 9, 12, out_m_ref, out_m_next),
        (0, 0, 12, up_m_ref, up_m_next),
        (2, 0, 12, down_m_ref, down_m_next),
    ):
        grad = told_ref[2 * z + lax.axis_index("c")].astype(F32)[first:last]
        m_next[...] = MOMENTUM * m_ref[...] + factor * grad
    near = (lax.axis_index("zl") == 0).astype(F32)
    small = near * small_near_ref[...].astype(F32) + (1.0 - near) * small_own_ref[...].astype(F32)
    norm_fresh = MOMENTUM * norm_m_ref[...] + factor * small[50:54]
    norm_m_next[...] = norm_fresh
    norms_next[...] = norms_ref[...] - NORM_RATE * norm_fresh
    pos_fresh = MOMENTUM * pos_m_ref[...] + factor * small[:50]
    pos_m_next[...] = pos_fresh
    table_next[...] = table_ref[...] - SMALL_RATE * pos_fresh


def update_kernel(
    orth0,
    orth1,
    orth2,
    orth3,
    qkv_ref,
    out_ref,
    up_ref,
    down_ref,
    qkv_next,
    out_next,
    up_next,
    down_next,
):
    here = chip_z()
    sources = [ref[...].astype(F32) for ref in (orth0, orth1, orth2, orth3)]
    for z, first, last, rate, w_ref, w_next in (
        (3, 0, 9, step_rate(D, 3 * D), qkv_ref, qkv_next),
        (1, 9, 12, step_rate(D, D), out_ref, out_next),
        (0, 0, 12, step_rate(D, FF), up_ref, up_next),
        (2, 0, 12, step_rate(FF, D), down_ref, down_next),
    ):
        orth = sources[z]
        for step in range(1, 4):
            orth = jnp.where(here == step, sources[(z - step) % 4], orth)
        w_next[...] = w_ref[...] - rate * orth[first:last]


def swapped(value):
    return lax.ppermute(value, "c", [(0, 1), (1, 0)])


def exchanged(value, axes):
    return lax.all_to_all(value, axes, 0, 0, tiled=True)


def everywhere(value, axes):
    peers = lax.axis_size(axes)
    return exchanged(jnp.broadcast_to(value[None], (peers, *value.shape)), axes)


def shards(
    tokens,
    cotangent,
    pos_table,
    norm_params,
    qkv_weight,
    out_weight,
    up_weight,
    down_weight,
    qkv_moment,
    out_moment,
    up_moment,
    down_moment,
    norm_moment,
    pos_moment,
    res_ids,
    offsets,
    pos_index,
):
    weights = (qkv_weight.T, out_weight, up_weight.T, down_weight)
    moments = (qkv_moment.T, out_moment, up_moment.T, down_moment)

    (rows,) = call(
        weights_kernel, "weights", (((16, SENT, D), BF),), weights, vmem_bytes=ALL_VMEM
    )
    old = call(
        moments_kernel,
        "moments",
        (((BLOCK, D), BF),) * 4,
        moments,
    )
    old = [old[0]] + [lax.ppermute(old[k], AXES, column_step(k)) for k in (1, 2, 3)]
    pos = pos_index.reshape(1, -1)
    stream, cotangent = call(
        embed_kernel,
        "embed",
        ((tokens.shape, F32), (tokens.shape, BF)),
        (tokens, cotangent, pos_table, pos),
        scratch=[pltpu.VMEM((64, D), F32)],
        vmem_bytes=ALL_VMEM,
    )

    own = [lax.all_to_all(rows, AXES, 0, 0, axis_index_groups=colour_groups(), tiled=True)]
    own[0], stream, cotangent, *old = lax.optimization_barrier(
        (own[0], stream, cotangent, *old)
    )
    old, old_sent = call(
        join_kernel,
        "join",
        (((GROUP, D), BF), ((16, GROUP, D), BF)),
        old,
    )
    own += [lax.ppermute(own[0], AXES, colour_step(step)) for step in (1, 2, 3)]
    other = [swapped(value) for value in own]
    old_sent, other[0] = lax.optimization_barrier((old_sent, other[0]))
    old_own = exchanged(old_sent, PLANE)

    colour = (chip_z() + 12 - lax.axis_index("x") - 2 * lax.axis_index("y")) & 3
    where = jnp.stack([lax.axis_index("c"), lax.axis_index("zh"), colour]).astype(jnp.int32)
    result, in_grad, keep, send = run_layer(
        where,
        res_ids,
        offsets,
        stream,
        cotangent,
        norm_params,
        pos,
        (*own, *other),
    )
    keep, send, old_own = lax.optimization_barrier((keep, send, old_own))
    old_other = swapped(old_own)
    (keep,) = call(hold_kernel, "hold", ((keep.shape, BF),), (keep,))
    pair = (keep.astype(F32) + swapped(send).astype(F32)).astype(BF)
    piece, sent = call(
        sum_kernel, "sum", (((GROUP, D), F32), ((16, GROUP, D), BF)), (exchanged(pair, HALF),)
    )
    grads = exchanged(sent, PLANE)
    (told,) = call(
        tell_kernel, "tell", (((8, 16, D), BF),), (grads, piece)
    )
    told, grads_sent = lax.optimization_barrier((told, grads))
    told = exchanged(told, COLUMN_CORES)
    grads_other = swapped(grads_sent)
    (small,) = call(
        small_kernel,
        "small",
        (((64, D), BF),),
        (grads_sent, jnp.asarray(small_places(), BF)),
    )
    small_near = lax.ppermute(small, "zl", [(1, 0)])
    orth = call(
        orth_kernel,
        "orth",
        (((BLOCK, D), BF),) * 4,
        (told, grads, grads_other, old_own, old_other, old, piece),
        flops=8_000_000_000,
        moved=4_000_000,
    )
    back = [orth[0]] + [lax.ppermute(orth[k], AXES, column_step(k)) for k in (1, 2, 3)]
    like = lambda a: (a.shape, F32)
    grad_norm, *fresh = call(
        moment_kernel,
        "moment",
        (
            ((1, 1), F32),
            *(like(a) for a in moments),
            like(norm_moment),
            like(norm_params),
            like(pos_moment),
            like(pos_table),
        ),
        (told, small, small_near, *moments, norm_params, norm_moment, pos_table, pos_moment),
    )
    news = call(
        update_kernel, "update", [like(a) for a in weights], (*back, *weights)
    )
    return (
        result,
        in_grad,
        grad_norm.reshape(()),
        fresh[0].T,
        news[0].T,
        fresh[1],
        news[1],
        fresh[2].T,
        news[2].T,
        fresh[3],
        news[3],
        *fresh[4:],
    )


def solution(mesh):
    finer = Mesh(
        mesh.devices.reshape(2, 4, 4, 2, mesh.shape["tensor"]), ("zl", "x", "y", "c", "zh")
    )
    columns = P(None, ROWS)
    rows = P(ROWS, None)
    return jax.shard_map(
        shards,
        mesh=finer,
        in_specs=(
            P(DP, None),
            P(DP, None),
            P(),
            P(),
            columns,
            rows,
            columns,
            rows,
            columns,
            rows,
            columns,
            rows,
            P(),
            P(),
            P(DP),
            P(DP),
            P(DP),
        ),
        out_specs=(
            P(DP, None),
            P(DP, None),
            P(),
            columns,
            columns,
            rows,
            rows,
            columns,
            columns,
            rows,
            rows,
            P(),
            P(),
            P(),
            P(),
        ),
        check_vma=False,
    )
```
